32 devices in a mesh: dp: 4 (over y, x), row: 4 (over z), col: 2 (over core).
Axes of the slice: x: 2, y: 2, z: 4, core: 2. Of those that a mesh axis runs over, the one named last changes fastest.
Arguments:
- hidden: bfloat16 [16384, 1024], P(('dp', 'row'), 'col'), may hold values from -6 to 6
- segments: int32 [16, 1024], P(('dp', 'row')), may hold values from 0 to 3, never falling along the last dimension, each value on 1 to 512 neighbouring positions
- ln1_gain: bfloat16 [1024], P('col'), may hold values from 0.5 to 1.5
- ln1_bias: bfloat16 [1024], P('col'), may hold values from -3 to 3
- qkv_weight: bfloat16 [1024, 3072], P('row', 'col'), may hold values from -0.25 to 0.25
- qkv_bias: bfloat16 [3072], P('col'), may hold values from -2 to 2
- out_weight: bfloat16 [1024, 1024], P('col', 'row'), may hold values from -0.75 to 0.75
- out_bias: bfloat16 [1024], P('col'), may hold values from -2 to 2
- ln2_gain: bfloat16 [1024], P('col'), may hold values from 0.5 to 1.5
- ln2_bias: bfloat16 [1024], P('col'), may hold values from -3 to 3
- up_weight: bfloat16 [1024, 4096], P('row', 'col'), may hold values from -0.1875 to 0.1875
- up_bias: bfloat16 [4096], P('col'), may hold values from -2 to 2
- down_weight: bfloat16 [4096, 1024], P('col', 'row'), may hold values from -0.125 to 0.125
- down_bias: bfloat16 [1024], P('col'), may hold values from -2 to 2
- cotangent: bfloat16 [16384, 1024], P(('dp', 'row'), 'col'), may hold values from -6 to 6
Outputs:
- output: float32 [16384, 1024], P(('dp', 'row'), 'col')
- input_grad: float32 [16384, 1024], P(('dp', 'row'), 'col')
- ln1_gain_grad: float32 [1024], P('col')
- ln1_bias_grad: float32 [1024], P('col')
- qkv_weight_grad: float32 [1024, 3072], P('row', 'col')
- qkv_bias_grad: float32 [3072], P('col')
- out_weight_grad: float32 [1024, 1024], P('col', 'row')
- out_bias_grad: float32 [1024], P('col')
- ln2_gain_grad: float32 [1024], P('col')
- ln2_bias_grad: float32 [1024], P('col')
- up_weight_grad: float32 [1024, 4096], P('row', 'col')
- up_bias_grad: float32 [4096], P('col')
- down_weight_grad: float32 [4096, 1024], P('col', 'row')
- down_bias_grad: float32 [1024], P('col')
The draws below stay inside these ranges and needn't reach their ends.
Inputs may be any that keep to these rules, and one draw needn't show every extreme that they name: `segments`: segment numbers never fall along a sequence; a document holds at most 512 tokens.
All inputs are finite; a program needn't handle non-finite values.
Results may differ from the reference program's by a relative error of at most 0.012.
The reference program's roundings to bfloat16 on the way count: a program that leaves them out, or rounds other values in their place, can miss the bound.
Values may be sent and summed in bfloat16 or wider, within the bound.
A program may use at most 256 MiB of HBM per device.

```python
import math
import jax
import jax.numpy as jnp
import numpy as np
from jax import lax

D = 1024
HEADS = 16
HEAD_DIM = 64
FF = 4096
ROT = 16
LEN = 1024
DOCS = 4
SEQS = 16
TOKENS = 16384


def shard_levels(stream_key, extent, cuts, low, high):
    level = 1.0
    for dim, shards_of in cuts:
        heights = jax.random.uniform(jax.random.fold_in(jax.random.fold_in(stream_key, 6), dim), (shards_of,), jnp.float32, low / len(cuts), high / len(cuts))
        level = level * jnp.repeat(jnp.exp(heights), extent[dim] // shards_of).reshape((-1,) + (1,) * (len(extent) - 1 - dim))
    return level


def split_up(number_of, total, bound, skew):
    loads = [(1 << 20) // math.isqrt(rank ** skew) + 1 for rank in range(2, number_of + 1)]
    spare, given = total - bound - (number_of - 1), [1] * (number_of - 1)
    while spare > 0:
        movable = [i for i in range(number_of - 1) if given[i] < bound]
        pool, remaining = sum([loads[i] for i in movable]), spare
        for i in movable:
            addition = min(bound - given[i], max(1, remaining * loads[i] // pool), spare)
            given[i] = given[i] + addition
            spare = spare - addition
    return np.array([bound] + given)


def ragged_sizes(key, number_of, total, bound, skew):
    if number_of == 2:
        one = jax.random.randint(key, (), max(1, total - bound), min(bound, total - 1) + 1)
        return jnp.stack([one, total - one])
    sizes = jnp.asarray(split_up(number_of, total, bound, skew), jnp.int32)
    pairs = (number_of - 1) // 2
    donor, taker = sizes[1:1 + 2 * pairs:2], sizes[2:2 + 2 * pairs:2]
    room = jnp.minimum(donor - 1, bound - taker)
    shifted = jax.random.randint(jax.random.fold_in(key, 1), (pairs,), 0, 1 << 20) % (room + 1)
    sizes = sizes.at[1:1 + 2 * pairs:2].set(donor - shifted).at[2:2 + 2 * pairs:2].set(taker + shifted)
    return sizes[jax.random.permutation(jax.random.fold_in(key, 2), number_of)]


def scatter_about(rng, shape, width, limit, split=(), kind=jnp.bfloat16):
    values = jax.random.normal(rng, shape, jnp.float32) * width
    if len(split) > 0:
        values = shard_levels(rng, shape, split, -0.22, 0.18) * values
    return jnp.clip(values, min=-limit, max=limit).astype(kind)


def setup_inputs(seed: int = 0) -> dict:
    arg_keys = jax.random.split(jax.random.key(seed), 16)
    hidden = scatter_about(arg_keys[0], (TOKENS, D), 1.0, 6.0, ((0, 16), (1, 2)))
    segments = jax.vmap(lambda own: jnp.searchsorted(jnp.cumsum(ragged_sizes(own, DOCS, LEN, LEN // 2, 2)), jnp.arange(LEN), side="right"))(jax.random.split(arg_keys[1], SEQS)).reshape((SEQS, LEN)).astype(jnp.int32)
    ln1_gain = jnp.clip(1.0 + 0.1 * jax.random.normal(arg_keys[2], (D,), jnp.float32), 0.5, 1.5).astype(jnp.bfloat16)
    ln1_bias = scatter_about(arg_keys[3], (D,), 0.5, 3.0, ((0, 2),))
    qkv_weight = scatter_about(arg_keys[4], (D, 3 * D), (D // 2) ** -0.5, 0.25, ((0, 4), (1, 2)))
    qkv_bias = scatter_about(arg_keys[5], (3 * D,), 0.3, 2.0, ((0, 2),))
    out_weight = scatter_about(arg_keys[6], (D, D), (D // 16) ** -0.5, 0.75, ((0, 2), (1, 4)))
    out_bias = scatter_about(arg_keys[7], (D,), 0.3, 2.0, ((0, 2),))
    ln2_gain = jnp.clip(1.0 + 0.1 * jax.random.normal(arg_keys[8], (D,), jnp.float32), 0.5, 1.5).astype(jnp.bfloat16)
    ln2_bias = scatter_about(arg_keys[9], (D,), 0.5, 3.0, ((0, 2),))
    up_weight = scatter_about(arg_keys[10], (D, FF), D ** -0.5, 0.1875, ((0, 4), (1, 2)))
    up_bias = scatter_about(arg_keys[11], (FF,), 0.3, 2.0, ((0, 2),))
    down_weight = scatter_about(arg_keys[12], (FF, D), (FF // 2) ** -0.5, 0.125, ((0, 2), (1, 4)))
    down_bias = scatter_about(arg_keys[13], (D,), 0.3, 2.0, ((0, 2),))
    cotangent = scatter_about(arg_keys[14], (TOKENS, D), 1.0, 6.0, ((0, 16), (1, 2)))
    return {"hidden": hidden, "segments": segments, "ln1_gain": ln1_gain, "ln1_bias": ln1_bias, "qkv_weight": qkv_weight, "qkv_bias": qkv_bias, "out_weight": out_weight, "out_bias": out_bias, "ln2_gain": ln2_gain, "ln2_bias": ln2_bias, "up_weight": up_weight, "up_bias": up_bias, "down_weight": down_weight, "down_bias": down_bias, "cotangent": cotangent}


EPS = 1e-05

@jax.custom_vjp
def low(v):
    return lax.optimization_barrier(v.astype(jnp.bfloat16)).astype(jnp.float32)

@jax.custom_vjp
def low_back(v):
    return v

def low_keep(v):
    return (low(v), None)

def low_pass(kept, grad):
    return (grad,)

def back_keep(v):
    return (v, None)

def back_low(kept, grad):
    return (low(grad),)
low.defvjp(low_keep, low_pass)
low_back.defvjp(back_keep, back_low)

def layer_norm(values, gain_vec, shift_vec):
    centred = values - lax.optimization_barrier(jnp.mean(values, axis=-1, keepdims=True))
    variance = lax.optimization_barrier(jnp.mean(centred * centred, axis=-1, keepdims=True))
    return centred * lax.rsqrt(variance + EPS) * gain_vec + shift_vec

def doc_positions(segments):
    length = segments.shape[-1]
    places = jnp.arange(length, dtype=jnp.int32)
    changed = jnp.concatenate([jnp.ones(segments.shape[:-1] + (1,), dtype=bool), segments[..., 1:] != segments[..., :-1]], axis=-1)
    starts = lax.cummax(jnp.where(changed, places, jnp.zeros_like(places)), axis=segments.ndim - 1)
    return places - starts

def rotary_tables(positions):
    frequency = 10000.0 ** (-jnp.arange(0, ROT, 2, dtype=jnp.float32) / ROT)
    angles = positions.astype(jnp.float32)[..., None] * frequency
    angles = jnp.concatenate([angles, angles], axis=-1)
    return (jnp.cos(angles), jnp.sin(angles))

def rotate(values, cos_table, sine_table):
    rot_part = values[..., :ROT]
    turned = jnp.concatenate([-rot_part[..., ROT // 2:], rot_part[..., :ROT // 2]], axis=-1)
    return jnp.concatenate([rot_part * cos_table + turned * sine_table, values[..., ROT:]], axis=-1)

def attend(queries, key_vecs, value_vecs, segment_row):
    highest = lax.Precision.HIGHEST
    scores = jnp.einsum('qhd,khd->hqk', queries, key_vecs, precision=highest) * HEAD_DIM ** (-0.5)
    scores = low_back(scores)
    places = jnp.arange(LEN)
    allowed = (segment_row[:, None] == segment_row[None, :]) & (places[:, None] >= places[None, :])
    scores = jnp.where(allowed[None], scores, -1e+30)
    row_max = lax.optimization_barrier(jnp.max(scores, axis=-1, keepdims=True))
    powers = jnp.exp(scores - row_max)
    attn_probs = powers / lax.optimization_barrier(jnp.sum(powers, axis=-1, keepdims=True))
    return jnp.einsum('hqk,khd->qhd', low(attn_probs), value_vecs, precision=highest)

def forward(params, inputs, segments):
    gain_one, shift_one, qkv_weight, qkv_bias, out_weight, out_bias, gain_two, shift_two, up_weight, up_bias, down_weight, down_bias = params
    highest = lax.Precision.HIGHEST
    seq_count = segments.shape[0]
    normed_one = low(layer_norm(inputs, gain_one, shift_one))
    qkv_rows = low_back(jnp.dot(normed_one, qkv_weight, precision=highest) + qkv_bias)
    qkv_rows = qkv_rows.reshape(seq_count, LEN, HEADS, 3, HEAD_DIM)
    cos_table, sine_table = rotary_tables(doc_positions(segments))
    cos_table = cos_table[:, :, None, :]
    sine_table = sine_table[:, :, None, :]
    queries = low(rotate(qkv_rows[:, :, :, 0], cos_table, sine_table))
    key_vecs = low(rotate(qkv_rows[:, :, :, 1], cos_table, sine_table))
    value_vecs = low(qkv_rows[:, :, :, 2])
    context = lax.map(jax.checkpoint(lambda pieces: attend(*pieces)), (queries, key_vecs, value_vecs, segments))
    context = low_back(low(context.reshape(seq_count * LEN, D)))
    attn_out = jnp.dot(context, out_weight, precision=highest) + out_bias
    normed_two = low(layer_norm(inputs, gain_two, shift_two))
    up_proj = low_back(jnp.dot(normed_two, up_weight, precision=highest) + up_bias)
    hidden_act = low(jax.nn.gelu(up_proj, approximate=False))
    mlp_out = jnp.dot(hidden_act, down_weight, precision=highest) + down_bias
    return inputs + attn_out + mlp_out

def reference(hidden, segments, ln1_gain, ln1_bias, qkv_weight, qkv_bias, out_weight, out_bias, ln2_gain, ln2_bias, up_weight, up_bias, down_weight, down_bias, cotangent):
    params = tuple((tensor.astype(jnp.float32) for tensor in (ln1_gain, ln1_bias, qkv_weight, qkv_bias, out_weight, out_bias, ln2_gain, ln2_bias, up_weight, up_bias, down_weight, down_bias)))
    per_round = max(1, min(SEQS, 4096 // LEN))
    rounds = SEQS // per_round
    in_groups = hidden.astype(jnp.float32).reshape(rounds, per_round * LEN, D)
    cot_groups = cotangent.astype(jnp.float32).reshape(rounds, per_round * LEN, D)
    seg_groups = segments.reshape(rounds, per_round, LEN)

    def advance(totals, pieces):
        part_in, part_seg, part_cot = pieces
        result, pullback = jax.vjp(lambda weights_now, inputs_now: forward(weights_now, inputs_now, part_seg), params, part_in)
        grad_params, grad_in = pullback(part_cot)
        return (jax.tree.map(jnp.add, totals, grad_params), (result, grad_in))
    initial = jax.tree.map(jnp.zeros_like, params)
    totals, (outputs, input_grads) = lax.scan(advance, initial, (in_groups, seg_groups, cot_groups))
    return (outputs.reshape(TOKENS, D), input_grads.reshape(TOKENS, D), totals[0], totals[1], totals[2], totals[3], totals[4], totals[5], totals[6], totals[7], totals[8], totals[9], totals[10], totals[11])
```

```python
import functools

import jax
import jax.numpy as jnp
from jax import lax
from jax.experimental import pallas as pl
from jax.experimental.pallas import tpu as pltpu
from jax.sharding import PartitionSpec as P

HEAD_DIM = 64
ROT = 16
EPS = 1e-05
MAX_DOC = 512
LANES = 128
BF16 = jnp.bfloat16
F32 = jnp.float32

NT = (((1,), (1,)), ((), ()))
TN = (((0,), (0,)), ((), ()))
NN = (((1,), (0,)), ((), ()))


def dot(a, b, dims=NN):
    return lax.dot_general(a, b, dims, preferred_element_type=F32)


def doc_positions(segments):
    length = segments.shape[-1]
    places = jnp.arange(length, dtype=jnp.int32)
    changed = jnp.concatenate(
        [jnp.ones(segments.shape[:-1] + (1,), dtype=bool), segments[..., 1:] != segments[..., :-1]],
        axis=-1,
    )
    starts = lax.cummax(jnp.where(changed, places, jnp.zeros_like(places)), axis=segments.ndim - 1)
    return places - starts


def rotary_tables(positions):
    lane = jnp.arange(LANES) % HEAD_DIM
    frequency = 10000.0 ** (-2.0 * (lane % (ROT // 2)).astype(F32) / ROT)
    turning = lane < ROT
    angles = positions.astype(F32)[:, None] * jnp.where(turning, frequency, 0.0)[None, :]
    sign = jnp.where(turning, jnp.where(lane < ROT // 2, -1.0, 1.0), 0.0)
    return jnp.cos(angles), jnp.sin(angles) * sign[None, :]


def turn(values, cos_rows, sine_rows, low_lanes):
    half = ROT // 2
    up = pltpu.roll(values, values.shape[1] - half, 1)
    down = pltpu.roll(values, half, 1)
    return values * cos_rows + jnp.where(low_lanes, up, down) * sine_rows


def attention_kernel(
    q_ref, k_ref, v_ref, gc_ref, seg_row_ref, seg_col_ref, cos_ref, sin_ref, ctx_ref, gm_ref, dk_acc, dv_acc, *, block
):
    pair = pl.program_id(0)
    pairs = pl.num_programs(0)
    length = q_ref.shape[0]
    lane = lax.broadcasted_iota(jnp.int32, (1, LANES), 1)
    low_lanes = lane % HEAD_DIM < ROT // 2
    first = lane < HEAD_DIM
    zero = jnp.zeros((), BF16)

    def split(values):
        return [jnp.where(first, values, zero), jnp.where(first, zero, values)]

    dk_acc[...] = jnp.zeros_like(dk_acc)
    dv_acc[...] = jnp.zeros_like(dv_acc)
    for begin in range(0, length, block):
        low = max(0, begin - (MAX_DOC - 1)) // LANES * LANES
        rows = pl.ds(begin, block)
        keys = pl.ds(low, begin + block - low)
        width = begin + block - low
        q_parts = split(q_ref[rows, :] * jnp.asarray(HEAD_DIM**-0.5, BF16))
        g_parts = split(gc_ref[rows, :])
        k_block = k_ref[keys, :]
        v_block = v_ref[keys, :]
        places = begin + lax.broadcasted_iota(jnp.int32, (block, width), 0)
        key_places = low + lax.broadcasted_iota(jnp.int32, (block, width), 1)
        allowed = (seg_col_ref[rows, :] == seg_row_ref[:, keys]) & (places >= key_places)
        probs = []
        grads = []
        for part in range(2):
            scores = dot(q_parts[part], k_block, NT)
            scores = jnp.where(allowed, scores, -1e30)
            top = jnp.max(scores, axis=1, keepdims=True)
            powers = jnp.exp(scores - top)
            total = jnp.sum(powers, axis=1, keepdims=True)
            chances = powers * (1.0 / total)
            slopes = dot(g_parts[part], v_block, NT)
            inner = jnp.sum(slopes * chances, axis=1, keepdims=True)
            probs.append(chances.astype(BF16))
            grads.append((chances * (slopes - inner)).astype(BF16))
        context = jnp.where(first, dot(probs[0], v_block), dot(probs[1], v_block))
        ctx_ref[rows, :] = context.astype(BF16)
        dq = jnp.where(first, dot(grads[0], k_block), dot(grads[1], k_block)) * HEAD_DIM**-0.5
        dq = turn(dq, cos_ref[rows, :], -sin_ref[rows, :], low_lanes)
        gm_ref[rows, pl.ds(pl.multiple_of(pair * LANES, LANES), LANES)] = dq.astype(BF16)
        dk_acc[keys, :] += dot(grads[0], q_parts[0], TN) + dot(grads[1], q_parts[1], TN)
        dv_acc[keys, :] += dot(probs[0], g_parts[0], TN) + dot(probs[1], g_parts[1], TN)
    dk = turn(dk_acc[...], cos_ref[...], -sin_ref[...], low_lanes)
    gm_ref[:, pl.ds(pl.multiple_of((pairs + pair) * LANES, LANES), LANES)] = dk.astype(BF16)
    gm_ref[:, pl.ds(pl.multiple_of((2 * pairs + pair) * LANES, LANES), LANES)] = dv_acc[...].astype(BF16)


def attention(qkv, grad_context, seg_row, cos_rows, sine_rows):
    length, wide = qkv.shape
    pairs = wide // (3 * LANES)
    block = min(256, length)
    column = lambda shift: pl.BlockSpec((length, LANES), lambda p: (0, shift + p))
    whole = lambda *shape: pl.BlockSpec(shape, lambda p: (0, 0))
    flops = pairs * 2 * 6 * 2 * length * length * LANES // 2
    return pl.pallas_call(
        functools.partial(attention_kernel, block=block),
        grid=(pairs,),
        in_specs=[
            column(0),
            column(pairs),
            column(2 * pairs),
            column(0),
            whole(1, length),
            whole(length, 1),
            whole(length, LANES),
            whole(length, LANES),
        ],
        out_specs=[column(0), whole(length, wide)],
        out_shape=[
            jax.ShapeDtypeStruct((length, pairs * LANES), BF16),
            jax.ShapeDtypeStruct((length, wide), BF16),
        ],
        scratch_shapes=[pltpu.VMEM((length, LANES), F32), pltpu.VMEM((length, LANES), F32)],
        compiler_params=pltpu.CompilerParams(vmem_limit_bytes=48 << 20),
        cost_estimate=pl.CostEstimate(
            flops=flops, bytes_accessed=6 * length * wide, transcendentals=pairs * length * length
        ),
        name="attention",
    )(qkv, qkv, qkv, grad_context, seg_row, seg_row.reshape(length, 1), cos_rows, sine_rows)


def feed_kernel(a_ref, g_ref, up_ref, bias_ref, down_ref, act_ref, gup_ref, sum_ref, *, chunk):
    units = up_ref.shape[1]

    @pl.when(pl.program_id(0) == 0)
    def _():
        sum_ref[...] = jnp.zeros_like(sum_ref)

    for begin in range(0, units, chunk):
        cols = pl.ds(begin, chunk)
        up = dot(a_ref[...], up_ref[:, cols]) + bias_ref[:, cols]
        pull = dot(g_ref[...], down_ref[cols, :], NT)
        gate = 0.5 * (1.0 + lax.erf(up * 0.5**0.5))
        bell = jnp.exp(-0.5 * up * up) * 0.3989422804014327
        act_ref[:, cols] = (up * gate).astype(BF16)
        grad = (pull * (gate + up * bell)).astype(BF16)
        gup_ref[:, cols] = grad
        sum_ref[:, cols] += jnp.sum(grad.astype(F32), axis=0, keepdims=True)


def feed(normed, cot, up_weight, up_bias, down_weight):
    tokens, width = normed.shape
    units = up_weight.shape[1]
    block = min(256, tokens)
    rows = lambda size: pl.BlockSpec((block, size), lambda i: (i, 0))
    whole = lambda *shape: pl.BlockSpec(shape, lambda i: (0, 0))
    return pl.pallas_call(
        functools.partial(feed_kernel, chunk=min(256, units)),
        grid=(tokens // block,),
        in_specs=[rows(width), rows(width), whole(width, units), whole(1, units), whole(units, width)],
        out_specs=[rows(units), rows(units), whole(1, units)],
        out_shape=[
            jax.ShapeDtypeStruct((tokens, units), BF16),
            jax.ShapeDtypeStruct((tokens, units), BF16),
            jax.ShapeDtypeStruct((1, units), F32),
        ],
        compiler_params=pltpu.CompilerParams(vmem_limit_bytes=48 << 20),
        cost_estimate=pl.CostEstimate(
            flops=4 * tokens * width * units,
            bytes_accessed=4 * tokens * width + 4 * width * units + 4 * tokens * units,
            transcendentals=2 * tokens * units,
        ),
        name="feed",
    )(normed, cot, up_weight, up_bias, down_weight)


def normalize(values):
    centred = values - jnp.mean(values, axis=-1, keepdims=True)
    variance = jnp.mean(centred * centred, axis=-1, keepdims=True)
    inv_std = lax.rsqrt(variance + EPS)
    return centred * inv_std, inv_std


def make_local(groups, rows, cols):
    quarters = groups // 2

    def pair_swap(value):
        return lax.ppermute(value, "dp", [(d, d ^ 1) for d in range(groups)])

    def quarter_shift(value, shift):
        moves = [(2 * a + b, 2 * ((a + shift) % quarters) + b) for a in range(quarters) for b in range(2)]
        return lax.ppermute(value, "dp", moves)

    def row_shift(value, shift):
        return lax.ppermute(value, "row", [(r, (r + shift) % rows) for r in range(rows)])

    def core_swap(value):
        return lax.ppermute(value, "col", [(0, 1), (1, 0)])

    def local(
        hidden,
        segments,
        ln1_gain,
        ln1_bias,
        qkv_weight,
        qkv_bias,
        out_weight,
        out_bias,
        ln2_gain,
        ln2_bias,
        up_weight,
        up_bias,
        down_weight,
        down_bias,
        cotangent,
    ):
        assert segments.shape[0] == 1 and cols == 2
        length = segments.shape[1]
        half_width = hidden.shape[1]
        width = 2 * half_width
        shard = qkv_weight.shape[0]
        heads = qkv_weight.shape[1] // (3 * HEAD_DIM) // 2
        wide = heads * HEAD_DIM
        units = up_weight.shape[1] // 2
        whole_heads = heads % quarters == 0
        dp = lax.axis_index("dp")
        row = lax.axis_index("row")
        col = lax.axis_index("col")
        side = lax.rem(dp, 2)
        quarter = dp // 2

        def both(mine, other):
            flip = col == 0
            return jnp.concatenate([jnp.where(flip, mine, other), jnp.where(flip, other, mine)], axis=-1)

        def half_of(value, axis):
            size = value.shape[axis] // 2
            return lax.dynamic_slice_in_dim(value, side * size, size, axis)

        def piece_of(value, shift, axis, placed=False):
            size = value.shape[axis] // quarters
            if placed:
                return lax.slice_in_dim(value, shift * size, (shift + 1) * size, axis=axis)
            return lax.dynamic_slice_in_dim(value, lax.rem(quarter - shift + quarters, quarters) * size, size, axis)

        def in_place(pieces, axis):
            if quarters == 1:
                return pieces[0]
            if quarters == 2:
                flip = quarter == 0
                first = jnp.where(flip, pieces[0], pieces[1])
                second = jnp.where(flip, pieces[1], pieces[0])
                return jnp.concatenate([first, second], axis=axis)
            order = lax.rem(quarter - jnp.arange(quarters) + quarters, quarters)
            stacked = jnp.take(jnp.stack(pieces), order, axis=0)
            return jnp.concatenate([stacked[i] for i in range(quarters)], axis=axis)

        def near(pieces, axis, keep):
            return jnp.concatenate(pieces, axis=axis) if keep else in_place(pieces, axis)

        def gather(value, width_axis, unit_axis, keep):
            mine = piece_of(value, 0, unit_axis)
            received = {0: mine}
            ahead = behind = mine
            for step in range(1, rows):
                if step <= rows // 2:
                    ahead = row_shift(ahead, -1)
                    received[step] = ahead
                if step <= (rows - 1) // 2:
                    behind = row_shift(behind, 1)
                    received[rows - step] = behind
            result = jnp.zeros(
                [width if i == width_axis else n for i, n in enumerate(value.shape)], value.dtype
            )
            for step in range(rows):
                if step == 0:
                    pieces = [piece_of(value, q, unit_axis) for q in range(quarters)]
                else:
                    pieces = [received[step]]
                    pieces += [quarter_shift(received[step], q) for q in range(1, quarters)]
                block = near(pieces, unit_axis, keep)
                place = lax.rem(row + step, rows) * shard
                result = lax.dynamic_update_slice_in_dim(result, block, place, width_axis)
            return result

        hidden_other = core_swap(hidden)
        hidden_far = pair_swap(hidden)
        cot_other = core_swap(cotangent)
        cot_far = pair_swap(cotangent)
        params = jnp.stack([ln1_gain, ln1_bias, ln2_gain, ln2_bias])
        params = both(params, core_swap(params)).astype(F32)
        gain_one, shift_one, gain_two, shift_two = [params[i][None, :] for i in range(4)]
        inputs = [both(hidden, hidden_other), both(hidden_far, core_swap(hidden_far))]
        cots = [both(cotangent, cot_other), both(cot_far, core_swap(cot_far))]
        segs = [segments, pair_swap(segments)]

        qkv_cols = qkv_weight.reshape(shard, 2, heads, 3, HEAD_DIM)
        qkv_cols = lax.dynamic_index_in_dim(qkv_cols, side, 1, keepdims=False)
        qkv_cols = jnp.swapaxes(qkv_cols, 1, 2).reshape(shard, 3, wide)
        qkv_all = gather(qkv_cols, 0, 2, whole_heads).reshape(width, 3 * wide)
        out_all = gather(half_of(out_weight, 0), 1, 0, whole_heads)
        up_all = gather(half_of(up_weight, 1), 0, 1, True)
        down_all = gather(half_of(down_weight, 0), 1, 0, True)

        bias_cols = lax.dynamic_index_in_dim(qkv_bias.reshape(2, heads, 3, HEAD_DIM), side, 0, keepdims=False)
        bias_cols = jnp.swapaxes(bias_cols, 0, 1).reshape(1, 3, wide)
        bias_cols = near([piece_of(bias_cols, q, 2) for q in range(quarters)], 2, whole_heads)
        bias_cols = bias_cols.reshape(1, 3 * wide).astype(F32)
        up_half = half_of(up_bias, 0)
        up_row = jnp.concatenate([piece_of(up_half, q, 0) for q in range(quarters)])[None, :].astype(F32)

        norms = []
        contexts = []
        grads_mixed = []
        for values, cot, seg in zip(inputs, cots, segs):
            unit, inv = normalize(values.astype(F32))
            act_one = (unit * gain_one + shift_one).astype(BF16)
            act_two = (unit * gain_two + shift_two).astype(BF16)
            norms.append((unit, inv, act_one, act_two))
            cos_rows, sine_rows = rotary_tables(doc_positions(seg).reshape(length))
            mixed = dot(act_one, qkv_all) + bias_cols
            cos_wide = jnp.tile(cos_rows, (1, 2 * wide // LANES))
            sine_wide = jnp.tile(sine_rows, (1, 2 * wide // LANES))
            turned = mixed[:, : 2 * wide]
            lane = jnp.arange(2 * wide) % HEAD_DIM
            swapped = jnp.where(
                lane < ROT // 2, jnp.roll(turned, -(ROT // 2), axis=1), jnp.roll(turned, ROT // 2, axis=1)
            )
            turned = turned * cos_wide + swapped * sine_wide
            qkv = jnp.concatenate([turned, mixed[:, 2 * wide :]], axis=1).astype(BF16)
            grad_context = dot(cot, out_all, NT).astype(BF16)
            context, grad_mixed = attention(qkv, grad_context, seg, cos_rows, sine_rows)
            contexts.append(context)
            grads_mixed.append(grad_mixed)

        feeds = [feed(norm[3], cot, up_all, up_row, down_all) for norm, cot in zip(norms, cots)]

        def reduce_grad(left, right, width_axis, unit_axis, placed, shape=None):
            total = dot(left[0], right[0], TN) + dot(left[1], right[1], TN)
            if shape is not None:
                total = total.reshape(shape)
            mine = piece_of(total, 0, unit_axis, placed)
            for q in range(1, quarters):
                part = piece_of(total, q, unit_axis, placed).astype(BF16)
                mine = mine + quarter_shift(part, -q).astype(F32)
            cut = lambda t: lax.dynamic_slice_in_dim(mine, lax.rem(row + t, rows) * shard, shard, width_axis)
            result = cut(0)
            for t in range(1, rows):
                result = result + row_shift(cut(t).astype(BF16), t).astype(F32)
            result = result.astype(BF16)
            pieces = [result] + [quarter_shift(result, q) for q in range(1, quarters)]
            result = in_place(pieces, unit_axis)
            far = pair_swap(result)
            flip = side == 0
            return jnp.concatenate(
                [jnp.where(flip, result, far), jnp.where(flip, far, result)], axis=unit_axis
            ).astype(F32)

        acts_one = [n[2] for n in norms]
        acts_two = [n[3] for n in norms]
        out_grad = reduce_grad(contexts, cots, 1, 0, whole_heads)
        qkv_grad = reduce_grad(acts_one, grads_mixed, 0, 2, whole_heads, (width, 3, wide))
        down_grad = reduce_grad([f[0] for f in feeds], cots, 1, 0, True)
        up_grad = reduce_grad(acts_two, [f[1] for f in feeds], 0, 1, True)
        qkv_grad = qkv_grad.reshape(shard, 3, 2 * heads, HEAD_DIM)
        qkv_grad = jnp.swapaxes(qkv_grad, 1, 2).reshape(shard, 6 * wide)

        outs = []
        slopes = []
        norm_sums = jnp.zeros((4, width), F32)
        for index in range(2):
            unit, inv, _, _ = norms[index]
            act, grad_up, _ = feeds[index]
            outs.append((dot(contexts[index], out_all) + dot(act, down_all)).astype(BF16))
            grad_one = dot(grads_mixed[index], qkv_all, NT)
            grad_two = dot(grad_up, up_all, NT)
            norm_sums += jnp.stack(
                [
                    jnp.sum(grad_one * unit, axis=0),
                    jnp.sum(grad_one, axis=0),
                    jnp.sum(grad_two * unit, axis=0),
                    jnp.sum(grad_two, axis=0),
                ]
            )
            scaled = grad_one * gain_one + grad_two * gain_two
            mean_scaled = jnp.mean(scaled, axis=1, keepdims=True)
            mean_unit = jnp.mean(scaled * unit, axis=1, keepdims=True)
            slopes.append((inv * (scaled - mean_scaled - unit * mean_unit)).astype(BF16))

        def fold(pair):
            sums = []
            for value in pair:
                kept = lax.dynamic_slice_in_dim(value, col * half_width, half_width, 1).astype(F32)
                given = lax.dynamic_slice_in_dim(value, (1 - col) * half_width, half_width, 1)
                sums.append(kept + core_swap(given).astype(F32))
            return sums[0] + pair_swap(sums[1].astype(BF16)).astype(F32)

        cot_local = cotangent.astype(F32)
        output = hidden.astype(F32) + fold(outs) + (out_bias.astype(F32) + down_bias.astype(F32))
        input_grad = cot_local + fold(slopes)

        qkv_sum = (
            jnp.sum(grads_mixed[0].astype(F32), axis=0) + jnp.sum(grads_mixed[1].astype(F32), axis=0)
        ).reshape(3, wide)
        if whole_heads:
            qkv_sum = in_place([piece_of(qkv_sum, q, 1, True) for q in range(quarters)], 1)
        up_sum = (feeds[0][2] + feeds[1][2])[0]
        up_sum = in_place([piece_of(up_sum, q, 0, True) for q in range(quarters)], 0)

        def widen(value):
            zeros = jnp.zeros_like(value)
            flip = side == 0
            return jnp.concatenate([jnp.where(flip, value, zeros), jnp.where(flip, zeros, value)], axis=-1)

        kept = lax.dynamic_slice_in_dim(norm_sums, col * half_width, half_width, 1)
        given = lax.dynamic_slice_in_dim(norm_sums, (1 - col) * half_width, half_width, 1)
        norm_sums = kept + core_swap(given)
        small = jnp.concatenate(
            [widen(qkv_sum).reshape(-1), widen(up_sum), jnp.sum(cot_local, axis=0), norm_sums.reshape(-1)]
        )
        small = lax.psum(small, ("dp", "row"))
        sizes = [6 * wide, 2 * units, half_width, half_width, half_width, half_width, half_width]
        parts = []
        start = 0
        for size in sizes:
            parts.append(lax.slice_in_dim(small, start, start + size))
            start += size
        qkv_sum, up_sum, cot_sum, gain_one_sum, shift_one_sum, gain_two_sum, shift_two_sum = parts
        qkv_sum = jnp.swapaxes(qkv_sum.reshape(3, 2 * heads, HEAD_DIM), 0, 1).reshape(-1)
        return (
            output,
            input_grad,
            gain_one_sum,
            shift_one_sum,
            qkv_grad,
            qkv_sum,
            out_grad,
            cot_sum,
            gain_two_sum,
            shift_two_sum,
            up_grad,
            up_sum,
            down_grad,
            cot_sum,
        )

    return local


def solution(mesh):
    placed = (
        P(("dp", "row"), "col"),
        P(("dp", "row"), None),
        P("col"),
        P("col"),
        P("row", "col"),
        P("col"),
        P("col", "row"),
        P("col"),
        P("col"),
        P("col"),
        P("row", "col"),
        P("col"),
        P("col", "row"),
        P("col"),
        P(("dp", "row"), "col"),
    )
    return jax.shard_map(
        make_local(mesh.shape["dp"], mesh.shape["row"], mesh.shape["col"]),
        mesh=mesh,
        in_specs=placed,
        out_specs=(
            P(("dp", "row"), "col"),
            P(("dp", "row"), "col"),
            P("col"),
            P("col"),
            P("row", "col"),
            P("col"),
            P("col", "row"),
            P("col"),
            P("col"),
            P("col"),
            P("row", "col"),
            P("col"),
            P("col", "row"),
            P("col"),
        ),
        check_vma=False,
    )
```

```python
import functools

import jax
import jax.numpy as jnp
from jax import lax
from jax.experimental import pallas as pl
from jax.experimental.pallas import tpu as pltpu
from jax.sharding import PartitionSpec as P

HEAD_DIM = 64
ROT = 16
EPS = 1e-05
MAX_DOC = 512
LANES = 128
BF16 = jnp.bfloat16
F32 = jnp.float32

NT = (((1,), (1,)), ((), ()))
TN = (((0,), (0,)), ((), ()))
NN = (((1,), (0,)), ((), ()))


def dot(a, b, dims=NN):
    return lax.dot_general(a, b, dims, preferred_element_type=F32)


def doc_positions(segments):
    length = segments.shape[-1]
    places = jnp.arange(length, dtype=jnp.int32)
    changed = jnp.concatenate(
        [jnp.ones(segments.shape[:-1] + (1,), dtype=bool), segments[..., 1:] != segments[..., :-1]],
        axis=-1,
    )
    starts = lax.cummax(jnp.where(changed, places, jnp.zeros_like(places)), axis=segments.ndim - 1)
    return places - starts


def rotary_tables(positions):
    lane = jnp.arange(LANES) % HEAD_DIM
    frequency = 10000.0 ** (-2.0 * (lane % (ROT // 2)).astype(F32) / ROT)
    turning = lane < ROT
    angles = positions.astype(F32)[:, None] * jnp.where(turning, frequency, 0.0)[None, :]
    sign = jnp.where(turning, jnp.where(lane < ROT // 2, -1.0, 1.0), 0.0)
    return jnp.cos(angles), jnp.sin(angles) * sign[None, :]


def turn(values, cos_rows, sine_rows, low_lanes):
    half = ROT // 2
    up = pltpu.roll(values, values.shape[1] - half, 1)
    down = pltpu.roll(values, half, 1)
    return values * cos_rows + jnp.where(low_lanes, up, down) * sine_rows


def attention_kernel(
    q_ref, k_ref, v_ref, gc_ref, seg_row_ref, seg_col_ref, cos_ref, sin_ref, ctx_ref, gm_ref, dk_acc, dv_acc, *, block
):
    pair = pl.program_id(0)
    pairs = pl.num_programs(0)
    length = q_ref.shape[0]
    lane = lax.broadcasted_iota(jnp.int32, (1, LANES), 1)
    low_lanes = lane % HEAD_DIM < ROT // 2
    first = lane < HEAD_DIM
    zero = jnp.zeros((), BF16)

    def split(values):
        return [jnp.where(first, values, zero), jnp.where(first, zero, values)]

    dk_acc[...] = jnp.zeros_like(dk_acc)
    dv_acc[...] = jnp.zeros_like(dv_acc)
    for begin in range(0, length, block):
        low = max(0, begin - (MAX_DOC - 1)) // LANES * LANES
        rows = pl.ds(begin, block)
        keys = pl.ds(low, begin + block - low)
        width = begin + block - low
        q_parts = split(q_ref[rows, :] * jnp.asarray(HEAD_DIM**-0.5, BF16))
        g_parts = split(gc_ref[rows, :])
        k_block = k_ref[keys, :]
        v_block = v_ref[keys, :]
        places = begin + lax.broadcasted_iota(jnp.int32, (block, width), 0)
        key_places = low + lax.broadcasted_iota(jnp.int32, (block, width), 1)
        allowed = (seg_col_ref[rows, :] == seg_row_ref[:, keys]) & (places >= key_places)
        probs = []
        grads = []
        for part in range(2):
            scores = dot(q_parts[part], k_block, NT)
            scores = jnp.where(allowed, scores, -1e30)
            top = jnp.max(scores, axis=1, keepdims=True)
            powers = jnp.exp(scores - top)
            total = jnp.sum(powers, axis=1, keepdims=True)
            chances = powers * (1.0 / total)
            slopes = dot(g_parts[part], v_block, NT)
            inner = jnp.sum(slopes * chances, axis=1, keepdims=True)
            probs.append(chances.astype(BF16))
            grads.append((chances * (slopes - inner)).astype(BF16))
        context = jnp.where(first, dot(probs[0], v_block), dot(probs[1], v_block))
        ctx_ref[rows, :] = context.astype(BF16)
        dq = jnp.where(first, dot(grads[0], k_block), dot(grads[1], k_block)) * HEAD_DIM**-0.5
        dq = turn(dq, cos_ref[rows, :], -sin_ref[rows, :], low_lanes)
        gm_ref[rows, pl.ds(pl.multiple_of(pair * LANES, LANES), LANES)] = dq.astype(BF16)
        dk_acc[keys, :] += dot(grads[0], q_parts[0], TN) + dot(grads[1], q_parts[1], TN)
        dv_acc[keys, :] += dot(probs[0], g_parts[0], TN) + dot(probs[1], g_parts[1], TN)
    dk = turn(dk_acc[...], cos_ref[...], -sin_ref[...], low_lanes)
    gm_ref[:, pl.ds(pl.multiple_of((pairs + pair) * LANES, LANES), LANES)] = dk.astype(BF16)
    gm_ref[:, pl.ds(pl.multiple_of((2 * pairs + pair) * LANES, LANES), LANES)] = dv_acc[...].astype(BF16)


def attention(qkv, grad_context, seg_row, cos_rows, sine_rows):
    length, wide = qkv.shape
    pairs = wide // (3 * LANES)
    block = min(256, length)
    column = lambda shift: pl.BlockSpec((length, LANES), lambda p: (0, shift + p))
    whole = lambda *shape: pl.BlockSpec(shape, lambda p: (0, 0))
    flops = pairs * 2 * 6 * 2 * length * length * LANES // 2
    return pl.pallas_call(
        functools.partial(attention_kernel, block=block),
        grid=(pairs,),
        in_specs=[
            column(0),
            column(pairs),
            column(2 * pairs),
            column(0),
            whole(1, length),
            whole(length, 1),
            whole(length, LANES),
            whole(length, LANES),
        ],
        out_specs=[column(0), whole(length, wide)],
        out_shape=[
            jax.ShapeDtypeStruct((length, pairs * LANES), BF16),
            jax.ShapeDtypeStruct((length, wide), BF16),
        ],
        scratch_shapes=[pltpu.VMEM((length, LANES), F32), pltpu.VMEM((length, LANES), F32)],
        compiler_params=pltpu.CompilerParams(vmem_limit_bytes=48 << 20),
        cost_estimate=pl.CostEstimate(
            flops=flops, bytes_accessed=6 * length * wide, transcendentals=pairs * length * length
        ),
        name="attention",
    )(qkv, qkv, qkv, grad_context, seg_row, seg_row.reshape(length, 1), cos_rows, sine_rows)


def feed_kernel(a_ref, g_ref, up_ref, bias_ref, down_ref, act_ref, gup_ref, sum_ref, *, chunk):
    units = up_ref.shape[1]

    @pl.when(pl.program_id(0) == 0)
    def _():
        sum_ref[...] = jnp.zeros_like(sum_ref)

    for begin in range(0, units, chunk):
        cols = pl.ds(begin, chunk)
        up = dot(a_ref[...], up_ref[:, cols]) + bias_ref[:, cols]
        pull = dot(g_ref[...], down_ref[cols, :], NT)
        gate = 0.5 * (1.0 + lax.erf(up * 0.5**0.5))
        bell = jnp.exp(-0.5 * up * up) * 0.3989422804014327
        act_ref[:, cols] = (up * gate).astype(BF16)
        grad = (pull * (gate + up * bell)).astype(BF16)
        gup_ref[:, cols] = grad
        sum_ref[:, cols] += jnp.sum(grad.astype(F32), axis=0, keepdims=True)


def feed(normed, cot, up_weight, up_bias, down_weight):
    tokens, width = normed.shape
    units = up_weight.shape[1]
    block = min(256, tokens)
    rows = lambda size: pl.BlockSpec((block, size), lambda i: (i, 0))
    whole = lambda *shape: pl.BlockSpec(shape, lambda i: (0, 0))
    return pl.pallas_call(
        functools.partial(feed_kernel, chunk=min(256, units)),
        grid=(tokens // block,),
        in_specs=[rows(width), rows(width), whole(width, units), whole(1, units), whole(units, width)],
        out_specs=[rows(units), rows(units), whole(1, units)],
        out_shape=[
            jax.ShapeDtypeStruct((tokens, units), BF16),
            jax.ShapeDtypeStruct((tokens, units), BF16),
            jax.ShapeDtypeStruct((1, units), F32),
        ],
        compiler_params=pltpu.CompilerParams(vmem_limit_bytes=48 << 20),
        cost_estimate=pl.CostEstimate(
            flops=4 * tokens * width * units,
            bytes_accessed=4 * tokens * width + 4 * width * units + 4 * tokens * units,
            transcendentals=2 * tokens * units,
        ),
        name="feed",
    )(normed, cot, up_weight, up_bias, down_weight)


MESH = pl.DeviceIdType.MESH


class Net:
    def __init__(self, send_sems, recv_sems):
        self.send_sems, self.recv_sems = send_sems, recv_sems
        self.slots = {}
        self.pending = []

    def slot(self, key):
        return self.slots.setdefault(key, len(self.slots))

    def make(self, key, source, target, device):
        i = self.slot(key)
        return pltpu.make_async_remote_copy(
            src_ref=source,
            dst_ref=target,
            send_sem=self.send_sems.at[i],
            recv_sem=self.recv_sems.at[i],
            device_id=device,
            device_id_type=MESH,
        )

    def send(self, key, source, target, device):
        copy = self.make(key, source, target, device)
        copy.start()
        self.pending.append(copy)

    def wait(self, key, landed, device):
        self.make(key, landed, landed, device).wait_recv()

    def drain(self):
        for copy in self.pending:
            copy.wait_send()
        self.pending = []


def spread(columns, width):
    return jnp.concatenate([columns] * (width // LANES), axis=1)


def attend_pair(mix, base, gc, gc_base, ctx, seg_row, seg_col, cos_tab, sin_tab, dk_acc, dv_acc, block):
    length = mix.shape[0]
    lane = lax.broadcasted_iota(jnp.int32, (1, LANES), 1)
    low_lanes = lane % HEAD_DIM < ROT // 2
    first = lane < HEAD_DIM
    zero = jnp.zeros((), BF16)
    cols = [pl.ds(base + i * LANES, LANES) for i in range(3)]
    head_cols = pl.ds(gc_base, LANES)

    def split(values):
        return [jnp.where(first, values, zero), jnp.where(first, zero, values)]

    dk_acc[...] = jnp.zeros_like(dk_acc)
    dv_acc[...] = jnp.zeros_like(dv_acc)
    for begin in range(0, length, block):
        low = max(0, begin - (MAX_DOC - 1)) // LANES * LANES
        width = begin + block - low
        rows = pl.ds(begin, block)
        keys = pl.ds(low, width)
        q_parts = split(mix[rows, cols[0]] * jnp.asarray(HEAD_DIM**-0.5, BF16))
        g_parts = split(gc[rows, head_cols])
        k_block = mix[keys, cols[1]]
        v_block = mix[keys, cols[2]]
        places = begin + lax.broadcasted_iota(jnp.int32, (block, width), 0)
        key_places = low + lax.broadcasted_iota(jnp.int32, (block, width), 1)
        allowed = (spread(seg_col[rows, :], width) == seg_row[0:1, keys]) & (places >= key_places)
        probs = []
        grads = []
        for part in range(2):
            scores = dot(q_parts[part], k_block, NT)
            scores = jnp.where(allowed, scores, -1e30)
            top = jnp.max(scores, axis=1, keepdims=True)
            powers = jnp.exp(scores - top)
            total = jnp.sum(powers, axis=1, keepdims=True)
            chances = powers * (1.0 / total)
            slopes = dot(g_parts[part], v_block, NT)
            inner = jnp.sum(slopes * chances, axis=1, keepdims=True)
            probs.append(chances.astype(BF16))
            grads.append((chances * (slopes - inner)).astype(BF16))
        ctx[rows, head_cols] = jnp.where(first, dot(probs[0], v_block), dot(probs[1], v_block)).astype(BF16)
        dq = jnp.where(first, dot(grads[0], k_block), dot(grads[1], k_block)) * HEAD_DIM**-0.5
        mix[rows, cols[0]] = turn(dq, cos_tab[rows, :], -sin_tab[rows, :], low_lanes).astype(BF16)
        dk_acc[keys, :] += dot(grads[0], q_parts[0], TN) + dot(grads[1], q_parts[1], TN)
        dv_acc[keys, :] += dot(probs[0], g_parts[0], TN) + dot(probs[1], g_parts[1], TN)
    mix[:, cols[1]] = turn(dk_acc[...], cos_tab[...], -sin_tab[...], low_lanes).astype(BF16)
    mix[:, cols[2]] = dv_acc[...].astype(BF16)


def first_kernel(
    hidden, cot, wq_in, wo_in, wu_in, wd_in, rows_in, params_in, bq_in, freq_in,
    x_out, g_out, a_out, wq_out, wo_out, wu_out, wd_out, mix_out, ctx_out, rows_out, params_out,
    X, G, A, WQ, WO, WU, WD, MIX, GC, CTX, rows_far, params, seg_col, cos_tab, sin_tab, dk_acc, dv_acc,
    send_sems, recv_sems, local_sems, *, rows_n,
):
    R = rows_n
    dp, row, col = lax.axis_index("dp"), lax.axis_index("row"), lax.axis_index("col")
    side, quarter = lax.rem(dp, 2), lax.div(dp, 2)
    length, half = hidden.shape
    shard = wq_in.shape[0]
    core = (dp, row, 1 - col)
    xdev = (dp + 1 - 2 * side, row, col)
    ydev = (side + 2 * (1 - quarter), row, col)

    def zdev(t):
        return (dp, lax.rem(row + t + R, R), col)

    barrier = pltpu.get_barrier_semaphore()
    peers = [core, xdev, ydev] + [zdev(t) for t in range(1, R)]
    for peer in peers:
        pl.semaphore_signal(barrier, inc=1, device_id=peer, device_id_type=MESH)
    pl.semaphore_wait(barrier, len(peers))

    net = Net(send_sems, recv_sems)
    own_cols = pl.ds(pl.multiple_of(col * half, half), half)
    far_cols = pl.ds(pl.multiple_of((1 - col) * half, half), half)
    local = []

    def move(source, target):
        copy = pltpu.make_async_copy(source, target, local_sems.at[len(local)])
        copy.start()
        local.append(copy)
        return copy

    net.send("core h", hidden, X.at[0, :, own_cols], core)
    net.send("core p", params_in, params.at[:, own_cols], core)
    net.send("x rows", rows_in, rows_far, xdev)
    here_h = move(hidden, X.at[0, :, own_cols])
    here_p = move(params_in, params.at[:, own_cols])

    qc = WQ.shape[1] // 2
    oc = WO.shape[0] // 2
    uc = WU.shape[1] // 2
    unit_at = pl.multiple_of((side * 2 + quarter) * uc, uc)
    unit_other = pl.multiple_of((side * 2 + 1 - quarter) * uc, uc)
    head_at = pl.multiple_of((side * 2 + quarter) * oc, oc)
    head_other = pl.multiple_of((side * 2 + 1 - quarter) * oc, oc)

    def block(t):
        return pl.ds(pl.multiple_of(lax.rem(row + t + R, R) * shard, shard), shard)

    weights = {
        "q": (wq_in.at[:, pl.ds(0, qc)], wq_in.at[:, pl.ds(qc, qc)], lambda t, h: WQ.at[block(t), pl.ds(h * qc, qc)]),
        "o": (wo_in.at[pl.ds(head_at, oc), :], wo_in.at[pl.ds(head_other, oc), :], lambda t, h: WO.at[pl.ds(h * oc, oc), block(t)]),
        "u": (wu_in.at[:, pl.ds(unit_at, uc)], wu_in.at[:, pl.ds(unit_other, uc)], lambda t, h: WU.at[block(t), pl.ds(h * uc, uc)]),
        "d": (wd_in.at[pl.ds(unit_at, uc), :], wd_in.at[pl.ds(unit_other, uc), :], lambda t, h: WD.at[pl.ds(h * uc, uc), block(t)]),
    }
    here_w = {}
    for name, (mine, other, place) in weights.items():
        net.send((name, 1), mine, place(0, 0), zdev(-1))
        if R > 2:
            net.send((name, R - 1), mine, place(0, 0), zdev(1))
        if name == "q":
            here_w[name] = [move(mine, place(0, 0)), move(other, place(0, 1))]
    chunks = 2
    piece = length // chunks
    for c in range(chunks):
        span = pl.ds(c * piece, piece)
        net.send(("x h", c), hidden.at[span, :], X.at[1, span, own_cols], xdev)
    net.send("core g", cot, G.at[0, :, own_cols], core)
    here_g = move(cot, G.at[0, :, own_cols])
    for c in range(chunks):
        span = pl.ds(c * piece, piece)
        net.send(("x g", c), cot.at[span, :], G.at[1, span, own_cols], xdev)
    for name in "oud":
        mine, other, place = weights[name]
        here_w[name] = [move(mine, place(0, 0)), move(other, place(0, 1))]

    def along(name, t):
        place = weights[name][2]
        net.wait((name, t), place(t, 0), zdev(t))
        if t < R // 2:
            net.send((name, t + 1), place(t, 0), place(t, 0), zdev(-1))
        elif R // 2 + 1 < t:
            net.send((name, t - 1), place(t, 0), place(t, 0), zdev(1))
        net.send((name, t, "y"), place(t, 0), place(t, 1), ydev)

    order = [1, R - 1] + [t for t in range(2, R - 1)] if R > 2 else [1]

    def arrive(name):
        place = weights[name][2]
        for copy in here_w[name]:
            copy.wait()
        for t in range(1, R):
            net.wait((name, t, "y"), place(t, 1), ydev)

    def hand_over(name, buffer, c):
        span = pl.ds(c * piece, piece)
        net.wait(("x " + name, c), buffer.at[1, span, own_cols], xdev)
        net.send(("core far " + name, c), buffer.at[1, span, own_cols], buffer.at[1, span, own_cols], core)

    tile = 256
    gain_one, shift_one = 0, 1

    def norm(s, at, gain, shift):
        values = X[s, at, :].astype(F32)
        centred = values - jnp.mean(values, axis=-1, keepdims=True)
        inv = lax.rsqrt(jnp.mean(centred * centred, axis=-1, keepdims=True) + EPS)
        A[s, at, :] = (centred * inv * params[gain : gain + 1, :] + params[shift : shift + 1, :]).astype(BF16)

    def each_tile(body):
        @pl.loop(0, length // tile)
        def _(i):
            body(pl.ds(pl.multiple_of(i * tile, tile), tile))

    lane = lax.broadcasted_iota(jnp.int32, (1, LANES), 1)
    low_lanes = lane % HEAD_DIM < ROT // 2

    def tables(rows):
        columns = jnp.transpose(jnp.broadcast_to(rows[0:1, :], (LANES, length)))
        seg_col[...] = columns
        columns = jnp.transpose(jnp.broadcast_to(rows[1:2, :], (LANES, length)))
        angles = columns * freq_in[0:1, :]
        cos_tab[...] = jnp.cos(angles)
        sin_tab[...] = jnp.sin(angles) * freq_in[1:2, :]

    def project(s):
        def body(at):
            mixed = dot(A[s, at, :], WQ[...]) + bq_in[...]
            for i in range(mixed.shape[1] // LANES):
                part = mixed[:, i * LANES : (i + 1) * LANES]
                if i % 3 < 2:
                    part = turn(part, cos_tab[at, :], sin_tab[at, :], low_lanes)
                MIX[s, at, pl.ds(i * LANES, LANES)] = part.astype(BF16)

        each_tile(body)

    def pull_context(s):
        def body(at):
            GC[at, :] = dot(G[s, at, :], WO[...], NT).astype(BF16)

        each_tile(body)

    def attend(s, rows, pair):
        attend_pair(
            MIX.at[s], pair * 3 * LANES, GC, pair * LANES, CTX.at[s], rows, seg_col, cos_tab, sin_tab, dk_acc, dv_acc, tile
        )

    pairs = CTX.shape[2] // LANES
    tables(rows_in)
    here_h.wait()
    here_p.wait()
    net.wait("core h", X.at[0, :, far_cols], core)
    net.wait("core p", params.at[:, far_cols], core)
    each_tile(lambda at: norm(0, at, gain_one, shift_one))
    for t in order:
        along("q", t)
    for t in order:
        along("o", t)
    arrive("q")
    project(0)
    here_g.wait()
    net.wait("core g", G.at[0, :, far_cols], core)
    hand_over("h", X, 0)
    arrive("o")
    pull_context(0)
    along("u", 1)
    along("u", R - 1)
    for pair in range(pairs):
        attend(0, rows_in, pair)
        hand_over("h" if pair == 0 else "g", X if pair == 0 else G, 1 if pair == 0 else 0)
        along("d", 1 if pair == 0 else R - 1)
        for t in order[2:]:
            along("u" if pair == 0 else "d", t)
    for c in range(chunks):
        span = pl.ds(c * piece, piece)
        net.wait(("core far h", c), X.at[1, span, far_cols], core)
    net.wait("x rows", rows_far, xdev)
    tables(rows_far)
    each_tile(lambda at: norm(1, at, gain_one, shift_one))
    project(1)
    hand_over("g", G, 1)
    for c in range(chunks):
        span = pl.ds(c * piece, piece)
        net.wait(("core far g", c), G.at[1, span, far_cols], core)
    pull_context(1)
    for pair in range(pairs):
        attend(1, rows_far, pair)
    arrive("u")
    arrive("d")
    net.drain()
    done = [
        move(a, b)
        for a, b in [
            (X, x_out), (G, g_out), (A, a_out), (WQ, wq_out), (WO, wo_out), (WU, wu_out), (WD, wd_out),
            (MIX, mix_out), (CTX, ctx_out), (rows_far, rows_out), (params, params_out),
        ]
    ]
    for copy in done:
        copy.wait()


def first(hidden, cot, wq, wo, wu, wd, rows, params, bq, freq, rows_n):
    length, half = hidden.shape
    width = 2 * half
    wide3 = wq.shape[1]
    wide = wide3 // 3
    units = wu.shape[1] // 2
    arrays = [
        ((2, length, width), BF16), ((2, length, width), BF16), ((2, length, width), BF16),
        ((width, wide3), BF16), ((wide, width), BF16), ((width, units), BF16), ((units, width), BF16),
        ((2, length, wide3), BF16), ((2, length, wide), BF16), (rows.shape, F32), ((params.shape[0], width), F32),
    ]
    out_shape = [jax.ShapeDtypeStruct(shape, kind) for shape, kind in arrays]
    buffers = [pltpu.VMEM(shape, kind) for shape, kind in arrays]
    buffers.insert(8, pltpu.VMEM((length, wide), BF16))
    table = pltpu.VMEM((length, LANES), F32)
    any_spec = pl.BlockSpec(memory_space=pl.ANY)
    vmem_spec = pl.BlockSpec(memory_space=pltpu.VMEM)
    return pl.pallas_call(
        functools.partial(first_kernel, rows_n=rows_n),
        out_shape=out_shape,
        in_specs=[any_spec] * 6 + [vmem_spec] * 4,
        out_specs=[any_spec] * len(out_shape),
        scratch_shapes=buffers + [table] * 5 + [
            pltpu.SemaphoreType.DMA((80,)), pltpu.SemaphoreType.DMA((80,)), pltpu.SemaphoreType.DMA((32,)),
        ],
        compiler_params=pltpu.CompilerParams(collective_id=0, has_side_effects=True, vmem_limit_bytes=60 << 20),
        name="first",
    )(hidden, cot, wq, wo, wu, wd, rows, params, bq, freq)


def normalize(values):
    centred = values - jnp.mean(values, axis=-1, keepdims=True)
    variance = jnp.mean(centred * centred, axis=-1, keepdims=True)
    inv_std = lax.rsqrt(variance + EPS)
    return centred * inv_std, inv_std


def make_general(groups, rows, cols):
    quarters = groups // 2

    def pair_swap(value):
        return lax.ppermute(value, "dp", [(d, d ^ 1) for d in range(groups)])

    def quarter_shift(value, shift):
        moves = [(2 * a + b, 2 * ((a + shift) % quarters) + b) for a in range(quarters) for b in range(2)]
        return lax.ppermute(value, "dp", moves)

    def row_shift(value, shift):
        return lax.ppermute(value, "row", [(r, (r + shift) % rows) for r in range(rows)])

    def core_swap(value):
        return lax.ppermute(value, "col", [(0, 1), (1, 0)])

    def local(
        hidden,
        segments,
        ln1_gain,
        ln1_bias,
        qkv_weight,
        qkv_bias,
        out_weight,
        out_bias,
        ln2_gain,
        ln2_bias,
        up_weight,
        up_bias,
        down_weight,
        down_bias,
        cotangent,
    ):
        assert segments.shape[0] == 1 and cols == 2
        length = segments.shape[1]
        half_width = hidden.shape[1]
        width = 2 * half_width
        shard = qkv_weight.shape[0]
        heads = qkv_weight.shape[1] // (3 * HEAD_DIM) // 2
        wide = heads * HEAD_DIM
        units = up_weight.shape[1] // 2
        whole_heads = heads % quarters == 0
        dp = lax.axis_index("dp")
        row = lax.axis_index("row")
        col = lax.axis_index("col")
        side = lax.rem(dp, 2)
        quarter = dp // 2

        def both(mine, other):
            flip = col == 0
            return jnp.concatenate([jnp.where(flip, mine, other), jnp.where(flip, other, mine)], axis=-1)

        def half_of(value, axis):
            size = value.shape[axis] // 2
            return lax.dynamic_slice_in_dim(value, side * size, size, axis)

        def piece_of(value, shift, axis, placed=False):
            size = value.shape[axis] // quarters
            if placed:
                return lax.slice_in_dim(value, shift * size, (shift + 1) * size, axis=axis)
            return lax.dynamic_slice_in_dim(value, lax.rem(quarter - shift + quarters, quarters) * size, size, axis)

        def in_place(pieces, axis):
            if quarters == 1:
                return pieces[0]
            if quarters == 2:
                flip = quarter == 0
                first = jnp.where(flip, pieces[0], pieces[1])
                second = jnp.where(flip, pieces[1], pieces[0])
                return jnp.concatenate([first, second], axis=axis)
            order = lax.rem(quarter - jnp.arange(quarters) + quarters, quarters)
            stacked = jnp.take(jnp.stack(pieces), order, axis=0)
            return jnp.concatenate([stacked[i] for i in range(quarters)], axis=axis)

        def near(pieces, axis, keep):
            return jnp.concatenate(pieces, axis=axis) if keep else in_place(pieces, axis)

        def gather(value, width_axis, unit_axis, keep):
            mine = piece_of(value, 0, unit_axis)
            received = {0: mine}
            ahead = behind = mine
            for step in range(1, rows):
                if step <= rows // 2:
                    ahead = row_shift(ahead, -1)
                    received[step] = ahead
                if step <= (rows - 1) // 2:
                    behind = row_shift(behind, 1)
                    received[rows - step] = behind
            result = jnp.zeros(
                [width if i == width_axis else n for i, n in enumerate(value.shape)], value.dtype
            )
            for step in range(rows):
                if step == 0:
                    pieces = [piece_of(value, q, unit_axis) for q in range(quarters)]
                else:
                    pieces = [received[step]]
                    pieces += [quarter_shift(received[step], q) for q in range(1, quarters)]
                block = near(pieces, unit_axis, keep)
                place = lax.rem(row + step, rows) * shard
                result = lax.dynamic_update_slice_in_dim(result, block, place, width_axis)
            return result

        hidden_other = core_swap(hidden)
        hidden_far = pair_swap(hidden)
        cot_other = core_swap(cotangent)
        cot_far = pair_swap(cotangent)
        params = jnp.stack([ln1_gain, ln1_bias, ln2_gain, ln2_bias])
        params = both(params, core_swap(params)).astype(F32)
        gain_one, shift_one, gain_two, shift_two = [params[i][None, :] for i in range(4)]
        inputs = [both(hidden, hidden_other), both(hidden_far, core_swap(hidden_far))]
        cots = [both(cotangent, cot_other), both(cot_far, core_swap(cot_far))]
        segs = [segments, pair_swap(segments)]

        qkv_cols = qkv_weight.reshape(shard, 2, heads, 3, HEAD_DIM)
        qkv_cols = lax.dynamic_index_in_dim(qkv_cols, side, 1, keepdims=False)
        qkv_cols = jnp.swapaxes(qkv_cols, 1, 2).reshape(shard, 3, wide)
        qkv_all = gather(qkv_cols, 0, 2, whole_heads).reshape(width, 3 * wide)
        out_all = gather(half_of(out_weight, 0), 1, 0, whole_heads)
        up_all = gather(half_of(up_weight, 1), 0, 1, True)
        down_all = gather(half_of(down_weight, 0), 1, 0, True)

        bias_cols = lax.dynamic_index_in_dim(qkv_bias.reshape(2, heads, 3, HEAD_DIM), side, 0, keepdims=False)
        bias_cols = jnp.swapaxes(bias_cols, 0, 1).reshape(1, 3, wide)
        bias_cols = near([piece_of(bias_cols, q, 2) for q in range(quarters)], 2, whole_heads)
        bias_cols = bias_cols.reshape(1, 3 * wide).astype(F32)
        up_half = half_of(up_bias, 0)
        up_row = jnp.concatenate([piece_of(up_half, q, 0) for q in range(quarters)])[None, :].astype(F32)

        norms = []
        contexts = []
        grads_mixed = []
        for values, cot, seg in zip(inputs, cots, segs):
            unit, inv = normalize(values.astype(F32))
            act_one = (unit * gain_one + shift_one).astype(BF16)
            act_two = (unit * gain_two + shift_two).astype(BF16)
            norms.append((unit, inv, act_one, act_two))
            cos_rows, sine_rows = rotary_tables(doc_positions(seg).reshape(length))
            mixed = dot(act_one, qkv_all) + bias_cols
            cos_wide = jnp.tile(cos_rows, (1, 2 * wide // LANES))
            sine_wide = jnp.tile(sine_rows, (1, 2 * wide // LANES))
            turned = mixed[:, : 2 * wide]
            lane = jnp.arange(2 * wide) % HEAD_DIM
            swapped = jnp.where(
                lane < ROT // 2, jnp.roll(turned, -(ROT // 2), axis=1), jnp.roll(turned, ROT // 2, axis=1)
            )
            turned = turned * cos_wide + swapped * sine_wide
            qkv = jnp.concatenate([turned, mixed[:, 2 * wide :]], axis=1).astype(BF16)
            grad_context = dot(cot, out_all, NT).astype(BF16)
            context, grad_mixed = attention(qkv, grad_context, seg, cos_rows, sine_rows)
            contexts.append(context)
            grads_mixed.append(grad_mixed)

        feeds = [feed(norm[3], cot, up_all, up_row, down_all) for norm, cot in zip(norms, cots)]

        def reduce_grad(left, right, width_axis, unit_axis, placed, shape=None):
            total = dot(left[0], right[0], TN) + dot(left[1], right[1], TN)
            if shape is not None:
                total = total.reshape(shape)
            mine = piece_of(total, 0, unit_axis, placed)
            for q in range(1, quarters):
                part = piece_of(total, q, unit_axis, placed).astype(BF16)
                mine = mine + quarter_shift(part, -q).astype(F32)
            cut = lambda t: lax.dynamic_slice_in_dim(mine, lax.rem(row + t, rows) * shard, shard, width_axis)
            result = cut(0)
            for t in range(1, rows):
                result = result + row_shift(cut(t).astype(BF16), t).astype(F32)
            result = result.astype(BF16)
            pieces = [result] + [quarter_shift(result, q) for q in range(1, quarters)]
            result = in_place(pieces, unit_axis)
            far = pair_swap(result)
            flip = side == 0
            return jnp.concatenate(
                [jnp.where(flip, result, far), jnp.where(flip, far, result)], axis=unit_axis
            ).astype(F32)

        acts_one = [n[2] for n in norms]
        acts_two = [n[3] for n in norms]
        out_grad = reduce_grad(contexts, cots, 1, 0, whole_heads)
        qkv_grad = reduce_grad(acts_one, grads_mixed, 0, 2, whole_heads, (width, 3, wide))
        down_grad = reduce_grad([f[0] for f in feeds], cots, 1, 0, True)
        up_grad = reduce_grad(acts_two, [f[1] for f in feeds], 0, 1, True)
        qkv_grad = qkv_grad.reshape(shard, 3, 2 * heads, HEAD_DIM)
        qkv_grad = jnp.swapaxes(qkv_grad, 1, 2).reshape(shard, 6 * wide)

        outs = []
        slopes = []
        norm_sums = jnp.zeros((4, width), F32)
        for index in range(2):
            unit, inv, _, _ = norms[index]
            act, grad_up, _ = feeds[index]
            outs.append((dot(contexts[index], out_all) + dot(act, down_all)).astype(BF16))
            grad_one = dot(grads_mixed[index], qkv_all, NT)
            grad_two = dot(grad_up, up_all, NT)
            norm_sums += jnp.stack(
                [
                    jnp.sum(grad_one * unit, axis=0),
                    jnp.sum(grad_one, axis=0),
                    jnp.sum(grad_two * unit, axis=0),
                    jnp.sum(grad_two, axis=0),
                ]
            )
            scaled = grad_one * gain_one + grad_two * gain_two
            mean_scaled = jnp.mean(scaled, axis=1, keepdims=True)
            mean_unit = jnp.mean(scaled * unit, axis=1, keepdims=True)
            slopes.append((inv * (scaled - mean_scaled - unit * mean_unit)).astype(BF16))

        def fold(pair):
            sums = []
            for value in pair:
                kept = lax.dynamic_slice_in_dim(value, col * half_width, half_width, 1).astype(F32)
                given = lax.dynamic_slice_in_dim(value, (1 - col) * half_width, half_width, 1)
                sums.append(kept + core_swap(given).astype(F32))
            return sums[0] + pair_swap(sums[1].astype(BF16)).astype(F32)

        cot_local = cotangent.astype(F32)
        output = hidden.astype(F32) + fold(outs) + (out_bias.astype(F32) + down_bias.astype(F32))
        input_grad = cot_local + fold(slopes)

        qkv_sum = (
            jnp.sum(grads_mixed[0].astype(F32), axis=0) + jnp.sum(grads_mixed[1].astype(F32), axis=0)
        ).reshape(3, wide)
        if whole_heads:
            qkv_sum = in_place([piece_of(qkv_sum, q, 1, True) for q in range(quarters)], 1)
        up_sum = (feeds[0][2] + feeds[1][2])[0]
        up_sum = in_place([piece_of(up_sum, q, 0, True) for q in range(quarters)], 0)

        def widen(value):
            zeros = jnp.zeros_like(value)
            flip = side == 0
            return jnp.concatenate([jnp.where(flip, value, zeros), jnp.where(flip, zeros, value)], axis=-1)

        kept = lax.dynamic_slice_in_dim(norm_sums, col * half_width, half_width, 1)
        given = lax.dynamic_slice_in_dim(norm_sums, (1 - col) * half_width, half_width, 1)
        norm_sums = kept + core_swap(given)
        small = jnp.concatenate(
            [widen(qkv_sum).reshape(-1), widen(up_sum), jnp.sum(cot_local, axis=0), norm_sums.reshape(-1)]
        )
        small = lax.psum(small, ("dp", "row"))
        sizes = [6 * wide, 2 * units, half_width, half_width, half_width, half_width, half_width]
        parts = []
        start = 0
        for size in sizes:
            parts.append(lax.slice_in_dim(small, start, start + size))
            start += size
        qkv_sum, up_sum, cot_sum, gain_one_sum, shift_one_sum, gain_two_sum, shift_two_sum = parts
        qkv_sum = jnp.swapaxes(qkv_sum.reshape(3, 2 * heads, HEAD_DIM), 0, 1).reshape(-1)
        return (
            output,
            input_grad,
            gain_one_sum,
            shift_one_sum,
            qkv_grad,
            qkv_sum,
            out_grad,
            cot_sum,
            gain_two_sum,
            shift_two_sum,
            up_grad,
            up_sum,
            down_grad,
            cot_sum,
        )

    return local


def make_fast(groups, rows, cols):
    quarters = groups // 2

    def pair_swap(value):
        return lax.ppermute(value, "dp", [(d, d ^ 1) for d in range(groups)])

    def quarter_shift(value, shift):
        moves = [(2 * a + b, 2 * ((a + shift) % quarters) + b) for a in range(quarters) for b in range(2)]
        return lax.ppermute(value, "dp", moves)

    def row_shift(value, shift):
        return lax.ppermute(value, "row", [(r, (r + shift) % rows) for r in range(rows)])

    def core_swap(value):
        return lax.ppermute(value, "col", [(0, 1), (1, 0)])

    def local(
        hidden,
        segments,
        ln1_gain,
        ln1_bias,
        qkv_weight,
        qkv_bias,
        out_weight,
        out_bias,
        ln2_gain,
        ln2_bias,
        up_weight,
        up_bias,
        down_weight,
        down_bias,
        cotangent,
    ):
        assert segments.shape[0] == 1 and cols == 2
        length = segments.shape[1]
        half_width = hidden.shape[1]
        width = 2 * half_width
        shard = qkv_weight.shape[0]
        heads = qkv_weight.shape[1] // (3 * HEAD_DIM) // 2
        wide = heads * HEAD_DIM
        units = up_weight.shape[1] // 2
        whole_heads = heads % quarters == 0
        dp = lax.axis_index("dp")
        row = lax.axis_index("row")
        col = lax.axis_index("col")
        side = lax.rem(dp, 2)
        quarter = dp // 2

        def both(mine, other):
            flip = col == 0
            return jnp.concatenate([jnp.where(flip, mine, other), jnp.where(flip, other, mine)], axis=-1)

        def half_of(value, axis):
            size = value.shape[axis] // 2
            return lax.dynamic_slice_in_dim(value, side * size, size, axis)

        def piece_of(value, shift, axis, placed=False):
            size = value.shape[axis] // quarters
            if placed:
                return lax.slice_in_dim(value, shift * size, (shift + 1) * size, axis=axis)
            return lax.dynamic_slice_in_dim(value, lax.rem(quarter - shift + quarters, quarters) * size, size, axis)

        def in_place(pieces, axis):
            if quarters == 1:
                return pieces[0]
            if quarters == 2:
                flip = quarter == 0
                first = jnp.where(flip, pieces[0], pieces[1])
                second = jnp.where(flip, pieces[1], pieces[0])
                return jnp.concatenate([first, second], axis=axis)
            order = lax.rem(quarter - jnp.arange(quarters) + quarters, quarters)
            stacked = jnp.take(jnp.stack(pieces), order, axis=0)
            return jnp.concatenate([stacked[i] for i in range(quarters)], axis=axis)

        def near(pieces, axis, keep):
            return jnp.concatenate(pieces, axis=axis) if keep else in_place(pieces, axis)

        def gather(value, width_axis, unit_axis, keep):
            mine = piece_of(value, 0, unit_axis)
            received = {0: mine}
            ahead = behind = mine
            for step in range(1, rows):
                if step <= rows // 2:
                    ahead = row_shift(ahead, -1)
                    received[step] = ahead
                if step <= (rows - 1) // 2:
                    behind = row_shift(behind, 1)
                    received[rows - step] = behind
            result = jnp.zeros(
                [width if i == width_axis else n for i, n in enumerate(value.shape)], value.dtype
            )
            for step in range(rows):
                if step == 0:
                    pieces = [piece_of(value, q, unit_axis) for q in range(quarters)]
                else:
                    pieces = [received[step]]
                    pieces += [quarter_shift(received[step], q) for q in range(1, quarters)]
                block = near(pieces, unit_axis, keep)
                place = lax.rem(row + step, rows) * shard
                result = lax.dynamic_update_slice_in_dim(result, block, place, width_axis)
            return result

        place = jnp.arange(length, dtype=jnp.int32)
        before = segments[0][None, :] < segments[0][:, None]
        position = place - jnp.sum(before.astype(jnp.int32), axis=1)
        rows_own = jnp.stack([segments[0].astype(F32), position.astype(F32)] + [jnp.zeros((length,), F32)] * 6)
        params = jnp.stack([ln1_gain, ln1_bias, ln2_gain, ln2_bias] * 2).astype(F32)
        lane = jnp.arange(LANES) % HEAD_DIM
        frequency = 10000.0 ** (-2.0 * (lane % (ROT // 2)).astype(F32) / ROT)
        sign = jnp.where(lane < ROT // 2, -1.0, 1.0)
        turning = lane < ROT
        freq = jnp.stack([jnp.where(turning, frequency, 0.0), jnp.where(turning, sign, 0.0)] * 4).astype(F32)

        def by_quarter(value):
            n = value.shape[0]
            value = value.reshape(n, 2, quarters, heads // quarters, 3, HEAD_DIM)
            value = lax.dynamic_index_in_dim(value, side, 1, keepdims=False)
            value = jnp.swapaxes(value, 2, 3).reshape(n, quarters, 3 * wide // quarters)
            flip = quarter == 0
            mine = jnp.where(flip, value[:, 0], value[:, 1])
            other = jnp.where(flip, value[:, 1], value[:, 0])
            return jnp.concatenate([mine, other], axis=1)

        wq = by_quarter(qkv_weight)
        bq = by_quarter(qkv_bias[None, :]).astype(F32)
        up_half = half_of(up_bias, 0)
        up_row = jnp.concatenate([piece_of(up_half, q, 0) for q in range(quarters)])[None, :].astype(F32)
        x_all, g_all, a_all, qkv_all, out_all, up_all, down_all, mixes, ctxs, rows_far, params = first(
            hidden, cotangent, wq, out_weight, up_weight, down_weight, rows_own, params, bq, freq, rows
        )
        gain_one, shift_one, gain_two, shift_two = [params[i][None, :] for i in range(4)]
        cots = [g_all[0], g_all[1]]
        norms = []
        for index in range(2):
            unit, inv = normalize(x_all[index].astype(F32))
            norms.append((unit, inv, a_all[index], (unit * gain_two + shift_two).astype(BF16)))
        contexts = [ctxs[0], ctxs[1]]
        grads_mixed = [mixes[0], mixes[1]]

        feeds = [feed(norm[3], cot, up_all, up_row, down_all) for norm, cot in zip(norms, cots)]

        def reduce_grad(left, right, width_axis, unit_axis, placed, shape=None):
            total = dot(left[0], right[0], TN) + dot(left[1], right[1], TN)
            if shape is not None:
                total = total.reshape(shape)
            mine = piece_of(total, 0, unit_axis, placed)
            for q in range(1, quarters):
                part = piece_of(total, q, unit_axis, placed).astype(BF16)
                mine = mine + quarter_shift(part, -q).astype(F32)
            cut = lambda t: lax.dynamic_slice_in_dim(mine, lax.rem(row + t, rows) * shard, shard, width_axis)
            result = cut(0)
            for t in range(1, rows):
                result = result + row_shift(cut(t).astype(BF16), t).astype(F32)
            result = result.astype(BF16)
            pieces = [result] + [quarter_shift(result, q) for q in range(1, quarters)]
            result = in_place(pieces, unit_axis)
            far = pair_swap(result)
            flip = side == 0
            return jnp.concatenate(
                [jnp.where(flip, result, far), jnp.where(flip, far, result)], axis=unit_axis
            ).astype(F32)

        acts_one = [n[2] for n in norms]
        acts_two = [n[3] for n in norms]
        out_grad = reduce_grad(contexts, cots, 1, 0, whole_heads)
        qkv_grad = reduce_grad(acts_one, grads_mixed, 0, 1, True)
        down_grad = reduce_grad([f[0] for f in feeds], cots, 1, 0, True)
        up_grad = reduce_grad(acts_two, [f[1] for f in feeds], 0, 1, True)
        qkv_grad = qkv_grad.reshape(shard, 2 * quarters, 3, heads // quarters, HEAD_DIM)
        qkv_grad = jnp.swapaxes(qkv_grad, 2, 3).reshape(shard, 6 * wide)

        outs = []
        slopes = []
        norm_sums = jnp.zeros((4, width), F32)
        for index in range(2):
            unit, inv, _, _ = norms[index]
            act, grad_up, _ = feeds[index]
            outs.append((dot(contexts[index], out_all) + dot(act, down_all)).astype(BF16))
            grad_one = dot(grads_mixed[index], qkv_all, NT)
            grad_two = dot(grad_up, up_all, NT)
            norm_sums += jnp.stack(
                [
                    jnp.sum(grad_one * unit, axis=0),
                    jnp.sum(grad_one, axis=0),
                    jnp.sum(grad_two * unit, axis=0),
                    jnp.sum(grad_two, axis=0),
                ]
            )
            scaled = grad_one * gain_one + grad_two * gain_two
            mean_scaled = jnp.mean(scaled, axis=1, keepdims=True)
            mean_unit = jnp.mean(scaled * unit, axis=1, keepdims=True)
            slopes.append((inv * (scaled - mean_scaled - unit * mean_unit)).astype(BF16))

        def fold(pair):
            sums = []
            for value in pair:
                kept = lax.dynamic_slice_in_dim(value, col * half_width, half_width, 1).astype(F32)
                given = lax.dynamic_slice_in_dim(value, (1 - col) * half_width, half_width, 1)
                sums.append(kept + core_swap(given).astype(F32))
            return sums[0] + pair_swap(sums[1].astype(BF16)).astype(F32)

        cot_local = cotangent.astype(F32)
        output = hidden.astype(F32) + fold(outs) + (out_bias.astype(F32) + down_bias.astype(F32))
        input_grad = cot_local + fold(slopes)

        qkv_sum = (
            jnp.sum(grads_mixed[0].astype(F32), axis=0) + jnp.sum(grads_mixed[1].astype(F32), axis=0)
        )
        qkv_sum = in_place([piece_of(qkv_sum, q, 0, True) for q in range(quarters)], 0)
        up_sum = (feeds[0][2] + feeds[1][2])[0]
        up_sum = in_place([piece_of(up_sum, q, 0, True) for q in range(quarters)], 0)

        def widen(value):
            zeros = jnp.zeros_like(value)
            flip = side == 0
            return jnp.concatenate([jnp.where(flip, value, zeros), jnp.where(flip, zeros, value)], axis=-1)

        kept = lax.dynamic_slice_in_dim(norm_sums, col * half_width, half_width, 1)
        given = lax.dynamic_slice_in_dim(norm_sums, (1 - col) * half_width, half_width, 1)
        norm_sums = kept + core_swap(given)
        small = jnp.concatenate(
            [widen(qkv_sum).reshape(-1), widen(up_sum), jnp.sum(cot_local, axis=0), norm_sums.reshape(-1)]
        )
        small = lax.psum(small, ("dp", "row"))
        sizes = [6 * wide, 2 * units, half_width, half_width, half_width, half_width, half_width]
        parts = []
        start = 0
        for size in sizes:
            parts.append(lax.slice_in_dim(small, start, start + size))
            start += size
        qkv_sum, up_sum, cot_sum, gain_one_sum, shift_one_sum, gain_two_sum, shift_two_sum = parts
        qkv_sum = jnp.swapaxes(qkv_sum.reshape(2 * quarters, 3, heads // quarters, HEAD_DIM), 1, 2).reshape(-1)
        return (
            output,
            input_grad,
            gain_one_sum,
            shift_one_sum,
            qkv_grad,
            qkv_sum,
            out_grad,
            cot_sum,
            gain_two_sum,
            shift_two_sum,
            up_grad,
            up_sum,
            down_grad,
            cot_sum,
        )

    return local


def solution(mesh):
    placed = (
        P(("dp", "row"), "col"),
        P(("dp", "row"), None),
        P("col"),
        P("col"),
        P("row", "col"),
        P("col"),
        P("col", "row"),
        P("col"),
        P("col"),
        P("col"),
        P("row", "col"),
        P("col"),
        P("col", "row"),
        P("col"),
        P(("dp", "row"), "col"),
    )
    groups = mesh.shape["dp"]
    make = make_fast if groups == 4 else make_general
    return jax.shard_map(
        make(mesh.shape["dp"], mesh.shape["row"], mesh.shape["col"]),
        mesh=mesh,
        in_specs=placed,
        out_specs=(
            P(("dp", "row"), "col"),
            P(("dp", "row"), "col"),
            P("col"),
            P("col"),
            P("row", "col"),
            P("col"),
            P("col", "row"),
            P("col"),
            P("col"),
            P("col"),
            P("row", "col"),
            P("col"),
            P("col", "row"),
            P("col"),
        ),
        check_vma=False,
    )
```

```python
import functools

import jax
import jax.numpy as jnp
from jax import lax
from jax.experimental import pallas as pl
from jax.experimental.pallas import tpu as pltpu
from jax.sharding import PartitionSpec as P

HEAD_DIM = 64
ROT = 16
EPS = 1e-05
MAX_DOC = 512
LANES = 128
BF16 = jnp.bfloat16
F32 = jnp.float32

NT = (((1,), (1,)), ((), ()))
TN = (((0,), (0,)), ((), ()))
NN = (((1,), (0,)), ((), ()))


def dot(a, b, dims=NN):
    return lax.dot_general(a, b, dims, preferred_element_type=F32)


def doc_positions(segments):
    length = segments.shape[-1]
    places = jnp.arange(length, dtype=jnp.int32)
    changed = jnp.concatenate(
        [jnp.ones(segments.shape[:-1] + (1,), dtype=bool), segments[..., 1:] != segments[..., :-1]],
        axis=-1,
    )
    starts = lax.cummax(jnp.where(changed, places, jnp.zeros_like(places)), axis=segments.ndim - 1)
    return places - starts


def rotary_tables(positions):
    lane = jnp.arange(LANES) % HEAD_DIM
    frequency = 10000.0 ** (-2.0 * (lane % (ROT // 2)).astype(F32) / ROT)
    turning = lane < ROT
    angles = positions.astype(F32)[:, None] * jnp.where(turning, frequency, 0.0)[None, :]
    sign = jnp.where(turning, jnp.where(lane < ROT // 2, -1.0, 1.0), 0.0)
    return jnp.cos(angles), jnp.sin(angles) * sign[None, :]


def turn(values, cos_rows, sine_rows, low_lanes):
    half = ROT // 2
    up = pltpu.roll(values, values.shape[1] - half, 1)
    down = pltpu.roll(values, half, 1)
    return values * cos_rows + jnp.where(low_lanes, up, down) * sine_rows


def attention_kernel(
    q_ref, k_ref, v_ref, gc_ref, seg_row_ref, seg_col_ref, cos_ref, sin_ref, ctx_ref, gm_ref, dk_acc, dv_acc, *, block
):
    pair = pl.program_id(0)
    pairs = pl.num_programs(0)
    length = q_ref.shape[0]
    lane = lax.broadcasted_iota(jnp.int32, (1, LANES), 1)
    low_lanes = lane % HEAD_DIM < ROT // 2
    first = lane < HEAD_DIM
    zero = jnp.zeros((), BF16)

    def split(values):
        return [jnp.where(first, values, zero), jnp.where(first, zero, values)]

    dk_acc[...] = jnp.zeros_like(dk_acc)
    dv_acc[...] = jnp.zeros_like(dv_acc)
    for begin in range(0, length, block):
        low = max(0, begin - (MAX_DOC - 1)) // LANES * LANES
        rows = pl.ds(begin, block)
        keys = pl.ds(low, begin + block - low)
        width = begin + block - low
        q_parts = split(q_ref[rows, :] * jnp.asarray(HEAD_DIM**-0.5, BF16))
        g_parts = split(gc_ref[rows, :])
        k_block = k_ref[keys, :]
        v_block = v_ref[keys, :]
        places = begin + lax.broadcasted_iota(jnp.int32, (block, width), 0)
        key_places = low + lax.broadcasted_iota(jnp.int32, (block, width), 1)
        allowed = (seg_col_ref[rows, :] == seg_row_ref[:, keys]) & (places >= key_places)
        probs = []
        grads = []
        for part in range(2):
            scores = dot(q_parts[part], k_block, NT)
            scores = jnp.where(allowed, scores, -1e30)
            top = jnp.max(scores, axis=1, keepdims=True)
            powers = jnp.exp(scores - top)
            total = jnp.sum(powers, axis=1, keepdims=True)
            chances = powers * (1.0 / total)
            slopes = dot(g_parts[part], v_block, NT)
            inner = jnp.sum(slopes * chances, axis=1, keepdims=True)
            probs.append(chances.astype(BF16))
            grads.append((chances * (slopes - inner)).astype(BF16))
        context = jnp.where(first, dot(probs[0], v_block), dot(probs[1], v_block))
        ctx_ref[rows, :] = context.astype(BF16)
        dq = jnp.where(first, dot(grads[0], k_block), dot(grads[1], k_block)) * HEAD_DIM**-0.5
        dq = turn(dq, cos_ref[rows, :], -sin_ref[rows, :], low_lanes)
        gm_ref[rows, pl.ds(pl.multiple_of(pair * LANES, LANES), LANES)] = dq.astype(BF16)
        dk_acc[keys, :] += dot(grads[0], q_parts[0], TN) + dot(grads[1], q_parts[1], TN)
        dv_acc[keys, :] += dot(probs[0], g_parts[0], TN) + dot(probs[1], g_parts[1], TN)
    dk = turn(dk_acc[...], cos_ref[...], -sin_ref[...], low_lanes)
    gm_ref[:, pl.ds(pl.multiple_of((pairs + pair) * LANES, LANES), LANES)] = dk.astype(BF16)
    gm_ref[:, pl.ds(pl.multiple_of((2 * pairs + pair) * LANES, LANES), LANES)] = dv_acc[...].astype(BF16)


def attention(qkv, grad_context, seg_row, cos_rows, sine_rows):
    length, wide = qkv.shape
    pairs = wide // (3 * LANES)
    block = min(256, length)
    column = lambda shift: pl.BlockSpec((length, LANES), lambda p: (0, shift + p))
    whole = lambda *shape: pl.BlockSpec(shape, lambda p: (0, 0))
    flops = pairs * 2 * 6 * 2 * length * length * LANES // 2
    return pl.pallas_call(
        functools.partial(attention_kernel, block=block),
        grid=(pairs,),
        in_specs=[
            column(0),
            column(pairs),
            column(2 * pairs),
            column(0),
            whole(1, length),
            whole(length, 1),
            whole(length, LANES),
            whole(length, LANES),
        ],
        out_specs=[column(0), whole(length, wide)],
        out_shape=[
            jax.ShapeDtypeStruct((length, pairs * LANES), BF16),
            jax.ShapeDtypeStruct((length, wide), BF16),
        ],
        scratch_shapes=[pltpu.VMEM((length, LANES), F32), pltpu.VMEM((length, LANES), F32)],
        compiler_params=pltpu.CompilerParams(vmem_limit_bytes=48 << 20),
        cost_estimate=pl.CostEstimate(
            flops=flops, bytes_accessed=6 * length * wide, transcendentals=pairs * length * length
        ),
        name="attention",
    )(qkv, qkv, qkv, grad_context, seg_row, seg_row.reshape(length, 1), cos_rows, sine_rows)


def feed_kernel(a_ref, g_ref, up_ref, bias_ref, down_ref, act_ref, gup_ref, sum_ref, *, chunk):
    units = up_ref.shape[1]

    @pl.when(pl.program_id(0) == 0)
    def _():
        sum_ref[...] = jnp.zeros_like(sum_ref)

    for begin in range(0, units, chunk):
        cols = pl.ds(begin, chunk)
        up = dot(a_ref[...], up_ref[:, cols]) + bias_ref[:, cols]
        pull = dot(g_ref[...], down_ref[cols, :], NT)
        gate = 0.5 * (1.0 + lax.erf(up * 0.5**0.5))
        bell = jnp.exp(-0.5 * up * up) * 0.3989422804014327
        act_ref[:, cols] = (up * gate).astype(BF16)
        grad = (pull * (gate + up * bell)).astype(BF16)
        gup_ref[:, cols] = grad
        sum_ref[:, cols] += jnp.sum(grad.astype(F32), axis=0, keepdims=True)


def feed(normed, cot, up_weight, up_bias, down_weight):
    tokens, width = normed.shape
    units = up_weight.shape[1]
    block = min(256, tokens)
    rows = lambda size: pl.BlockSpec((block, size), lambda i: (i, 0))
    whole = lambda *shape: pl.BlockSpec(shape, lambda i: (0, 0))
    return pl.pallas_call(
        functools.partial(feed_kernel, chunk=min(256, units)),
        grid=(tokens // block,),
        in_specs=[rows(width), rows(width), whole(width, units), whole(1, units), whole(units, width)],
        out_specs=[rows(units), rows(units), whole(1, units)],
        out_shape=[
            jax.ShapeDtypeStruct((tokens, units), BF16),
            jax.ShapeDtypeStruct((tokens, units), BF16),
            jax.ShapeDtypeStruct((1, units), F32),
        ],
        compiler_params=pltpu.CompilerParams(vmem_limit_bytes=48 << 20),
        cost_estimate=pl.CostEstimate(
            flops=4 * tokens * width * units,
            bytes_accessed=4 * tokens * width + 4 * width * units + 4 * tokens * units,
            transcendentals=2 * tokens * units,
        ),
        name="feed",
    )(normed, cot, up_weight, up_bias, down_weight)


MESH = pl.DeviceIdType.MESH


class Net:
    def __init__(self, send_sems, recv_sems):
        self.send_sems, self.recv_sems = send_sems, recv_sems
        self.slots = {}
        self.pending = []

    def slot(self, key):
        return self.slots.setdefault(key, len(self.slots))

    def make(self, key, source, target, device):
        i = self.slot(key)
        return pltpu.make_async_remote_copy(
            src_ref=source,
            dst_ref=target,
            send_sem=self.send_sems.at[i],
            recv_sem=self.recv_sems.at[i],
            device_id=device,
            device_id_type=MESH,
        )

    def send(self, key, source, target, device):
        copy = self.make(key, source, target, device)
        copy.start()
        self.pending.append(copy)

    def wait(self, key, landed, device):
        self.make(key, landed, landed, device).wait_recv()

    def drain(self):
        for copy in self.pending:
            copy.wait_send()
        self.pending = []


def spread(columns, width):
    return jnp.concatenate([columns] * (width // LANES), axis=1)


def attend_pair(mix, base, gc, gc_base, ctx, seg_row, seg_col, cos_tab, sin_tab, dk_acc, dv_acc, block):
    length = mix.shape[0]
    lane = lax.broadcasted_iota(jnp.int32, (1, LANES), 1)
    low_lanes = lane % HEAD_DIM < ROT // 2
    first = lane < HEAD_DIM
    zero = jnp.zeros((), BF16)
    cols = [pl.ds(base + i * LANES, LANES) for i in range(3)]
    head_cols = pl.ds(gc_base, LANES)

    def split(values):
        return [jnp.where(first, values, zero), jnp.where(first, zero, values)]

    dk_acc[...] = jnp.zeros_like(dk_acc)
    dv_acc[...] = jnp.zeros_like(dv_acc)
    for begin in range(0, length, block):
        low = max(0, begin - (MAX_DOC - 1)) // LANES * LANES
        width = begin + block - low
        rows = pl.ds(begin, block)
        keys = pl.ds(low, width)
        q_parts = split(mix[rows, cols[0]] * jnp.asarray(HEAD_DIM**-0.5, BF16))
        g_parts = split(gc[rows, head_cols])
        k_block = mix[keys, cols[1]]
        v_block = mix[keys, cols[2]]
        places = begin + lax.broadcasted_iota(jnp.int32, (block, width), 0)
        key_places = low + lax.broadcasted_iota(jnp.int32, (block, width), 1)
        allowed = (spread(seg_col[rows, :], width) == seg_row[0:1, keys]) & (places >= key_places)
        probs = []
        grads = []
        for part in range(2):
            scores = dot(q_parts[part], k_block, NT)
            scores = jnp.where(allowed, scores, -1e30)
            top = jnp.max(scores, axis=1, keepdims=True)
            powers = jnp.exp(scores - top)
            total = jnp.sum(powers, axis=1, keepdims=True)
            chances = powers * (1.0 / total)
            slopes = dot(g_parts[part], v_block, NT)
            inner = jnp.sum(slopes * chances, axis=1, keepdims=True)
            probs.append(chances.astype(BF16))
            grads.append((chances * (slopes - inner)).astype(BF16))
        ctx[rows, head_cols] = jnp.where(first, dot(probs[0], v_block), dot(probs[1], v_block)).astype(BF16)
        dq = jnp.where(first, dot(grads[0], k_block), dot(grads[1], k_block)) * HEAD_DIM**-0.5
        mix[rows, cols[0]] = turn(dq, cos_tab[rows, :], -sin_tab[rows, :], low_lanes).astype(BF16)
        dk_acc[keys, :] += dot(grads[0], q_parts[0], TN) + dot(grads[1], q_parts[1], TN)
        dv_acc[keys, :] += dot(probs[0], g_parts[0], TN) + dot(probs[1], g_parts[1], TN)
    mix[:, cols[1]] = turn(dk_acc[...], cos_tab[...], -sin_tab[...], low_lanes).astype(BF16)
    mix[:, cols[2]] = dv_acc[...].astype(BF16)


def block_kernel(
    hidden, cot, wq_in, wo_in, wu_in, wd_in, rows_in, params_in, bq_in, bu_in, freq_in,
    rq_out, ro_out, ru_out, rd_out, keep_out, near_out, far_out, small_out,
    X, G, A, WQ, WO, WU, WD, MIX, GC, CTX, ACT, GUP, rows_far, params, seg_col, cos_tab, sin_tab, dk_acc, dv_acc,
    SQ, SO, SU, SD, YQ, YO, YU, YD, ZQ, ZO, ZU, ZD, HQ, HO, HU, HD, RQ, RO, RU, RD, LAND, SMALL, SMALL_Z, SMALL_P,
    send_sems, recv_sems, local_sems, *, rows_n,
):
    R = rows_n
    dp, row, col = lax.axis_index("dp"), lax.axis_index("row"), lax.axis_index("col")
    side, quarter = lax.rem(dp, 2), lax.div(dp, 2)
    length, half = hidden.shape
    shard = wq_in.shape[0]
    core = (dp, row, 1 - col)
    xdev = (dp + 1 - 2 * side, row, col)
    ydev = (side + 2 * (1 - quarter), row, col)

    def zdev(t):
        return (dp, lax.rem(row + t + R, R), col)

    barrier = pltpu.get_barrier_semaphore()
    peers = [core, xdev, ydev] + [zdev(t) for t in range(1, R)]
    for peer in peers:
        pl.semaphore_signal(barrier, inc=1, device_id=peer, device_id_type=MESH)
    pl.semaphore_wait(barrier, len(peers))

    net = Net(send_sems, recv_sems)
    own_cols = pl.ds(pl.multiple_of(col * half, half), half)
    far_cols = pl.ds(pl.multiple_of((1 - col) * half, half), half)
    local = []

    def move(source, target):
        copy = pltpu.make_async_copy(source, target, local_sems.at[len(local)])
        copy.start()
        local.append(copy)
        return copy

    net.send("core h", hidden, X.at[0, :, own_cols], core)
    net.send("core p", params_in, params.at[:, own_cols], core)
    net.send("x rows", rows_in, rows_far, xdev)
    here_h = move(hidden, X.at[0, :, own_cols])
    here_p = move(params_in, params.at[:, own_cols])

    qc = WQ.shape[1] // 2
    oc = WO.shape[0] // 2
    uc = WU.shape[1] // 2
    unit_at = pl.multiple_of((side * 2 + quarter) * uc, uc)
    unit_other = pl.multiple_of((side * 2 + 1 - quarter) * uc, uc)
    head_at = pl.multiple_of((side * 2 + quarter) * oc, oc)
    head_other = pl.multiple_of((side * 2 + 1 - quarter) * oc, oc)

    def block(t):
        return pl.ds(pl.multiple_of(lax.rem(row + t + R, R) * shard, shard), shard)

    weights = {
        "q": (wq_in.at[:, pl.ds(0, qc)], wq_in.at[:, pl.ds(qc, qc)], lambda t, h: WQ.at[block(t), pl.ds(h * qc, qc)]),
        "o": (wo_in.at[pl.ds(head_at, oc), :], wo_in.at[pl.ds(head_other, oc), :], lambda t, h: WO.at[pl.ds(h * oc, oc), block(t)]),
        "u": (wu_in.at[:, pl.ds(unit_at, uc)], wu_in.at[:, pl.ds(unit_other, uc)], lambda t, h: WU.at[block(t), pl.ds(h * uc, uc)]),
        "d": (wd_in.at[pl.ds(unit_at, uc), :], wd_in.at[pl.ds(unit_other, uc), :], lambda t, h: WD.at[pl.ds(h * uc, uc), block(t)]),
    }
    here_w = {}
    for name, (mine, other, place) in weights.items():
        net.send((name, 1), mine, place(0, 0), zdev(-1))
        if R > 2:
            net.send((name, R - 1), mine, place(0, 0), zdev(1))
        if name == "q":
            here_w[name] = [move(mine, place(0, 0)), move(other, place(0, 1))]
    chunks = 2
    piece = length // chunks
    for c in range(chunks):
        span = pl.ds(c * piece, piece)
        net.send(("x h", c), hidden.at[span, :], X.at[1, span, own_cols], xdev)
    net.send("core g", cot, G.at[0, :, own_cols], core)
    here_g = move(cot, G.at[0, :, own_cols])
    for c in range(chunks):
        span = pl.ds(c * piece, piece)
        net.send(("x g", c), cot.at[span, :], G.at[1, span, own_cols], xdev)
    for name in "oud":
        mine, other, place = weights[name]
        here_w[name] = [move(mine, place(0, 0)), move(other, place(0, 1))]

    def along(name, t):
        place = weights[name][2]
        net.wait((name, t), place(t, 0), zdev(t))
        if t < R // 2:
            net.send((name, t + 1), place(t, 0), place(t, 0), zdev(-1))
        elif R // 2 + 1 < t:
            net.send((name, t - 1), place(t, 0), place(t, 0), zdev(1))
        net.send((name, t, "y"), place(t, 0), place(t, 1), ydev)

    order = [1, R - 1] + [t for t in range(2, R - 1)] if R > 2 else [1]

    def arrive(name):
        place = weights[name][2]
        for copy in here_w[name]:
            copy.wait()
        for t in range(1, R):
            net.wait((name, t, "y"), place(t, 1), ydev)

    def hand_over(name, buffer, c):
        span = pl.ds(c * piece, piece)
        net.wait(("x " + name, c), buffer.at[1, span, own_cols], xdev)
        net.send(("core far " + name, c), buffer.at[1, span, own_cols], buffer.at[1, span, own_cols], core)

    tile = 256
    gain_one, shift_one = 0, 1

    def norm(s, at, gain, shift):
        values = X[s, at, :].astype(F32)
        centred = values - jnp.mean(values, axis=-1, keepdims=True)
        inv = lax.rsqrt(jnp.mean(centred * centred, axis=-1, keepdims=True) + EPS)
        A[s, at, :] = (centred * inv * params[gain : gain + 1, :] + params[shift : shift + 1, :]).astype(BF16)

    def each_tile(body):
        @pl.loop(0, length // tile)
        def _(i):
            body(pl.ds(pl.multiple_of(i * tile, tile), tile))

    lane = lax.broadcasted_iota(jnp.int32, (1, LANES), 1)
    low_lanes = lane % HEAD_DIM < ROT // 2

    def tables(rows):
        columns = jnp.transpose(jnp.broadcast_to(rows[0:1, :], (LANES, length)))
        seg_col[...] = columns
        columns = jnp.transpose(jnp.broadcast_to(rows[1:2, :], (LANES, length)))
        angles = columns * freq_in[0:1, :]
        cos_tab[...] = jnp.cos(angles)
        sin_tab[...] = jnp.sin(angles) * freq_in[1:2, :]

    def project(s):
        def body(at):
            mixed = dot(A[s, at, :], WQ[...]) + bq_in[...]
            for i in range(mixed.shape[1] // LANES):
                part = mixed[:, i * LANES : (i + 1) * LANES]
                if i % 3 < 2:
                    part = turn(part, cos_tab[at, :], sin_tab[at, :], low_lanes)
                MIX[s, at, pl.ds(i * LANES, LANES)] = part.astype(BF16)

        each_tile(body)

    def pull_context(s):
        def body(at):
            GC[at, :] = dot(G[s, at, :], WO[...], NT).astype(BF16)

        each_tile(body)

    def attend(s, rows, pair):
        attend_pair(
            MIX.at[s], pair * 3 * LANES, GC, pair * LANES, CTX.at[s], rows, seg_col, cos_tab, sin_tab, dk_acc, dv_acc, tile
        )

    pairs = CTX.shape[2] // LANES
    tables(rows_in)
    here_h.wait()
    here_p.wait()
    net.wait("core h", X.at[0, :, far_cols], core)
    net.wait("core p", params.at[:, far_cols], core)
    each_tile(lambda at: norm(0, at, gain_one, shift_one))
    for t in order:
        along("q", t)
    for t in order:
        along("o", t)
    arrive("q")
    project(0)
    here_g.wait()
    net.wait("core g", G.at[0, :, far_cols], core)
    hand_over("h", X, 0)
    arrive("o")
    pull_context(0)
    along("u", 1)
    along("u", R - 1)
    for pair in range(pairs):
        attend(0, rows_in, pair)
        hand_over("h" if pair == 0 else "g", X if pair == 0 else G, 1 if pair == 0 else 0)
        along("d", 1 if pair == 0 else R - 1)
        for t in order[2:]:
            along("u" if pair == 0 else "d", t)
    for c in range(chunks):
        span = pl.ds(c * piece, piece)
        net.wait(("core far h", c), X.at[1, span, far_cols], core)
    net.wait("x rows", rows_far, xdev)
    tables(rows_far)
    each_tile(lambda at: norm(1, at, gain_one, shift_one))
    project(1)
    hand_over("g", G, 1)
    for c in range(chunks):
        span = pl.ds(c * piece, piece)
        net.wait(("core far g", c), G.at[1, span, far_cols], core)
    pull_context(1)
    for pair in range(pairs):
        attend(1, rows_far, pair)
    everything = pl.ds(0, length)
    grads = {
        "q": (SQ, YQ, ZQ, HQ, RQ, rq_out, lambda t: (block(t), slice(None)), lambda q: (slice(None), pl.ds(q * qc, qc))),
        "o": (SO, YO, ZO, HO, RO, ro_out, lambda t: (slice(None), block(t)), lambda q: (pl.ds(q * oc, oc), slice(None))),
        "u": (SU, YU, ZU, HU, RU, ru_out, lambda t: (block(t), slice(None)), lambda q: (slice(None), pl.ds(q * uc, uc))),
        "d": (SD, YD, ZD, HD, RD, rd_out, lambda t: (slice(None), block(t)), lambda q: (pl.ds(q * uc, uc), slice(None))),
    }

    def multiply(name, h, t):
        if name == "q":
            pairs_of = [(A[s, :, block(t)], MIX[s, :, pl.ds(h * qc, qc)]) for s in range(2)]
        elif name == "u":
            pairs_of = [(A[s, :, block(t)], GUP[s, :, pl.ds(h * uc, uc)]) for s in range(2)]
        elif name == "o":
            pairs_of = [(CTX[s, :, pl.ds(h * oc, oc)], G[s, :, block(t)]) for s in range(2)]
        else:
            pairs_of = [(ACT[s, :, pl.ds(h * uc, uc)], G[s, :, block(t)]) for s in range(2)]
        return (dot(*pairs_of[0], TN) + dot(*pairs_of[1], TN)).astype(BF16)

    turns = list(range(1, R)) + [0]

    def other_part(name):
        source, landed, _, _, _, _, spot, _ = grads[name]
        for t in turns:
            source[spot(t)] = multiply(name, 1, t)
            net.send(("gy", name, t), source.at[spot(t)], landed.at[spot(t)], ydev)

    def own_part(name):
        kept, spot = grads[name][2], grads[name][6]

        @pl.loop(0, R)
        def _(t):
            kept[spot(t)] = multiply(name, 0, t)

    def across(name):
        _, landed, kept, hops, _, _, spot, _ = grads[name]
        for t in turns:
            net.wait(("gy", name, t), landed.at[spot(t)], ydev)
            kept[spot(t)] = (kept[spot(t)].astype(F32) + landed[spot(t)].astype(F32)).astype(BF16)
            if t:
                net.send(("gz", name, t), kept.at[spot(t)], hops.at[t - 1], zdev(t))

    def finish(name):
        _, _, kept, hops, result, _, spot, seat = grads[name]
        total = kept[spot(0)].astype(F32)
        for t in range(1, R):
            net.wait(("gz", name, t), hops.at[t - 1], zdev(-t))
            total = total + hops[t - 1].astype(F32)
        spot_here = seat(side * 2 + quarter)
        result[spot_here] = total.astype(BF16)
        net.send(("ry", name), result.at[spot_here], result.at[spot_here], ydev)
        net.send(("rx", name), result.at[spot_here], result.at[spot_here], xdev)

    def spread_out(name):
        result, seat = grads[name][4], grads[name][7]
        spot_y = seat(side * 2 + 1 - quarter)
        net.wait(("ry", name), result.at[spot_y], ydev)
        net.send(("rxy", name), result.at[spot_y], result.at[spot_y], xdev)

    def collect(name):
        result, seat = grads[name][4], grads[name][7]
        net.wait(("rx", name), result.at[seat((1 - side) * 2 + quarter)], xdev)
        net.wait(("rxy", name), result.at[seat((1 - side) * 2 + 1 - quarter)], xdev)
        return move(result, grads[name][5])

    SMALL[...] = jnp.zeros_like(SMALL)
    for name in "oq":
        other_part(name)
    for name in "oq":
        own_part(name)
    for h in range(2):
        sums = [jnp.sum(MIX[s, :, pl.ds(h * qc, qc)].astype(F32), axis=0, keepdims=True) for s in range(2)]
        seat = quarter if h == 0 else 1 - quarter
        SMALL[0:1, pl.ds(pl.multiple_of(seat * qc, LANES), qc)] = sums[0] + sums[1]

    arrive("u")
    arrive("d")
    for s in range(2):
        each_tile(lambda at: norm(s, at, 2, 3))

    def feed_part(s, h):
        seat = quarter if h == 0 else 1 - quarter

        def body(at):
            for begin in range(0, uc, tile):
                cols = pl.ds(h * uc + begin, tile)
                up = dot(A[s, at, :], WU[:, cols]) + bu_in[:, cols]
                pull = dot(G[s, at, :], WD[cols, :], NT)
                gate = 0.5 * (1.0 + lax.erf(up * 0.5**0.5))
                bell = jnp.exp(-0.5 * up * up) * 0.3989422804014327
                ACT[s, at, cols] = (up * gate).astype(BF16)
                grad = (pull * (gate + up * bell)).astype(BF16)
                GUP[s, at, cols] = grad
                SMALL[1:2, pl.ds(pl.multiple_of(seat * uc + begin, tile), tile)] += jnp.sum(
                    grad.astype(F32), axis=0, keepdims=True
                )

        each_tile(body)

    for s in range(2):
        feed_part(s, 1)
    for name in "du":
        other_part(name)
    for name in "oq":
        across(name)
    for s in range(2):
        feed_part(s, 0)
    for name in "du":
        own_part(name)

    def leave(s, c):
        @pl.loop(0, piece // tile)
        def _(i):
            at = pl.ds(pl.multiple_of(c * piece + i * tile, tile), tile)
            result = dot(CTX[s, at, :], WO[...]) + dot(ACT[s, at, :], WD[...])
            ACT[s, at, :] = result.astype(BF16)
            grad_one = dot(MIX[s, at, :], WQ[...], NT)
            grad_two = dot(GUP[s, at, :], WU[...], NT)
            values = X[s, at, :].astype(F32)
            centred = values - jnp.mean(values, axis=-1, keepdims=True)
            inv = lax.rsqrt(jnp.mean(centred * centred, axis=-1, keepdims=True) + EPS)
            unit = centred * inv
            for i_row, value in enumerate([grad_one * unit, grad_one, grad_two * unit, grad_two]):
                SMALL[2 + i_row : 3 + i_row, :] += jnp.sum(value, axis=0, keepdims=True)
            scaled = grad_one * params[0:1, :] + grad_two * params[2:3, :]
            mean_scaled = jnp.mean(scaled, axis=1, keepdims=True)
            mean_unit = jnp.mean(scaled * unit, axis=1, keepdims=True)
            GUP[s, at, :] = (inv * (scaled - mean_scaled - unit * mean_unit)).astype(BF16)
            if s == 0:
                SMALL[6:7, own_cols] += jnp.sum(G[0, at, own_cols].astype(F32), axis=0, keepdims=True)

        span = pl.ds(c * piece, piece)
        for i, buffer in enumerate([ACT, GUP]):
            if s == 1:
                net.send(("out", i, c), buffer.at[1, span, far_cols], LAND.at[i, span, :], core)
            else:
                net.send(("own out", i, c), buffer.at[0, span, far_cols], near_out.at[i, span, :], core)

    def leave_far(c):
        span = pl.ds(c * piece, piece)
        for i, buffer in enumerate([ACT, GUP]):
            net.wait(("out", i, c), LAND.at[i, span, :], core)
            LAND[i, span, :] = (LAND[i, span, :].astype(F32) + buffer[1, span, own_cols].astype(F32)).astype(BF16)
            net.send(("far out", i, c), LAND.at[i, span, :], far_out.at[i, span, :], xdev)

    leave(1, 0)
    leave(1, 1)
    leave_far(0)
    for name in "d":
        across(name)
    leave_far(1)
    for name in "oq":
        finish(name)
    leave(0, 0)
    for name in "oq":
        spread_out(name)
    leave(0, 1)
    kept_copies = [move(ACT.at[0, :, own_cols], keep_out.at[0]), move(GUP.at[0, :, own_cols], keep_out.at[1])]

    for t in range(1, R):
        net.send(("sz", t), SMALL, SMALL_Z.at[row], zdev(t))
    across("u")
    finish("d")
    SMALL_Z[row] = SMALL[...]
    for t in range(1, R):
        net.wait(("sz", t), SMALL_Z.at[lax.rem(row - t + R, R)], zdev(-t))
    total = SMALL_Z[0]
    for r in range(1, R):
        total = total + SMALL_Z[r]
    SMALL_P[0] = total
    net.send("sy", SMALL_P.at[0], SMALL_P.at[1], ydev)
    spread_out("d")
    finish("u")
    net.wait("sy", SMALL_P.at[1], ydev)
    SMALL_P[2] = SMALL_P[0] + SMALL_P[1]
    net.send("sx", SMALL_P.at[2], SMALL_P.at[3], xdev)
    done = [collect(name) for name in "oq"]
    net.wait("sx", SMALL_P.at[3], xdev)
    SMALL_P[4] = SMALL_P[2] + SMALL_P[3]
    net.send("sc", SMALL_P.at[4], SMALL_P.at[5], core)
    spread_out("u")
    net.wait("sc", SMALL_P.at[5], core)
    SMALL_P[5] = SMALL_P[4] + SMALL_P[5]
    done += [
        move(SMALL_P.at[2], small_out.at[side]),
        move(SMALL_P.at[3], small_out.at[1 - side]),
        move(SMALL_P.at[4], small_out.at[2]),
        move(SMALL_P.at[5], small_out.at[3]),
    ]
    for c in range(chunks):
        span = pl.ds(c * piece, piece)
        for i in range(2):
            net.wait(("own out", i, c), near_out.at[i, span, :], core)
            net.wait(("far out", i, c), far_out.at[i, span, :], xdev)
    done += [collect(name) for name in "du"]
    for copy in kept_copies + done:
        copy.wait()
    net.drain()


def whole_block(hidden, cot, wq, wo, wu, wd, rows, params, bq, bu, freq, rows_n):
    length, half = hidden.shape
    width = 2 * half
    shard = wq.shape[0]
    wide3 = wq.shape[1]
    wide = wide3 // 3
    units = wu.shape[1] // 2
    qc, oc, uc = wide3 // 2, wide // 2, units // 2
    out_shape = [
        jax.ShapeDtypeStruct(shape, kind)
        for shape, kind in [
            ((shard, 4 * qc), BF16), ((4 * oc, shard), BF16), ((shard, 4 * uc), BF16), ((4 * uc, shard), BF16),
            ((2, length, half), BF16), ((2, length, half), BF16), ((2, length, half), BF16), ((4, 8, width), F32),
        ]
    ]
    both = lambda n, kind=BF16: pltpu.VMEM((2, length, n), kind)
    plain = lambda *shape: pltpu.VMEM(shape, BF16)
    floats = lambda *shape: pltpu.VMEM(shape, F32)
    quarter_grads = [plain(width, qc), plain(oc, width), plain(width, uc), plain(uc, width)]
    scratch = [
        both(width), both(width), both(width),
        plain(width, wide3), plain(wide, width), plain(width, units), plain(units, width),
        both(wide3), plain(length, wide), both(wide), both(units), both(units),
        floats(*rows.shape), floats(params.shape[0], width),
        *[floats(length, LANES)] * 5,
        *quarter_grads * 3,
        plain(rows_n - 1, shard, qc), plain(rows_n - 1, oc, shard), plain(rows_n - 1, shard, uc), plain(rows_n - 1, uc, shard),
        plain(shard, 4 * qc), plain(4 * oc, shard), plain(shard, 4 * uc), plain(4 * uc, shard),
        both(half), floats(8, width), floats(rows_n, 8, width), floats(6, 8, width),
    ]
    any_spec = pl.BlockSpec(memory_space=pl.ANY)
    vmem_spec = pl.BlockSpec(memory_space=pltpu.VMEM)
    return pl.pallas_call(
        functools.partial(block_kernel, rows_n=rows_n),
        out_shape=out_shape,
        in_specs=[any_spec] * 6 + [vmem_spec] * 5,
        out_specs=[any_spec] * len(out_shape),
        scratch_shapes=scratch + [
            pltpu.SemaphoreType.DMA((128,)), pltpu.SemaphoreType.DMA((128,)), pltpu.SemaphoreType.DMA((32,)),
        ],
        compiler_params=pltpu.CompilerParams(collective_id=0, has_side_effects=True, vmem_limit_bytes=62 << 20),
        name="block",
    )(hidden, cot, wq, wo, wu, wd, rows, params, bq, bu, freq)


def normalize(values):
    centred = values - jnp.mean(values, axis=-1, keepdims=True)
    variance = jnp.mean(centred * centred, axis=-1, keepdims=True)
    inv_std = lax.rsqrt(variance + EPS)
    return centred * inv_std, inv_std


def make_general(groups, rows, cols):
    quarters = groups // 2

    def pair_swap(value):
        return lax.ppermute(value, "dp", [(d, d ^ 1) for d in range(groups)])

    def quarter_shift(value, shift):
        moves = [(2 * a + b, 2 * ((a + shift) % quarters) + b) for a in range(quarters) for b in range(2)]
        return lax.ppermute(value, "dp", moves)

    def row_shift(value, shift):
        return lax.ppermute(value, "row", [(r, (r + shift) % rows) for r in range(rows)])

    def core_swap(value):
        return lax.ppermute(value, "col", [(0, 1), (1, 0)])

    def local(
        hidden,
        segments,
        ln1_gain,
        ln1_bias,
        qkv_weight,
        qkv_bias,
        out_weight,
        out_bias,
        ln2_gain,
        ln2_bias,
        up_weight,
        up_bias,
        down_weight,
        down_bias,
        cotangent,
    ):
        assert segments.shape[0] == 1 and cols == 2
        length = segments.shape[1]
        half_width = hidden.shape[1]
        width = 2 * half_width
        shard = qkv_weight.shape[0]
        heads = qkv_weight.shape[1] // (3 * HEAD_DIM) // 2
        wide = heads * HEAD_DIM
        units = up_weight.shape[1] // 2
        whole_heads = heads % quarters == 0
        dp = lax.axis_index("dp")
        row = lax.axis_index("row")
        col = lax.axis_index("col")
        side = lax.rem(dp, 2)
        quarter = dp // 2

        def both(mine, other):
            flip = col == 0
            return jnp.concatenate([jnp.where(flip, mine, other), jnp.where(flip, other, mine)], axis=-1)

        def half_of(value, axis):
            size = value.shape[axis] // 2
            return lax.dynamic_slice_in_dim(value, side * size, size, axis)

        def piece_of(value, shift, axis, placed=False):
            size = value.shape[axis] // quarters
            if placed:
                return lax.slice_in_dim(value, shift * size, (shift + 1) * size, axis=axis)
            return lax.dynamic_slice_in_dim(value, lax.rem(quarter - shift + quarters, quarters) * size, size, axis)

        def in_place(pieces, axis):
            if quarters == 1:
                return pieces[0]
            if quarters == 2:
                flip = quarter == 0
                first = jnp.where(flip, pieces[0], pieces[1])
                second = jnp.where(flip, pieces[1], pieces[0])
                return jnp.concatenate([first, second], axis=axis)
            order = lax.rem(quarter - jnp.arange(quarters) + quarters, quarters)
            stacked = jnp.take(jnp.stack(pieces), order, axis=0)
            return jnp.concatenate([stacked[i] for i in range(quarters)], axis=axis)

        def near(pieces, axis, keep):
            return jnp.concatenate(pieces, axis=axis) if keep else in_place(pieces, axis)

        def gather(value, width_axis, unit_axis, keep):
            mine = piece_of(value, 0, unit_axis)
            received = {0: mine}
            ahead = behind = mine
            for step in range(1, rows):
                if step <= rows // 2:
                    ahead = row_shift(ahead, -1)
                    received[step] = ahead
                if step <= (rows - 1) // 2:
                    behind = row_shift(behind, 1)
                    received[rows - step] = behind
            result = jnp.zeros(
                [width if i == width_axis else n for i, n in enumerate(value.shape)], value.dtype
            )
            for step in range(rows):
                if step == 0:
                    pieces = [piece_of(value, q, unit_axis) for q in range(quarters)]
                else:
                    pieces = [received[step]]
                    pieces += [quarter_shift(received[step], q) for q in range(1, quarters)]
                block = near(pieces, unit_axis, keep)
                place = lax.rem(row + step, rows) * shard
                result = lax.dynamic_update_slice_in_dim(result, block, place, width_axis)
            return result

        hidden_other = core_swap(hidden)
        hidden_far = pair_swap(hidden)
        cot_other = core_swap(cotangent)
        cot_far = pair_swap(cotangent)
        params = jnp.stack([ln1_gain, ln1_bias, ln2_gain, ln2_bias])
        params = both(params, core_swap(params)).astype(F32)
        gain_one, shift_one, gain_two, shift_two = [params[i][None, :] for i in range(4)]
        inputs = [both(hidden, hidden_other), both(hidden_far, core_swap(hidden_far))]
        cots = [both(cotangent, cot_other), both(cot_far, core_swap(cot_far))]
        segs = [segments, pair_swap(segments)]

        qkv_cols = qkv_weight.reshape(shard, 2, heads, 3, HEAD_DIM)
        qkv_cols = lax.dynamic_index_in_dim(qkv_cols, side, 1, keepdims=False)
        qkv_cols = jnp.swapaxes(qkv_cols, 1, 2).reshape(shard, 3, wide)
        qkv_all = gather(qkv_cols, 0, 2, whole_heads).reshape(width, 3 * wide)
        out_all = gather(half_of(out_weight, 0), 1, 0, whole_heads)
        up_all = gather(half_of(up_weight, 1), 0, 1, True)
        down_all = gather(half_of(down_weight, 0), 1, 0, True)

        bias_cols = lax.dynamic_index_in_dim(qkv_bias.reshape(2, heads, 3, HEAD_DIM), side, 0, keepdims=False)
        bias_cols = jnp.swapaxes(bias_cols, 0, 1).reshape(1, 3, wide)
        bias_cols = near([piece_of(bias_cols, q, 2) for q in range(quarters)], 2, whole_heads)
        bias_cols = bias_cols.reshape(1, 3 * wide).astype(F32)
        up_half = half_of(up_bias, 0)
        up_row = jnp.concatenate([piece_of(up_half, q, 0) for q in range(quarters)])[None, :].astype(F32)

        norms = []
        contexts = []
        grads_mixed = []
        for values, cot, seg in zip(inputs, cots, segs):
            unit, inv = normalize(values.astype(F32))
            act_one = (unit * gain_one + shift_one).astype(BF16)
            act_two = (unit * gain_two + shift_two).astype(BF16)
            norms.append((unit, inv, act_one, act_two))
            cos_rows, sine_rows = rotary_tables(doc_positions(seg).reshape(length))
            mixed = dot(act_one, qkv_all) + bias_cols
            cos_wide = jnp.tile(cos_rows, (1, 2 * wide // LANES))
            sine_wide = jnp.tile(sine_rows, (1, 2 * wide // LANES))
            turned = mixed[:, : 2 * wide]
            lane = jnp.arange(2 * wide) % HEAD_DIM
            swapped = jnp.where(
                lane < ROT // 2, jnp.roll(turned, -(ROT // 2), axis=1), jnp.roll(turned, ROT // 2, axis=1)
            )
            turned = turned * cos_wide + swapped * sine_wide
            qkv = jnp.concatenate([turned, mixed[:, 2 * wide :]], axis=1).astype(BF16)
            grad_context = dot(cot, out_all, NT).astype(BF16)
            context, grad_mixed = attention(qkv, grad_context, seg, cos_rows, sine_rows)
            contexts.append(context)
            grads_mixed.append(grad_mixed)

        feeds = [feed(norm[3], cot, up_all, up_row, down_all) for norm, cot in zip(norms, cots)]

        def reduce_grad(left, right, width_axis, unit_axis, placed, shape=None):
            total = dot(left[0], right[0], TN) + dot(left[1], right[1], TN)
            if shape is not None:
                total = total.reshape(shape)
            mine = piece_of(total, 0, unit_axis, placed)
            for q in range(1, quarters):
                part = piece_of(total, q, unit_axis, placed).astype(BF16)
                mine = mine + quarter_shift(part, -q).astype(F32)
            cut = lambda t: lax.dynamic_slice_in_dim(mine, lax.rem(row + t, rows) * shard, shard, width_axis)
            result = cut(0)
            for t in range(1, rows):
                result = result + row_shift(cut(t).astype(BF16), t).astype(F32)
            result = result.astype(BF16)
            pieces = [result] + [quarter_shift(result, q) for q in range(1, quarters)]
            result = in_place(pieces, unit_axis)
            far = pair_swap(result)
            flip = side == 0
            return jnp.concatenate(
                [jnp.where(flip, result, far), jnp.where(flip, far, result)], axis=unit_axis
            ).astype(F32)

        acts_one = [n[2] for n in norms]
        acts_two = [n[3] for n in norms]
        out_grad = reduce_grad(contexts, cots, 1, 0, whole_heads)
        qkv_grad = reduce_grad(acts_one, grads_mixed, 0, 2, whole_heads, (width, 3, wide))
        down_grad = reduce_grad([f[0] for f in feeds], cots, 1, 0, True)
        up_grad = reduce_grad(acts_two, [f[1] for f in feeds], 0, 1, True)
        qkv_grad = qkv_grad.reshape(shard, 3, 2 * heads, HEAD_DIM)
        qkv_grad = jnp.swapaxes(qkv_grad, 1, 2).reshape(shard, 6 * wide)

        outs = []
        slopes = []
        norm_sums = jnp.zeros((4, width), F32)
        for index in range(2):
            unit, inv, _, _ = norms[index]
            act, grad_up, _ = feeds[index]
            outs.append((dot(contexts[index], out_all) + dot(act, down_all)).astype(BF16))
            grad_one = dot(grads_mixed[index], qkv_all, NT)
            grad_two = dot(grad_up, up_all, NT)
            norm_sums += jnp.stack(
                [
                    jnp.sum(grad_one * unit, axis=0),
                    jnp.sum(grad_one, axis=0),
                    jnp.sum(grad_two * unit, axis=0),
                    jnp.sum(grad_two, axis=0),
                ]
            )
            scaled = grad_one * gain_one + grad_two * gain_two
            mean_scaled = jnp.mean(scaled, axis=1, keepdims=True)
            mean_unit = jnp.mean(scaled * unit, axis=1, keepdims=True)
            slopes.append((inv * (scaled - mean_scaled - unit * mean_unit)).astype(BF16))

        def fold(pair):
            sums = []
            for value in pair:
                kept = lax.dynamic_slice_in_dim(value, col * half_width, half_width, 1).astype(F32)
                given = lax.dynamic_slice_in_dim(value, (1 - col) * half_width, half_width, 1)
                sums.append(kept + core_swap(given).astype(F32))
            return sums[0] + pair_swap(sums[1].astype(BF16)).astype(F32)

        cot_local = cotangent.astype(F32)
        output = hidden.astype(F32) + fold(outs) + (out_bias.astype(F32) + down_bias.astype(F32))
        input_grad = cot_local + fold(slopes)

        qkv_sum = (
            jnp.sum(grads_mixed[0].astype(F32), axis=0) + jnp.sum(grads_mixed[1].astype(F32), axis=0)
        ).reshape(3, wide)
        if whole_heads:
            qkv_sum = in_place([piece_of(qkv_sum, q, 1, True) for q in range(quarters)], 1)
        up_sum = (feeds[0][2] + feeds[1][2])[0]
        up_sum = in_place([piece_of(up_sum, q, 0, True) for q in range(quarters)], 0)

        def widen(value):
            zeros = jnp.zeros_like(value)
            flip = side == 0
            return jnp.concatenate([jnp.where(flip, value, zeros), jnp.where(flip, zeros, value)], axis=-1)

        kept = lax.dynamic_slice_in_dim(norm_sums, col * half_width, half_width, 1)
        given = lax.dynamic_slice_in_dim(norm_sums, (1 - col) * half_width, half_width, 1)
        norm_sums = kept + core_swap(given)
        small = jnp.concatenate(
            [widen(qkv_sum).reshape(-1), widen(up_sum), jnp.sum(cot_local, axis=0), norm_sums.reshape(-1)]
        )
        small = lax.psum(small, ("dp", "row"))
        sizes = [6 * wide, 2 * units, half_width, half_width, half_width, half_width, half_width]
        parts = []
        start = 0
        for size in sizes:
            parts.append(lax.slice_in_dim(small, start, start + size))
            start += size
        qkv_sum, up_sum, cot_sum, gain_one_sum, shift_one_sum, gain_two_sum, shift_two_sum = parts
        qkv_sum = jnp.swapaxes(qkv_sum.reshape(3, 2 * heads, HEAD_DIM), 0, 1).reshape(-1)
        return (
            output,
            input_grad,
            gain_one_sum,
            shift_one_sum,
            qkv_grad,
            qkv_sum,
            out_grad,
            cot_sum,
            gain_two_sum,
            shift_two_sum,
            up_grad,
            up_sum,
            down_grad,
            cot_sum,
        )

    return local


def make_fast(groups, rows, cols):
    quarters = groups // 2

    def pair_swap(value):
        return lax.ppermute(value, "dp", [(d, d ^ 1) for d in range(groups)])

    def quarter_shift(value, shift):
        moves = [(2 * a + b, 2 * ((a + shift) % quarters) + b) for a in range(quarters) for b in range(2)]
        return lax.ppermute(value, "dp", moves)

    def row_shift(value, shift):
        return lax.ppermute(value, "row", [(r, (r + shift) % rows) for r in range(rows)])

    def core_swap(value):
        return lax.ppermute(value, "col", [(0, 1), (1, 0)])

    def local(
        hidden,
        segments,
        ln1_gain,
        ln1_bias,
        qkv_weight,
        qkv_bias,
        out_weight,
        out_bias,
        ln2_gain,
        ln2_bias,
        up_weight,
        up_bias,
        down_weight,
        down_bias,
        cotangent,
    ):
        assert segments.shape[0] == 1 and cols == 2
        length = segments.shape[1]
        half_width = hidden.shape[1]
        width = 2 * half_width
        shard = qkv_weight.shape[0]
        heads = qkv_weight.shape[1] // (3 * HEAD_DIM) // 2
        wide = heads * HEAD_DIM
        units = up_weight.shape[1] // 2
        whole_heads = heads % quarters == 0
        dp = lax.axis_index("dp")
        row = lax.axis_index("row")
        col = lax.axis_index("col")
        side = lax.rem(dp, 2)
        quarter = dp // 2

        def both(mine, other):
            flip = col == 0
            return jnp.concatenate([jnp.where(flip, mine, other), jnp.where(flip, other, mine)], axis=-1)

        def half_of(value, axis):
            size = value.shape[axis] // 2
            return lax.dynamic_slice_in_dim(value, side * size, size, axis)

        def piece_of(value, shift, axis, placed=False):
            size = value.shape[axis] // quarters
            if placed:
                return lax.slice_in_dim(value, shift * size, (shift + 1) * size, axis=axis)
            return lax.dynamic_slice_in_dim(value, lax.rem(quarter - shift + quarters, quarters) * size, size, axis)

        def in_place(pieces, axis):
            if quarters == 1:
                return pieces[0]
            if quarters == 2:
                flip = quarter == 0
                first = jnp.where(flip, pieces[0], pieces[1])
                second = jnp.where(flip, pieces[1], pieces[0])
                return jnp.concatenate([first, second], axis=axis)
            order = lax.rem(quarter - jnp.arange(quarters) + quarters, quarters)
            stacked = jnp.take(jnp.stack(pieces), order, axis=0)
            return jnp.concatenate([stacked[i] for i in range(quarters)], axis=axis)

        def near(pieces, axis, keep):
            return jnp.concatenate(pieces, axis=axis) if keep else in_place(pieces, axis)

        def gather(value, width_axis, unit_axis, keep):
            mine = piece_of(value, 0, unit_axis)
            received = {0: mine}
            ahead = behind = mine
            for step in range(1, rows):
                if step <= rows // 2:
                    ahead = row_shift(ahead, -1)
                    received[step] = ahead
                if step <= (rows - 1) // 2:
                    behind = row_shift(behind, 1)
                    received[rows - step] = behind
            result = jnp.zeros(
                [width if i == width_axis else n for i, n in enumerate(value.shape)], value.dtype
            )
            for step in range(rows):
                if step == 0:
                    pieces = [piece_of(value, q, unit_axis) for q in range(quarters)]
                else:
                    pieces = [received[step]]
                    pieces += [quarter_shift(received[step], q) for q in range(1, quarters)]
                block = near(pieces, unit_axis, keep)
                place = lax.rem(row + step, rows) * shard
                result = lax.dynamic_update_slice_in_dim(result, block, place, width_axis)
            return result

        place = jnp.arange(length, dtype=jnp.int32)
        before = segments[0][None, :] < segments[0][:, None]
        position = place - jnp.sum(before.astype(jnp.int32), axis=1)
        rows_own = jnp.stack([segments[0].astype(F32), position.astype(F32)] + [jnp.zeros((length,), F32)] * 6)
        params = jnp.stack([ln1_gain, ln1_bias, ln2_gain, ln2_bias] * 2).astype(F32)
        lane = jnp.arange(LANES) % HEAD_DIM
        frequency = 10000.0 ** (-2.0 * (lane % (ROT // 2)).astype(F32) / ROT)
        sign = jnp.where(lane < ROT // 2, -1.0, 1.0)
        turning = lane < ROT
        freq = jnp.stack([jnp.where(turning, frequency, 0.0), jnp.where(turning, sign, 0.0)] * 4).astype(F32)

        def by_quarter(value):
            n = value.shape[0]
            value = value.reshape(n, 2, quarters, heads // quarters, 3, HEAD_DIM)
            value = lax.dynamic_index_in_dim(value, side, 1, keepdims=False)
            value = jnp.swapaxes(value, 2, 3).reshape(n, quarters, 3 * wide // quarters)
            flip = quarter == 0
            mine = jnp.where(flip, value[:, 0], value[:, 1])
            other = jnp.where(flip, value[:, 1], value[:, 0])
            return jnp.concatenate([mine, other], axis=1)

        wq = by_quarter(qkv_weight)
        bq = by_quarter(qkv_bias[None, :]).astype(F32)
        up_half = half_of(up_bias, 0)
        up_row = jnp.concatenate([piece_of(up_half, q, 0) for q in range(quarters)])[None, :].astype(F32)
        grad_q, grad_o, grad_u, grad_d, keep, near_parts, far_parts, small = whole_block(
            hidden, cotangent, wq, out_weight, up_weight, down_weight, rows_own, params, bq, up_row, freq, rows
        )
        heads_of = lambda value, n: jnp.swapaxes(
            value.reshape(n, 2 * quarters, 3, heads // quarters, HEAD_DIM), 2, 3
        ).reshape(n, 6 * wide)
        sums = lambda i: keep[i].astype(F32) + near_parts[i].astype(F32) + far_parts[i].astype(F32)
        output = hidden.astype(F32) + sums(0) + (out_bias.astype(F32) + down_bias.astype(F32))
        input_grad = cotangent.astype(F32) + sums(1)
        qkv_sum = heads_of(jnp.concatenate([small[0, 0, : 3 * wide], small[1, 0, : 3 * wide]])[None, :], 1)[0]
        up_sum = jnp.concatenate([small[0, 1], small[1, 1]])
        tail = lax.dynamic_slice_in_dim(small[3, 2:6], col * half_width, half_width, 1)
        cot_sum = lax.dynamic_slice_in_dim(small[2, 6], col * half_width, half_width, 0)
        return (
            output,
            input_grad,
            tail[0],
            tail[1],
            heads_of(grad_q, shard).astype(F32),
            qkv_sum,
            grad_o.astype(F32),
            cot_sum,
            tail[2],
            tail[3],
            grad_u.astype(F32),
            up_sum,
            grad_d.astype(F32),
            cot_sum,
        )

    return local


def solution(mesh):
    placed = (
        P(("dp", "row"), "col"),
        P(("dp", "row"), None),
        P("col"),
        P("col"),
        P("row", "col"),
        P("col"),
        P("col", "row"),
        P("col"),
        P("col"),
        P("col"),
        P("row", "col"),
        P("col"),
        P("col", "row"),
        P("col"),
        P(("dp", "row"), "col"),
    )
    groups = mesh.shape["dp"]
    make = make_fast if groups == 4 else make_general
    return jax.shard_map(
        make(mesh.shape["dp"], mesh.shape["row"], mesh.shape["col"]),
        mesh=mesh,
        in_specs=placed,
        out_specs=(
            P(("dp", "row"), "col"),
            P(("dp", "row"), "col"),
            P("col"),
            P("col"),
            P("row", "col"),
            P("col"),
            P("col", "row"),
            P("col"),
            P("col"),
            P("col"),
            P("row", "col"),
            P("col"),
            P("col", "row"),
            P("col"),
        ),
        check_vma=False,
    )
```

```python
import functools

import jax
import jax.numpy as jnp
import numpy as np
from jax import lax
from jax.experimental import pallas as pl
from jax.experimental.pallas import tpu as pltpu
from jax.sharding import PartitionSpec as P

HEAD_DIM = 64
ROT = 16
EPS = 1e-05
MAX_DOC = 512
DOCS = 4
LANES = 128
BF16 = jnp.bfloat16
F32 = jnp.float32

NT = (((1,), (1,)), ((), ()))
TN = (((0,), (0,)), ((), ()))
NN = (((1,), (0,)), ((), ()))


def dot(a, b, dims=NN):
    return lax.dot_general(a, b, dims, preferred_element_type=F32)


def doc_positions(segments):
    length = segments.shape[-1]
    places = jnp.arange(length, dtype=jnp.int32)
    changed = jnp.concatenate(
        [jnp.ones(segments.shape[:-1] + (1,), dtype=bool), segments[..., 1:] != segments[..., :-1]],
        axis=-1,
    )
    starts = lax.cummax(jnp.where(changed, places, jnp.zeros_like(places)), axis=segments.ndim - 1)
    return places - starts


def rotary_tables(positions):
    lane = jnp.arange(LANES) % HEAD_DIM
    frequency = 10000.0 ** (-2.0 * (lane % (ROT // 2)).astype(F32) / ROT)
    turning = lane < ROT
    angles = positions.astype(F32)[:, None] * jnp.where(turning, frequency, 0.0)[None, :]
    sign = jnp.where(turning, jnp.where(lane < ROT // 2, -1.0, 1.0), 0.0)
    return jnp.cos(angles), jnp.sin(angles) * sign[None, :]


def turn(values, cos_rows, sine_rows, low_lanes):
    half = ROT // 2
    up = pltpu.roll(values, values.shape[1] - half, 1)
    down = pltpu.roll(values, half, 1)
    return values * cos_rows + jnp.where(low_lanes, up, down) * sine_rows


def attention_kernel(
    q_ref, k_ref, v_ref, gc_ref, seg_row_ref, seg_col_ref, cos_ref, sin_ref, ctx_ref, gm_ref, dk_acc, dv_acc, *, block
):
    pair = pl.program_id(0)
    pairs = pl.num_programs(0)
    length = q_ref.shape[0]
    lane = lax.broadcasted_iota(jnp.int32, (1, LANES), 1)
    low_lanes = lane % HEAD_DIM < ROT // 2
    first = lane < HEAD_DIM
    zero = jnp.zeros((), BF16)

    def split(values):
        return [jnp.where(first, values, zero), jnp.where(first, zero, values)]

    dk_acc[...] = jnp.zeros_like(dk_acc)
    dv_acc[...] = jnp.zeros_like(dv_acc)
    for begin in range(0, length, block):
        low = max(0, begin - (MAX_DOC - 1)) // LANES * LANES
        rows = pl.ds(begin, block)
        keys = pl.ds(low, begin + block - low)
        width = begin + block - low
        q_parts = split(q_ref[rows, :] * jnp.asarray(HEAD_DIM**-0.5, BF16))
        g_parts = split(gc_ref[rows, :])
        k_block = k_ref[keys, :]
        v_block = v_ref[keys, :]
        places = begin + lax.broadcasted_iota(jnp.int32, (block, width), 0)
        key_places = low + lax.broadcasted_iota(jnp.int32, (block, width), 1)
        allowed = (seg_col_ref[rows, :] == seg_row_ref[:, keys]) & (places >= key_places)
        probs = []
        grads = []
        for part in range(2):
            scores = dot(q_parts[part], k_block, NT)
            scores = jnp.where(allowed, scores, -1e30)
            top = jnp.max(scores, axis=1, keepdims=True)
            powers = jnp.exp(scores - top)
            total = jnp.sum(powers, axis=1, keepdims=True)
            chances = powers * (1.0 / total)
            slopes = dot(g_parts[part], v_block, NT)
            inner = jnp.sum(slopes * chances, axis=1, keepdims=True)
            probs.append(chances.astype(BF16))
            grads.append((chances * (slopes - inner)).astype(BF16))
        context = jnp.where(first, dot(probs[0], v_block), dot(probs[1], v_block))
        ctx_ref[rows, :] = context.astype(BF16)
        dq = jnp.where(first, dot(grads[0], k_block), dot(grads[1], k_block)) * HEAD_DIM**-0.5
        dq = turn(dq, cos_ref[rows, :], -sin_ref[rows, :], low_lanes)
        gm_ref[rows, pl.ds(pl.multiple_of(pair * LANES, LANES), LANES)] = dq.astype(BF16)
        dk_acc[keys, :] += dot(grads[0], q_parts[0], TN) + dot(grads[1], q_parts[1], TN)
        dv_acc[keys, :] += dot(probs[0], g_parts[0], TN) + dot(probs[1], g_parts[1], TN)
    dk = turn(dk_acc[...], cos_ref[...], -sin_ref[...], low_lanes)
    gm_ref[:, pl.ds(pl.multiple_of((pairs + pair) * LANES, LANES), LANES)] = dk.astype(BF16)
    gm_ref[:, pl.ds(pl.multiple_of((2 * pairs + pair) * LANES, LANES), LANES)] = dv_acc[...].astype(BF16)


def attention(qkv, grad_context, seg_row, cos_rows, sine_rows):
    length, wide = qkv.shape
    pairs = wide // (3 * LANES)
    block = min(256, length)
    column = lambda shift: pl.BlockSpec((length, LANES), lambda p: (0, shift + p))
    whole = lambda *shape: pl.BlockSpec(shape, lambda p: (0, 0))
    flops = pairs * 2 * 6 * 2 * length * length * LANES // 2
    return pl.pallas_call(
        functools.partial(attention_kernel, block=block),
        grid=(pairs,),
        in_specs=[
            column(0),
            column(pairs),
            column(2 * pairs),
            column(0),
            whole(1, length),
            whole(length, 1),
            whole(length, LANES),
            whole(length, LANES),
        ],
        out_specs=[column(0), whole(length, wide)],
        out_shape=[
            jax.ShapeDtypeStruct((length, pairs * LANES), BF16),
            jax.ShapeDtypeStruct((length, wide), BF16),
        ],
        scratch_shapes=[pltpu.VMEM((length, LANES), F32), pltpu.VMEM((length, LANES), F32)],
        compiler_params=pltpu.CompilerParams(vmem_limit_bytes=48 << 20),
        cost_estimate=pl.CostEstimate(
            flops=flops, bytes_accessed=6 * length * wide, transcendentals=pairs * length * length
        ),
        name="attention",
    )(qkv, qkv, qkv, grad_context, seg_row, seg_row.reshape(length, 1), cos_rows, sine_rows)


def feed_kernel(a_ref, g_ref, up_ref, bias_ref, down_ref, act_ref, gup_ref, sum_ref, *, chunk):
    units = up_ref.shape[1]

    @pl.when(pl.program_id(0) == 0)
    def _():
        sum_ref[...] = jnp.zeros_like(sum_ref)

    for begin in range(0, units, chunk):
        cols = pl.ds(begin, chunk)
        up = dot(a_ref[...], up_ref[:, cols]) + bias_ref[:, cols]
        pull = dot(g_ref[...], down_ref[cols, :], NT)
        gate = 0.5 * (1.0 + lax.erf(up * 0.5**0.5))
        bell = jnp.exp(-0.5 * up * up) * 0.3989422804014327
        act_ref[:, cols] = (up * gate).astype(BF16)
        grad = (pull * (gate + up * bell)).astype(BF16)
        gup_ref[:, cols] = grad
        sum_ref[:, cols] += jnp.sum(grad.astype(F32), axis=0, keepdims=True)


def feed(normed, cot, up_weight, up_bias, down_weight):
    tokens, width = normed.shape
    units = up_weight.shape[1]
    block = min(256, tokens)
    rows = lambda size: pl.BlockSpec((block, size), lambda i: (i, 0))
    whole = lambda *shape: pl.BlockSpec(shape, lambda i: (0, 0))
    return pl.pallas_call(
        functools.partial(feed_kernel, chunk=min(256, units)),
        grid=(tokens // block,),
        in_specs=[rows(width), rows(width), whole(width, units), whole(1, units), whole(units, width)],
        out_specs=[rows(units), rows(units), whole(1, units)],
        out_shape=[
            jax.ShapeDtypeStruct((tokens, units), BF16),
            jax.ShapeDtypeStruct((tokens, units), BF16),
            jax.ShapeDtypeStruct((1, units), F32),
        ],
        compiler_params=pltpu.CompilerParams(vmem_limit_bytes=48 << 20),
        cost_estimate=pl.CostEstimate(
            flops=4 * tokens * width * units,
            bytes_accessed=4 * tokens * width + 4 * width * units + 4 * tokens * units,
            transcendentals=2 * tokens * units,
        ),
        name="feed",
    )(normed, cot, up_weight, up_bias, down_weight)


MESH = pl.DeviceIdType.MESH


class Net:
    def __init__(self, send_sems, recv_sems):
        self.send_sems, self.recv_sems = send_sems, recv_sems
        self.slots = {}
        self.pending = []

    def slot(self, key):
        return self.slots.setdefault(key, len(self.slots))

    def make(self, key, source, target, device):
        i = self.slot(key)
        return pltpu.make_async_remote_copy(
            src_ref=source,
            dst_ref=target,
            send_sem=self.send_sems.at[i],
            recv_sem=self.recv_sems.at[i],
            device_id=device,
            device_id_type=MESH,
        )

    def send(self, key, source, target, device):
        copy = self.make(key, source, target, device)
        copy.start()
        self.pending.append(copy)
        return copy

    def sent(self, copy):
        copy.wait_send()
        self.pending = [other for other in self.pending if other is not copy]

    def wait(self, key, landed, device):
        self.make(key, landed, landed, device).wait_recv()

    def drain(self):
        for copy in self.pending:
            copy.wait_send()
        self.pending = []


def spread(columns, width):
    return jnp.concatenate([columns] * (width // LANES), axis=1)


def attend_pair(mix, base, gc, gc_base, ctx, seg_row, seg_col, cos_tab, sin_tab, dk_acc, dv_acc, block):
    length = mix.shape[0]
    lane = lax.broadcasted_iota(jnp.int32, (1, LANES), 1)
    low_lanes = lane % HEAD_DIM < ROT // 2
    first = lane < HEAD_DIM
    zero = jnp.zeros((), BF16)
    cols = [pl.ds(base + i * LANES, LANES) for i in range(3)]
    head_cols = pl.ds(gc_base, LANES)

    def split(values):
        return [jnp.where(first, values, zero), jnp.where(first, zero, values)]

    dk_acc[...] = jnp.zeros_like(dk_acc)
    dv_acc[...] = jnp.zeros_like(dv_acc)
    for begin in range(0, length, block):
        low = max(0, begin - (MAX_DOC - 1)) // LANES * LANES
        width = begin + block - low
        rows = pl.ds(begin, block)
        keys = pl.ds(low, width)
        q_parts = split(mix[rows, cols[0]] * jnp.asarray(HEAD_DIM**-0.5, BF16))
        g_parts = split(gc[rows, head_cols])
        k_block = mix[keys, cols[1]]
        v_block = mix[keys, cols[2]]
        places = begin + lax.broadcasted_iota(jnp.int32, (block, width), 0)
        key_places = low + lax.broadcasted_iota(jnp.int32, (block, width), 1)
        allowed = (spread(seg_col[rows, :], width) == seg_row[0:1, keys]) & (places >= key_places)
        probs = []
        grads = []
        for part in range(2):
            scores = dot(q_parts[part], k_block, NT)
            scores = jnp.where(allowed, scores, -1e30)
            top = jnp.max(scores, axis=1, keepdims=True)
            powers = jnp.exp(scores - top)
            total = jnp.sum(powers, axis=1, keepdims=True)
            chances = powers * (1.0 / total)
            slopes = dot(g_parts[part], v_block, NT)
            inner = jnp.sum(slopes * chances, axis=1, keepdims=True)
            probs.append(chances.astype(BF16))
            grads.append((chances * (slopes - inner)).astype(BF16))
        ctx[rows, head_cols] = jnp.where(first, dot(probs[0], v_block), dot(probs[1], v_block)).astype(BF16)
        dq = jnp.where(first, dot(grads[0], k_block), dot(grads[1], k_block)) * HEAD_DIM**-0.5
        mix[rows, cols[0]] = turn(dq, cos_tab[rows, :], -sin_tab[rows, :], low_lanes).astype(BF16)
        dk_acc[keys, :] += dot(grads[0], q_parts[0], TN) + dot(grads[1], q_parts[1], TN)
        dv_acc[keys, :] += dot(probs[0], g_parts[0], TN) + dot(probs[1], g_parts[1], TN)
    dq = mix[:, cols[0]].astype(F32)
    dk = pltpu.roll(turn(dk_acc[...], cos_tab[...], -sin_tab[...], low_lanes), HEAD_DIM, 1)
    dv = dv_acc[...]
    mix[:, cols[0]] = jnp.where(first, dq, dk).astype(BF16)
    mix[:, cols[1]] = jnp.where(first, dv, dq).astype(BF16)
    mix[:, cols[2]] = jnp.where(first, dk, dv).astype(BF16)


def block_kernel(
    hidden, cot, wq_in, wo_in, wu_in, wd_in,
    segments_in, freq_in, gain_one_in, shift_one_in, gain_two_in, shift_two_in, bq_in, bu_in,
    rq_out, ro_out, ru_out, rd_out, sum_out, slope_out, gains_out, bq_out, bu_out, cot_out,
    X, G, A, B, OUT, WQ, WO, WU, WD, MIX, CTX, ACT, GUP, rows_own, rows_far, params, biases, seg_col, cos_tab, sin_tab,
    dk_acc, dv_acc, SQ, SO, SU, SD, YQ, YO, YU, YD, ZQ, ZO, ZU, ZD, HQ, HO, HU, HD, LAND, FAR, SMALL, SMALL_Z, SMALL_P,
    send_sems, recv_sems, local_sems,
):
    R = 4
    dp, row, col = lax.axis_index("dp"), lax.axis_index("row"), lax.axis_index("col")
    side, quarter = lax.rem(dp, 2), lax.div(dp, 2)
    length, half = hidden.shape
    shard = wq_in.shape[0]
    core = (dp, row, 1 - col)
    xdev = (dp + 1 - 2 * side, row, col)
    ydev = (side + 2 * (1 - quarter), row, col)

    def zdev(t):
        return (dp, lax.rem(row + t + R, R), col)

    barrier = pltpu.get_barrier_semaphore()
    peers = [core, xdev, ydev] + [zdev(t) for t in range(1, R)]
    for peer in peers:
        pl.semaphore_signal(barrier, inc=1, device_id=peer, device_id_type=MESH)
    pl.semaphore_wait(barrier, len(peers))

    net = Net(send_sems, recv_sems)
    own_cols = pl.ds(pl.multiple_of(col * half, half), half)
    far_cols = pl.ds(pl.multiple_of((1 - col) * half, half), half)
    local = []

    def move(source, target):
        copy = pltpu.make_async_copy(source, target, local_sems.at[len(local)])
        copy.start()
        local.append(copy)
        return copy

    qc = WQ.shape[1] // 2
    oc = WO.shape[0] // 2
    uc = WU.shape[1] // 2

    def seat(h, size):
        return pl.ds(pl.multiple_of((side * 2 + (quarter if h == 0 else 1 - quarter)) * size, size), size)

    def block(t):
        return pl.ds(pl.multiple_of(lax.rem(row + t + R, R) * shard, shard), shard)

    every = slice(None)
    weights = {
        "q": (lambda h: wq_in.at[:, seat(h, qc)], lambda t, h: WQ.at[block(t), pl.ds(h * qc, qc)]),
        "o": (lambda h: wo_in.at[seat(h, oc), :], lambda t, h: WO.at[pl.ds(h * oc, oc), block(t)]),
        "u": (lambda h: wu_in.at[:, seat(h, uc)], lambda t, h: WU.at[block(t), pl.ds(h * uc, uc)]),
        "d": (lambda h: wd_in.at[seat(h, uc), :], lambda t, h: WD.at[pl.ds(h * uc, uc), block(t)]),
    }
    here_w = {}

    def start_along(name):
        here, place = weights[name]
        net.send((name, 1), here(0), place(0, 0), zdev(-1))
        net.send((name, 3), here(0), place(0, 0), zdev(1))

    def start_here(name):
        here, place = weights[name]
        here_w[name] = [move(here(h), place(0, h)) for h in range(2)]

    def along(name, t):
        place = weights[name][1]
        net.wait((name, t), place(t, 0), zdev(t))
        if t == 1:
            net.send((name, 2), place(t, 0), place(t, 0), zdev(-1))
        net.send((name, t, "y"), place(t, 0), place(t, 1), ydev)

    def across_y(name):
        place = weights[name][1]
        for t in (1, 3, 2):
            net.wait((name, t, "y"), place(t, 1), ydev)

    def have_here(name):
        for copy in here_w[name]:
            copy.wait()

    chunks = 2
    piece = length // chunks

    def chunk(c):
        return pl.ds(c * piece, piece)

    handed = []

    def hand_over(name, buffer, c):
        net.wait(("x " + name, c), buffer.at[1, chunk(c), own_cols], xdev)
        spot = buffer.at[1, chunk(c), own_cols]
        handed.append(net.send(("far " + name, c), spot, spot, core))

    def have_far(name, buffer):
        for c in range(chunks):
            net.wait(("far " + name, c), buffer.at[1, chunk(c), far_cols], core)

    start_along("q")
    net.send("core h", hidden, X.at[0, :, own_cols], core)
    start_along("o")
    here_h = move(hidden, X.at[0, :, own_cols])
    lane = lax.broadcasted_iota(jnp.int32, (1, LANES), 1)
    low_lanes = lane % HEAD_DIM < ROT // 2
    first = lane < HEAD_DIM

    seg = segments_in[...]
    start = jnp.zeros_like(seg)
    for number in range(1, DOCS):
        count = jnp.sum((seg < number).astype(jnp.int32), axis=1, keepdims=True)
        start = jnp.where(seg == number, count, start)
    rows_own[0:1, :] = seg.astype(F32)
    rows_own[1:2, :] = (lax.broadcasted_iota(jnp.int32, seg.shape, 1) - start).astype(F32)
    for i, source in enumerate([gain_one_in, shift_one_in, gain_two_in, shift_two_in]):
        params[i : i + 1, own_cols] = source[...].astype(F32).reshape(1, half)
    biases[0:1, pl.ds(0, bq_in.shape[0])] = bq_in[...].astype(F32).reshape(1, -1)
    biases[1:2, :] = bu_in[...].astype(F32).reshape(1, -1)
    net.send("core p", params.at[:, own_cols], params.at[:, own_cols], core)
    net.send("x rows", rows_own, rows_far, xdev)
    for c in range(chunks):
        net.send(("x h", c), hidden.at[chunk(c), :], X.at[1, chunk(c), own_cols], xdev)
    for c in range(chunks):
        net.send(("x g", c), cot.at[chunk(c), :], G.at[1, chunk(c), own_cols], xdev)
    net.send("core g", cot, G.at[0, :, own_cols], core)
    start_here("q")
    start_here("o")
    here_g = move(cot, G.at[0, :, own_cols])
    start_here("u")
    start_here("d")

    tile = 256
    GC = ACT.at[0]

    def each_tile(body):
        @pl.loop(0, length // tile)
        def _(i):
            body(pl.ds(pl.multiple_of(i * tile, tile), tile))

    def unit_rows(s, at):
        values = X[s, at, :].astype(F32)
        centred = values - jnp.mean(values, axis=-1, keepdims=True)
        inv = lax.rsqrt(jnp.mean(centred * centred, axis=-1, keepdims=True) + EPS)
        return centred * inv, inv

    def norm(s, at):
        unit, _ = unit_rows(s, at)
        A[s, at, :] = (unit * params[0:1, :] + params[1:2, :]).astype(BF16)
        B[s, at, :] = (unit * params[2:3, :] + params[3:4, :]).astype(BF16)

    def tables(rows):
        seg_col[...] = jnp.transpose(jnp.broadcast_to(rows[0:1, :], (LANES, length)))
        angles = jnp.transpose(jnp.broadcast_to(rows[1:2, :], (LANES, length))) * freq_in[0:1, :]
        cos_tab[...] = jnp.cos(angles)
        sin_tab[...] = jnp.sin(angles) * freq_in[1:2, :]

    def project(s, h):
        def body(at):
            mixed = dot(A[s, at, :], WQ[:, pl.ds(h * qc, qc)]) + biases[0:1, seat(h, qc)]
            t0, t1, t2 = [mixed[:, i * LANES : (i + 1) * LANES] for i in range(3)]
            query = jnp.where(first, t0, t1)
            key = pltpu.roll(jnp.where(first, t2, t0), HEAD_DIM, 1)
            value = jnp.where(first, t1, t2)
            cos_rows, sin_rows = cos_tab[at, :], sin_tab[at, :]
            MIX[s, at, pl.ds(h * qc, LANES)] = turn(query, cos_rows, sin_rows, low_lanes).astype(BF16)
            MIX[s, at, pl.ds(h * qc + LANES, LANES)] = turn(key, cos_rows, sin_rows, low_lanes).astype(BF16)
            MIX[s, at, pl.ds(h * qc + 2 * LANES, LANES)] = value.astype(BF16)

        each_tile(body)

    def pull_context(s, h):
        def body(at):
            GC[at, pl.ds(h * oc, oc)] = dot(G[s, at, :], WO[pl.ds(h * oc, oc), :], NT).astype(BF16)

        each_tile(body)

    def attend(s, rows, h):
        attend_pair(
            MIX.at[s], h * qc, GC, h * oc, CTX.at[s], rows, seg_col, cos_tab, sin_tab, dk_acc, dv_acc, tile
        )

    tables(rows_own)
    here_h.wait()
    net.wait("core h", X.at[0, :, far_cols], core)
    net.wait("core p", params.at[:, far_cols], core)
    along("q", 1)
    each_tile(lambda at: norm(0, at))
    along("q", 3)
    along("o", 1)
    along("o", 3)
    start_along("u")
    start_along("d")
    along("q", 2)
    have_here("q")
    project(0, 0)
    along("o", 2)
    have_here("o")
    here_g.wait()
    net.wait("core g", G.at[0, :, far_cols], core)
    pull_context(0, 0)
    hand_over("h", X, 0)
    attend(0, rows_own, 0)
    along("u", 1)
    across_y("q")
    project(0, 1)
    across_y("o")
    pull_context(0, 1)
    hand_over("h", X, 1)
    attend(0, rows_own, 1)
    along("u", 3)
    net.wait("x rows", rows_far, xdev)
    tables(rows_far)
    have_far("h", X)
    each_tile(lambda at: norm(1, at))
    along("d", 1)
    hand_over("g", G, 0)
    project(1, 0)
    project(1, 1)
    along("d", 3)
    along("u", 2)
    hand_over("g", G, 1)
    have_far("g", G)
    pull_context(1, 0)
    pull_context(1, 1)
    attend(1, rows_far, 0)
    along("d", 2)
    attend(1, rows_far, 1)

    grads = {
        "q": (SQ, YQ, ZQ, HQ, rq_out, lambda t: (block(t), every), lambda p: (every, p), qc),
        "o": (SO, YO, ZO, HO, ro_out, lambda t: (every, block(t)), lambda p: (p, every), oc),
        "u": (SU, YU, ZU, HU, ru_out, lambda t: (block(t), every), lambda p: (every, p), uc),
        "d": (SD, YD, ZD, HD, rd_out, lambda t: (every, block(t)), lambda p: (p, every), uc),
    }

    def multiply(name, h, t):
        if name == "q":
            pairs_of = [(A[s, :, block(t)], MIX[s, :, pl.ds(h * qc, qc)]) for s in range(2)]
        elif name == "u":
            pairs_of = [(B[s, :, block(t)], GUP[s, :, pl.ds(h * uc, uc)]) for s in range(2)]
        elif name == "o":
            pairs_of = [(CTX[s, :, pl.ds(h * oc, oc)], G[s, :, block(t)]) for s in range(2)]
        else:
            pairs_of = [(ACT[s, :, pl.ds(h * uc, uc)], G[s, :, block(t)]) for s in range(2)]
        return (dot(*pairs_of[0], TN) + dot(*pairs_of[1], TN)).astype(BF16)

    turns = (2, 3, 1, 0)

    def other_part(name):
        source, landed, spot = grads[name][0], grads[name][1], grads[name][5]
        for t in turns:
            source[spot(t)] = multiply(name, 1, t)
            net.send(("gy", name, t), source.at[spot(t)], landed.at[spot(t)], ydev)

    def own_part(name):
        kept, spot = grads[name][2], grads[name][5]

        @pl.loop(0, R)
        def _(t):
            kept[spot(t)] = multiply(name, 0, t)

    def across(name, t):
        _, landed, kept, hops, _, spot, _, _ = grads[name]
        net.wait(("gy", name, t), landed.at[spot(t)], ydev)
        total = kept[spot(t)].astype(F32) + landed[spot(t)].astype(F32)
        if t == 1:
            net.wait(("gz", name, 2), hops.at[0], zdev(-1))
            total = total + hops[0].astype(F32)
        kept[spot(t)] = total.astype(BF16)
        if t == 2:
            net.send(("gz", name, 2), kept.at[spot(t)], hops.at[0], zdev(1))
        elif t == 3:
            net.send(("gz", name, 3), kept.at[spot(t)], hops.at[1], zdev(-1))
        elif t == 1:
            net.send(("gz", name, 1), kept.at[spot(t)], hops.at[2], zdev(1))

    def finish(name):
        _, _, kept, hops, result, spot, place, size = grads[name]
        net.wait(("gz", name, 3), hops.at[1], zdev(1))
        net.wait(("gz", name, 1), hops.at[2], zdev(-1))
        total = kept[spot(0)].astype(F32) + hops[1].astype(F32) + hops[2].astype(F32)
        kept[spot(0)] = total.astype(BF16)
        target = result.at[place(seat(0, size))]
        net.send(("ry", name), kept.at[spot(0)], target, ydev)
        net.send(("rx", name), kept.at[spot(0)], target, xdev)
        return move(kept.at[spot(0)], target)

    def far_seat(h, size):
        return pl.ds(pl.multiple_of(((1 - side) * 2 + (quarter if h == 0 else 1 - quarter)) * size, size), size)

    by_x = "u"

    def spread_out(name):
        _, _, _, _, result, _, place, size = grads[name]
        if name in by_x:
            target = result.at[place(far_seat(0, size))]
            net.wait(("rx", name), target, xdev)
            net.send(("rr", name), target, target, ydev)
        else:
            target = result.at[place(seat(1, size))]
            net.wait(("ry", name), target, ydev)
            net.send(("rr", name), target, target, xdev)

    def collect(name):
        _, _, _, _, result, _, place, size = grads[name]
        if name in by_x:
            net.wait(("ry", name), result.at[place(seat(1, size))], ydev)
        else:
            net.wait(("rx", name), result.at[place(far_seat(0, size))], xdev)
        net.wait(("rr", name), result.at[place(far_seat(1, size))], ydev if name in by_x else xdev)

    SMALL[...] = jnp.zeros_like(SMALL)
    other_part("o")
    other_part("q")
    have_here("u")
    have_here("d")
    across_y("u")
    across_y("d")

    def seat_of(h, size):
        return (quarter if h == 0 else 1 - quarter) * size

    def feed_part(s, h):
        def body(at):
            for begin in range(0, uc, tile):
                cols = pl.ds(h * uc + begin, tile)
                bias_at = (side * 2) * uc + seat_of(h, uc) + begin
                up = dot(B[s, at, :], WU[:, cols]) + biases[1:2, pl.ds(pl.multiple_of(bias_at, tile), tile)]
                pull = dot(G[s, at, :], WD[cols, :], NT)
                gate = 0.5 * (1.0 + lax.erf(up * 0.5**0.5))
                bell = jnp.exp(-0.5 * up * up) * 0.3989422804014327
                ACT[s, at, cols] = (up * gate).astype(BF16)
                grad = (pull * (gate + up * bell)).astype(BF16)
                GUP[s, at, cols] = grad
                SMALL[1:2, pl.ds(pl.multiple_of(seat_of(h, uc) + begin, tile), tile)] += jnp.sum(
                    grad.astype(F32), axis=0, keepdims=True
                )

        each_tile(body)

    def halves(value):
        left, right = value[:, :half], value[:, half:]
        return jnp.where(col == 0, left, right).astype(BF16), jnp.where(col == 0, right, left).astype(BF16)

    def leave(s, c, out, slope):
        @pl.loop(0, piece // tile)
        def _(i):
            at = pl.ds(pl.multiple_of(c * piece + i * tile, tile), tile)
            result = dot(CTX[s, at, :], WO[...]) + dot(ACT[s, at, :], WD[...])
            grad_one = dot(MIX[s, at, :], WQ[...], NT)
            grad_two = dot(GUP[s, at, :], WU[...], NT)
            out[0][at, :], out[1][at, :] = halves(result)
            unit, inv = unit_rows(s, at)
            for i_row, value in enumerate([grad_one * unit, grad_one, grad_two * unit, grad_two]):
                SMALL[2 + i_row : 3 + i_row, :] += jnp.sum(value, axis=0, keepdims=True)
            scaled = grad_one * params[0:1, :] + grad_two * params[2:3, :]
            mean_scaled = jnp.mean(scaled, axis=1, keepdims=True)
            mean_unit = jnp.mean(scaled * unit, axis=1, keepdims=True)
            slope[0][at, :], slope[1][at, :] = halves(inv * (scaled - mean_scaled - unit * mean_unit))
            if s == 0:
                SMALL[6:7, own_cols] += jnp.sum(G[0, at, own_cols].astype(F32), axis=0, keepdims=True)

    given = [ZU, SU]
    given_copies = []
    near = [X.at[1, :, pl.ds(0, half)], X.at[1, :, pl.ds(half, half)]]

    def leave_far(c):
        leave(1, c, (OUT.at[0], given[0]), (OUT.at[1], given[1]))
        for i in range(2):
            given_copies.append(net.send(("out", i, c), given[i].at[chunk(c), :], LAND.at[i, chunk(c), :], core))

    def pass_far(c):
        for i in range(2):
            net.wait(("out", i, c), LAND.at[i, chunk(c), :], core)
            LAND[i, chunk(c), :] = (LAND[i, chunk(c), :].astype(F32) + OUT[i, chunk(c), :].astype(F32)).astype(BF16)
            net.send(("far out", i, c), LAND.at[i, chunk(c), :], FAR.at[i, chunk(c), :], xdev)

    def leave_own(c):
        sides = [[buffer.at[0, :, pl.ds(h * half, half)] for h in range(2)] for buffer in (ACT, GUP)]
        leave(0, c, *sides)
        for i in range(2):
            net.send(("own out", i, c), sides[i][1].at[chunk(c), :], near[i].at[chunk(c), :], core)

    def add_up(i, c):
        buffer = (ACT, GUP)[i]
        net.wait(("own out", i, c), near[i].at[chunk(c), :], core)
        net.wait(("far out", i, c), FAR.at[i, chunk(c), :], xdev)
        total = buffer[0, chunk(c), pl.ds(0, half)].astype(F32) + near[i][chunk(c), :].astype(F32)
        FAR[i, chunk(c), :] = (total + FAR[i, chunk(c), :].astype(F32)).astype(BF16)
        return move(FAR.at[i, chunk(c), :], (sum_out, slope_out)[i].at[chunk(c), :])

    feed_part(1, 1)
    feed_part(1, 0)
    for copy in handed:
        net.sent(copy)
    leave_far(0)
    leave_far(1)
    pass_far(0)
    feed_part(0, 1)
    pass_far(1)
    other_part("d")
    for copy in given_copies:
        net.sent(copy)
    other_part("u")
    own_part("o")
    own_part("q")
    for name in "oq":
        for t in (2, 3):
            across(name, t)
    for h in range(2):
        sums = [jnp.sum(MIX[s, :, pl.ds(h * qc, qc)].astype(F32), axis=0, keepdims=True) for s in range(2)]
        SMALL[0:1, pl.ds(pl.multiple_of(seat_of(h, qc), LANES), qc)] = sums[0] + sums[1]
    feed_part(0, 0)
    own_part("d")
    for name in "oq":
        for t in (1, 0):
            across(name, t)
    own_part("u")
    across("d", 2)
    leave_own(0)
    across("d", 3)
    across("d", 1)
    leave_own(1)
    for t in range(1, R):
        net.send(("sz", t), SMALL, SMALL_Z.at[row], zdev(t))
    SMALL_Z[row] = SMALL[...]
    across("d", 0)
    done = [finish(name) for name in "oq"]
    across("u", 2)
    across("u", 3)
    done.append(finish("d"))

    for t in range(1, R):
        net.wait(("sz", t), SMALL_Z.at[lax.rem(row - t + R, R)], zdev(-t))
    total = SMALL_Z[0]
    for r in range(1, R):
        total = total + SMALL_Z[r]
    SMALL_P[0] = total
    net.send("sy", SMALL_P.at[0], SMALL_P.at[1], ydev)
    across("u", 1)
    done += [add_up(0, 0), add_up(0, 1)]
    across("u", 0)
    done.append(finish("u"))
    net.wait("sy", SMALL_P.at[1], ydev)
    SMALL_P[2] = SMALL_P[0] + SMALL_P[1]
    net.send("sx", SMALL_P.at[2], SMALL_P.at[3], xdev)
    for name in "oqud":
        spread_out(name)
    net.wait("sx", SMALL_P.at[3], xdev)
    SMALL_P[4] = SMALL_P[2] + SMALL_P[3]
    net.send("sc", SMALL_P.at[4], SMALL_P.at[5], core)
    done += [add_up(1, 0), add_up(1, 1)]
    net.wait("sc", SMALL_P.at[5], core)
    SMALL_P[5] = SMALL_P[4] + SMALL_P[5]

    def side_span(which, size):
        return pl.ds(pl.multiple_of(which * size, LANES), size)

    for i, which in [(2, side), (3, 1 - side)]:
        done += [
            move(SMALL_P.at[i, pl.ds(0, 1), pl.ds(0, 2 * qc)], bq_out.at[:, side_span(which, 2 * qc)]),
            move(SMALL_P.at[i, pl.ds(1, 1), pl.ds(0, 2 * uc)], bu_out.at[:, side_span(which, 2 * uc)]),
        ]
    done += [
        move(SMALL_P.at[5, pl.ds(2, 4), own_cols], gains_out),
        move(SMALL_P.at[4, pl.ds(6, 1), own_cols], cot_out),
    ]
    for name in "oqdu":
        collect(name)
    for copy in done:
        copy.wait()
    net.drain()


def whole_block(hidden, cot, wq, wo, wu, wd, *rest):
    length, half = hidden.shape
    width = 2 * half
    shard = wq.shape[0]
    wide3 = wq.shape[1] // 2
    wide = wide3 // 3
    units = wu.shape[1] // 2
    qc, oc, uc = wide3 // 2, wide // 2, units // 2
    out_shape = [
        jax.ShapeDtypeStruct(shape, kind)
        for shape, kind in [
            ((shard, 4 * qc), BF16), ((4 * oc, shard), BF16), ((shard, 4 * uc), BF16), ((4 * uc, shard), BF16),
            ((length, half), BF16), ((length, half), BF16),
            ((4, half), F32), ((1, 4 * qc), F32), ((1, 4 * uc), F32), ((1, half), F32),
        ]
    ]
    both = lambda n: pltpu.VMEM((2, length, n), BF16)
    plain = lambda *shape: pltpu.VMEM(shape, BF16)
    floats = lambda *shape: pltpu.VMEM(shape, F32)
    quarter_grads = [plain(width, qc), plain(oc, width), plain(width, uc), plain(uc, width)]
    scratch = [
        both(width), both(width), both(width), both(width), both(half),
        plain(width, wide3), plain(wide, width), plain(width, units), plain(units, width),
        both(wide3), both(wide), both(units), both(units),
        floats(8, length), floats(8, length), floats(8, width), floats(8, 4 * uc),
        *[floats(length, LANES)] * 5,
        *quarter_grads * 3,
        plain(3, shard, qc), plain(3, oc, shard), plain(3, shard, uc), plain(3, uc, shard),
        both(half), both(half), floats(8, width), floats(4, 8, width), floats(6, 8, width),
    ]
    any_spec = pl.BlockSpec(memory_space=pl.ANY)
    vmem_spec = pl.BlockSpec(memory_space=pltpu.VMEM)
    return pl.pallas_call(
        block_kernel,
        out_shape=out_shape,
        in_specs=[any_spec] * 6 + [vmem_spec] * len(rest),
        out_specs=[any_spec] * len(out_shape),
        scratch_shapes=scratch + [
            pltpu.SemaphoreType.DMA((128,)), pltpu.SemaphoreType.DMA((128,)), pltpu.SemaphoreType.DMA((32,)),
        ],
        compiler_params=pltpu.CompilerParams(collective_id=0, has_side_effects=True, vmem_limit_bytes=63 << 20),
        name="block",
    )(hidden, cot, wq, wo, wu, wd, *rest)


def widen_kernel(
    hidden, branch, cot, slope, grad_q, grad_o, grad_u, grad_d, bias_one, bias_two, gains, qkv_sum, up_sum, cot_sum,
    output, input_grad, out_q, out_o, out_u, out_d, *small,
):
    bias = (bias_one[...].astype(F32) + bias_two[...].astype(F32)).reshape(1, -1)
    output[...] = hidden[...].astype(F32) + branch[...].astype(F32) + bias
    input_grad[...] = cot[...].astype(F32) + slope[...].astype(F32)
    for source, target in [(grad_q, out_q), (grad_o, out_o), (grad_u, out_u), (grad_d, out_d)]:
        target[...] = source[...].astype(F32)
    for i in range(4):
        small[i][...] = gains[i, :]
    small[4][...] = qkv_sum[0, :]
    small[5][...] = up_sum[0, :]
    small[6][...] = cot_sum[0, :]
    small[7][...] = cot_sum[0, :]


def widen_all(hidden, branch, cot, slope, grad_q, grad_o, grad_u, grad_d, bias_one, bias_two, gains, *sums):
    steps = 8
    rows = lambda v: pl.BlockSpec((v.shape[0] // steps, v.shape[1]), lambda i: (i, 0))
    whole = lambda v: pl.BlockSpec(v.shape, lambda i: (0,) * v.ndim)
    large = [hidden, branch, cot, slope, grad_q, grad_o, grad_u, grad_d]
    tiny = [bias_one, bias_two, gains, *sums]
    wide = [hidden, cot, grad_q, grad_o, grad_u, grad_d]
    flat = [gains.shape[1]] * 4 + [v.shape[1] for v in sums] + [sums[-1].shape[1]]
    return pl.pallas_call(
        widen_kernel,
        grid=(steps,),
        in_specs=[rows(v) for v in large] + [whole(v) for v in tiny],
        out_specs=[rows(v) for v in wide] + [pl.BlockSpec((n,), lambda i: (0,)) for n in flat],
        out_shape=[jax.ShapeDtypeStruct(v.shape, F32) for v in wide] + [jax.ShapeDtypeStruct((n,), F32) for n in flat],
        compiler_params=pltpu.CompilerParams(vmem_limit_bytes=63 << 20),
        name="widen",
    )(*large, *tiny)


def local_block(
    hidden,
    segments,
    ln1_gain,
    ln1_bias,
    qkv_weight,
    qkv_bias,
    out_weight,
    out_bias,
    ln2_gain,
    ln2_bias,
    up_weight,
    up_bias,
    down_weight,
    down_bias,
    cotangent,
):
    lane = np.arange(LANES) % HEAD_DIM
    frequency = np.where(lane < ROT, 10000.0 ** (-2.0 * (lane % (ROT // 2)) / ROT), 0.0)
    sign = np.where(lane < ROT, np.where(lane < ROT // 2, -1.0, 1.0), 0.0)
    freq = np.stack([frequency, sign] * 4).astype(np.float32)
    flat = [ln1_gain, ln1_bias, ln2_gain, ln2_bias, qkv_bias, up_bias]
    grad_q, grad_o, grad_u, grad_d, branch, slope, gains, qkv_sum, up_sum, cot_sum = whole_block(
        hidden, cotangent, qkv_weight, out_weight, up_weight, down_weight, segments, jnp.asarray(freq), *flat
    )
    output, input_grad, grad_q, grad_o, grad_u, grad_d, *small = widen_all(
        hidden, branch, cotangent, slope, grad_q, grad_o, grad_u, grad_d,
        out_bias, down_bias, gains, qkv_sum, up_sum, cot_sum,
    )
    gain_one, shift_one, gain_two, shift_two, qkv_sum, up_sum, cot_sum, cot_again = small
    return (
        output, input_grad, gain_one, shift_one, grad_q, qkv_sum, grad_o, cot_sum,
        gain_two, shift_two, grad_u, up_sum, grad_d, cot_again,
    )


def normalize(values):
    centred = values - jnp.mean(values, axis=-1, keepdims=True)
    variance = jnp.mean(centred * centred, axis=-1, keepdims=True)
    inv_std = lax.rsqrt(variance + EPS)
    return centred * inv_std, inv_std


def make_general(groups, rows, cols):
    quarters = groups // 2

    def pair_swap(value):
        return lax.ppermute(value, "dp", [(d, d ^ 1) for d in range(groups)])

    def quarter_shift(value, shift):
        moves = [(2 * a + b, 2 * ((a + shift) % quarters) + b) for a in range(quarters) for b in range(2)]
        return lax.ppermute(value, "dp", moves)

    def row_shift(value, shift):
        return lax.ppermute(value, "row", [(r, (r + shift) % rows) for r in range(rows)])

    def core_swap(value):
        return lax.ppermute(value, "col", [(0, 1), (1, 0)])

    def local(
        hidden,
        segments,
        ln1_gain,
        ln1_bias,
        qkv_weight,
        qkv_bias,
        out_weight,
        out_bias,
        ln2_gain,
        ln2_bias,
        up_weight,
        up_bias,
        down_weight,
        down_bias,
        cotangent,
    ):
        assert segments.shape[0] == 1 and cols == 2
        length = segments.shape[1]
        half_width = hidden.shape[1]
        width = 2 * half_width
        shard = qkv_weight.shape[0]
        heads = qkv_weight.shape[1] // (3 * HEAD_DIM) // 2
        wide = heads * HEAD_DIM
        units = up_weight.shape[1] // 2
        whole_heads = heads % quarters == 0
        dp = lax.axis_index("dp")
        row = lax.axis_index("row")
        col = lax.axis_index("col")
        side = lax.rem(dp, 2)
        quarter = dp // 2

        def both(mine, other):
            flip = col == 0
            return jnp.concatenate([jnp.where(flip, mine, other), jnp.where(flip, other, mine)], axis=-1)

        def half_of(value, axis):
            size = value.shape[axis] // 2
            return lax.dynamic_slice_in_dim(value, side * size, size, axis)

        def piece_of(value, shift, axis, placed=False):
            size = value.shape[axis] // quarters
            if placed:
                return lax.slice_in_dim(value, shift * size, (shift + 1) * size, axis=axis)
            return lax.dynamic_slice_in_dim(value, lax.rem(quarter - shift + quarters, quarters) * size, size, axis)

        def in_place(pieces, axis):
            if quarters == 1:
                return pieces[0]
            if quarters == 2:
                flip = quarter == 0
                first = jnp.where(flip, pieces[0], pieces[1])
                second = jnp.where(flip, pieces[1], pieces[0])
                return jnp.concatenate([first, second], axis=axis)
            order = lax.rem(quarter - jnp.arange(quarters) + quarters, quarters)
            stacked = jnp.take(jnp.stack(pieces), order, axis=0)
            return jnp.concatenate([stacked[i] for i in range(quarters)], axis=axis)

        def near(pieces, axis, keep):
            return jnp.concatenate(pieces, axis=axis) if keep else in_place(pieces, axis)

        def gather(value, width_axis, unit_axis, keep):
            mine = piece_of(value, 0, unit_axis)
            received = {0: mine}
            ahead = behind = mine
            for step in range(1, rows):
                if step <= rows // 2:
                    ahead = row_shift(ahead, -1)
                    received[step] = ahead
                if step <= (rows - 1) // 2:
                    behind = row_shift(behind, 1)
                    received[rows - step] = behind
            result = jnp.zeros(
                [width if i == width_axis else n for i, n in enumerate(value.shape)], value.dtype
            )
            for step in range(rows):
                if step == 0:
                    pieces = [piece_of(value, q, unit_axis) for q in range(quarters)]
                else:
                    pieces = [received[step]]
                    pieces += [quarter_shift(received[step], q) for q in range(1, quarters)]
                block = near(pieces, unit_axis, keep)
                place = lax.rem(row + step, rows) * shard
                result = lax.dynamic_update_slice_in_dim(result, block, place, width_axis)
            return result

        hidden_other = core_swap(hidden)
        hidden_far = pair_swap(hidden)
        cot_other = core_swap(cotangent)
        cot_far = pair_swap(cotangent)
        params = jnp.stack([ln1_gain, ln1_bias, ln2_gain, ln2_bias])
        params = both(params, core_swap(params)).astype(F32)
        gain_one, shift_one, gain_two, shift_two = [params[i][None, :] for i in range(4)]
        inputs = [both(hidden, hidden_other), both(hidden_far, core_swap(hidden_far))]
        cots = [both(cotangent, cot_other), both(cot_far, core_swap(cot_far))]
        segs = [segments, pair_swap(segments)]

        qkv_cols = qkv_weight.reshape(shard, 2, heads, 3, HEAD_DIM)
        qkv_cols = lax.dynamic_index_in_dim(qkv_cols, side, 1, keepdims=False)
        qkv_cols = jnp.swapaxes(qkv_cols, 1, 2).reshape(shard, 3, wide)
        qkv_all = gather(qkv_cols, 0, 2, whole_heads).reshape(width, 3 * wide)
        out_all = gather(half_of(out_weight, 0), 1, 0, whole_heads)
        up_all = gather(half_of(up_weight, 1), 0, 1, True)
        down_all = gather(half_of(down_weight, 0), 1, 0, True)

        bias_cols = lax.dynamic_index_in_dim(qkv_bias.reshape(2, heads, 3, HEAD_DIM), side, 0, keepdims=False)
        bias_cols = jnp.swapaxes(bias_cols, 0, 1).reshape(1, 3, wide)
        bias_cols = near([piece_of(bias_cols, q, 2) for q in range(quarters)], 2, whole_heads)
        bias_cols = bias_cols.reshape(1, 3 * wide).astype(F32)
        up_half = half_of(up_bias, 0)
        up_row = jnp.concatenate([piece_of(up_half, q, 0) for q in range(quarters)])[None, :].astype(F32)

        norms = []
        contexts = []
        grads_mixed = []
        for values, cot, seg in zip(inputs, cots, segs):
            unit, inv = normalize(values.astype(F32))
            act_one = (unit * gain_one + shift_one).astype(BF16)
            act_two = (unit * gain_two + shift_two).astype(BF16)
            norms.append((unit, inv, act_one, act_two))
            cos_rows, sine_rows = rotary_tables(doc_positions(seg).reshape(length))
            mixed = dot(act_one, qkv_all) + bias_cols
            cos_wide = jnp.tile(cos_rows, (1, 2 * wide // LANES))
            sine_wide = jnp.tile(sine_rows, (1, 2 * wide // LANES))
            turned = mixed[:, : 2 * wide]
            lane = jnp.arange(2 * wide) % HEAD_DIM
            swapped = jnp.where(
                lane < ROT // 2, jnp.roll(turned, -(ROT // 2), axis=1), jnp.roll(turned, ROT // 2, axis=1)
            )
            turned = turned * cos_wide + swapped * sine_wide
            qkv = jnp.concatenate([turned, mixed[:, 2 * wide :]], axis=1).astype(BF16)
            grad_context = dot(cot, out_all, NT).astype(BF16)
            context, grad_mixed = attention(qkv, grad_context, seg, cos_rows, sine_rows)
            contexts.append(context)
            grads_mixed.append(grad_mixed)

        feeds = [feed(norm[3], cot, up_all, up_row, down_all) for norm, cot in zip(norms, cots)]

        def reduce_grad(left, right, width_axis, unit_axis, placed, shape=None):
            total = dot(left[0], right[0], TN) + dot(left[1], right[1], TN)
            if shape is not None:
                total = total.reshape(shape)
            mine = piece_of(total, 0, unit_axis, placed)
            for q in range(1, quarters):
                part = piece_of(total, q, unit_axis, placed).astype(BF16)
                mine = mine + quarter_shift(part, -q).astype(F32)
            cut = lambda t: lax.dynamic_slice_in_dim(mine, lax.rem(row + t, rows) * shard, shard, width_axis)
            result = cut(0)
            for t in range(1, rows):
                result = result + row_shift(cut(t).astype(BF16), t).astype(F32)
            result = result.astype(BF16)
            pieces = [result] + [quarter_shift(result, q) for q in range(1, quarters)]
            result = in_place(pieces, unit_axis)
            far = pair_swap(result)
            flip = side == 0
            return jnp.concatenate(
                [jnp.where(flip, result, far), jnp.where(flip, far, result)], axis=unit_axis
            ).astype(F32)

        acts_one = [n[2] for n in norms]
        acts_two = [n[3] for n in norms]
        out_grad = reduce_grad(contexts, cots, 1, 0, whole_heads)
        qkv_grad = reduce_grad(acts_one, grads_mixed, 0, 2, whole_heads, (width, 3, wide))
        down_grad = reduce_grad([f[0] for f in feeds], cots, 1, 0, True)
        up_grad = reduce_grad(acts_two, [f[1] for f in feeds], 0, 1, True)
        qkv_grad = qkv_grad.reshape(shard, 3, 2 * heads, HEAD_DIM)
        qkv_grad = jnp.swapaxes(qkv_grad, 1, 2).reshape(shard, 6 * wide)

        outs = []
        slopes = []
        norm_sums = jnp.zeros((4, width), F32)
        for index in range(2):
            unit, inv, _, _ = norms[index]
            act, grad_up, _ = feeds[index]
            outs.append((dot(contexts[index], out_all) + dot(act, down_all)).astype(BF16))
            grad_one = dot(grads_mixed[index], qkv_all, NT)
            grad_two = dot(grad_up, up_all, NT)
            norm_sums += jnp.stack(
                [
                    jnp.sum(grad_one * unit, axis=0),
                    jnp.sum(grad_one, axis=0),
                    jnp.sum(grad_two * unit, axis=0),
                    jnp.sum(grad_two, axis=0),
                ]
            )
            scaled = grad_one * gain_one + grad_two * gain_two
            mean_scaled = jnp.mean(scaled, axis=1, keepdims=True)
            mean_unit = jnp.mean(scaled * unit, axis=1, keepdims=True)
            slopes.append((inv * (scaled - mean_scaled - unit * mean_unit)).astype(BF16))

        def fold(pair):
            sums = []
            for value in pair:
                kept = lax.dynamic_slice_in_dim(value, col * half_width, half_width, 1).astype(F32)
                given = lax.dynamic_slice_in_dim(value, (1 - col) * half_width, half_width, 1)
                sums.append(kept + core_swap(given).astype(F32))
            return sums[0] + pair_swap(sums[1].astype(BF16)).astype(F32)

        cot_local = cotangent.astype(F32)
        output = hidden.astype(F32) + fold(outs) + (out_bias.astype(F32) + down_bias.astype(F32))
        input_grad = cot_local + fold(slopes)

        qkv_sum = (
            jnp.sum(grads_mixed[0].astype(F32), axis=0) + jnp.sum(grads_mixed[1].astype(F32), axis=0)
        ).reshape(3, wide)
        if whole_heads:
            qkv_sum = in_place([piece_of(qkv_sum, q, 1, True) for q in range(quarters)], 1)
        up_sum = (feeds[0][2] + feeds[1][2])[0]
        up_sum = in_place([piece_of(up_sum, q, 0, True) for q in range(quarters)], 0)

        def widen(value):
            zeros = jnp.zeros_like(value)
            flip = side == 0
            return jnp.concatenate([jnp.where(flip, value, zeros), jnp.where(flip, zeros, value)], axis=-1)

        kept = lax.dynamic_slice_in_dim(norm_sums, col * half_width, half_width, 1)
        given = lax.dynamic_slice_in_dim(norm_sums, (1 - col) * half_width, half_width, 1)
        norm_sums = kept + core_swap(given)
        small = jnp.concatenate(
            [widen(qkv_sum).reshape(-1), widen(up_sum), jnp.sum(cot_local, axis=0), norm_sums.reshape(-1)]
        )
        small = lax.psum(small, ("dp", "row"))
        sizes = [6 * wide, 2 * units, half_width, half_width, half_width, half_width, half_width]
        parts = []
        start = 0
        for size in sizes:
            parts.append(lax.slice_in_dim(small, start, start + size))
            start += size
        qkv_sum, up_sum, cot_sum, gain_one_sum, shift_one_sum, gain_two_sum, shift_two_sum = parts
        qkv_sum = jnp.swapaxes(qkv_sum.reshape(3, 2 * heads, HEAD_DIM), 0, 1).reshape(-1)
        return (
            output,
            input_grad,
            gain_one_sum,
            shift_one_sum,
            qkv_grad,
            qkv_sum,
            out_grad,
            cot_sum,
            gain_two_sum,
            shift_two_sum,
            up_grad,
            up_sum,
            down_grad,
            cot_sum,
        )

    return local


def solution(mesh):
    placed = (
        P(("dp", "row"), "col"),
        P(("dp", "row"), None),
        P("col"),
        P("col"),
        P("row", "col"),
        P("col"),
        P("col", "row"),
        P("col"),
        P("col"),
        P("col"),
        P("row", "col"),
        P("col"),
        P("col", "row"),
        P("col"),
        P(("dp", "row"), "col"),
    )
    groups, rows, cols = mesh.shape["dp"], mesh.shape["row"], mesh.shape["col"]
    paired = (groups, rows, cols) == (4, 4, 2)
    return jax.shard_map(
        local_block if paired else make_general(groups, rows, cols),
        mesh=mesh,
        in_specs=placed,
        out_specs=(
            P(("dp", "row"), "col"),
            P(("dp", "row"), "col"),
            P("col"),
            P("col"),
            P("row", "col"),
            P("col"),
            P("col", "row"),
            P("col"),
            P("col"),
            P("col"),
            P("row", "col"),
            P("col"),
            P("col", "row"),
            P("col"),
        ),
        check_vma=False,
    )
```

```python
import functools

import jax
import jax.numpy as jnp
import numpy as np
from jax import lax
from jax.experimental import pallas as pl
from jax.experimental.pallas import tpu as pltpu
from jax.sharding import PartitionSpec as P

HEAD_DIM = 64
ROT = 16
EPS = 1e-05
MAX_DOC = 512
DOCS = 4
LANES = 128
BF16 = jnp.bfloat16
F32 = jnp.float32

NT = (((1,), (1,)), ((), ()))
TN = (((0,), (0,)), ((), ()))
NN = (((1,), (0,)), ((), ()))


def dot(a, b, dims=NN):
    return lax.dot_general(a, b, dims, preferred_element_type=F32)


def doc_positions(segments):
    length = segments.shape[-1]
    places = jnp.arange(length, dtype=jnp.int32)
    changed = jnp.concatenate(
        [jnp.ones(segments.shape[:-1] + (1,), dtype=bool), segments[..., 1:] != segments[..., :-1]],
        axis=-1,
    )
    starts = lax.cummax(jnp.where(changed, places, jnp.zeros_like(places)), axis=segments.ndim - 1)
    return places - starts


def rotary_tables(positions):
    lane = jnp.arange(LANES) % HEAD_DIM
    frequency = 10000.0 ** (-2.0 * (lane % (ROT // 2)).astype(F32) / ROT)
    turning = lane < ROT
    angles = positions.astype(F32)[:, None] * jnp.where(turning, frequency, 0.0)[None, :]
    sign = jnp.where(turning, jnp.where(lane < ROT // 2, -1.0, 1.0), 0.0)
    return jnp.cos(angles), jnp.sin(angles) * sign[None, :]


def turn(values, cos_rows, sine_rows, low_lanes):
    half = ROT // 2
    up = pltpu.roll(values, values.shape[1] - half, 1)
    down = pltpu.roll(values, half, 1)
    return values * cos_rows + jnp.where(low_lanes, up, down) * sine_rows


def attention_kernel(
    q_ref, k_ref, v_ref, gc_ref, seg_row_ref, seg_col_ref, cos_ref, sin_ref, ctx_ref, gm_ref, dk_acc, dv_acc, *, block
):
    pair = pl.program_id(0)
    pairs = pl.num_programs(0)
    length = q_ref.shape[0]
    lane = lax.broadcasted_iota(jnp.int32, (1, LANES), 1)
    low_lanes = lane % HEAD_DIM < ROT // 2
    first = lane < HEAD_DIM
    zero = jnp.zeros((), BF16)

    def split(values):
        return [jnp.where(first, values, zero), jnp.where(first, zero, values)]

    dk_acc[...] = jnp.zeros_like(dk_acc)
    dv_acc[...] = jnp.zeros_like(dv_acc)
    for begin in range(0, length, block):
        low = max(0, begin - (MAX_DOC - 1)) // LANES * LANES
        rows = pl.ds(begin, block)
        keys = pl.ds(low, begin + block - low)
        width = begin + block - low
        q_parts = split(q_ref[rows, :] * jnp.asarray(HEAD_DIM**-0.5, BF16))
        g_parts = split(gc_ref[rows, :])
        k_block = k_ref[keys, :]
        v_block = v_ref[keys, :]
        places = begin + lax.broadcasted_iota(jnp.int32, (block, width), 0)
        key_places = low + lax.broadcasted_iota(jnp.int32, (block, width), 1)
        allowed = (seg_col_ref[rows, :] == seg_row_ref[:, keys]) & (places >= key_places)
        probs = []
        grads = []
        for part in range(2):
            scores = dot(q_parts[part], k_block, NT)
            scores = jnp.where(allowed, scores, -1e30)
            top = jnp.max(scores, axis=1, keepdims=True)
            powers = jnp.exp(scores - top)
            total = jnp.sum(powers, axis=1, keepdims=True)
            chances = powers * (1.0 / total)
            slopes = dot(g_parts[part], v_block, NT)
            inner = jnp.sum(slopes * chances, axis=1, keepdims=True)
            probs.append(chances.astype(BF16))
            grads.append((chances * (slopes - inner)).astype(BF16))
        context = jnp.where(first, dot(probs[0], v_block), dot(probs[1], v_block))
        ctx_ref[rows, :] = context.astype(BF16)
        dq = jnp.where(first, dot(grads[0], k_block), dot(grads[1], k_block)) * HEAD_DIM**-0.5
        dq = turn(dq, cos_ref[rows, :], -sin_ref[rows, :], low_lanes)
        gm_ref[rows, pl.ds(pl.multiple_of(pair * LANES, LANES), LANES)] = dq.astype(BF16)
        dk_acc[keys, :] += dot(grads[0], q_parts[0], TN) + dot(grads[1], q_parts[1], TN)
        dv_acc[keys, :] += dot(probs[0], g_parts[0], TN) + dot(probs[1], g_parts[1], TN)
    dk = turn(dk_acc[...], cos_ref[...], -sin_ref[...], low_lanes)
    gm_ref[:, pl.ds(pl.multiple_of((pairs + pair) * LANES, LANES), LANES)] = dk.astype(BF16)
    gm_ref[:, pl.ds(pl.multiple_of((2 * pairs + pair) * LANES, LANES), LANES)] = dv_acc[...].astype(BF16)


def attention(qkv, grad_context, seg_row, cos_rows, sine_rows):
    length, wide = qkv.shape
    pairs = wide // (3 * LANES)
    block = min(256, length)
    column = lambda shift: pl.BlockSpec((length, LANES), lambda p: (0, shift + p))
    whole = lambda *shape: pl.BlockSpec(shape, lambda p: (0, 0))
    flops = pairs * 2 * 6 * 2 * length * length * LANES // 2
    return pl.pallas_call(
        functools.partial(attention_kernel, block=block),
        grid=(pairs,),
        in_specs=[
            column(0),
            column(pairs),
            column(2 * pairs),
            column(0),
            whole(1, length),
            whole(length, 1),
            whole(length, LANES),
            whole(length, LANES),
        ],
        out_specs=[column(0), whole(length, wide)],
        out_shape=[
            jax.ShapeDtypeStruct((length, pairs * LANES), BF16),
            jax.ShapeDtypeStruct((length, wide), BF16),
        ],
        scratch_shapes=[pltpu.VMEM((length, LANES), F32), pltpu.VMEM((length, LANES), F32)],
        compiler_params=pltpu.CompilerParams(vmem_limit_bytes=48 << 20),
        cost_estimate=pl.CostEstimate(
            flops=flops, bytes_accessed=6 * length * wide, transcendentals=pairs * length * length
        ),
        name="attention",
    )(qkv, qkv, qkv, grad_context, seg_row, seg_row.reshape(length, 1), cos_rows, sine_rows)


def feed_kernel(a_ref, g_ref, up_ref, bias_ref, down_ref, act_ref, gup_ref, sum_ref, *, chunk):
    units = up_ref.shape[1]

    @pl.when(pl.program_id(0) == 0)
    def _():
        sum_ref[...] = jnp.zeros_like(sum_ref)

    for begin in range(0, units, chunk):
        cols = pl.ds(begin, chunk)
        up = dot(a_ref[...], up_ref[:, cols]) + bias_ref[:, cols]
        pull = dot(g_ref[...], down_ref[cols, :], NT)
        gate = 0.5 * (1.0 + lax.erf(up * 0.5**0.5))
        bell = jnp.exp(-0.5 * up * up) * 0.3989422804014327
        act_ref[:, cols] = (up * gate).astype(BF16)
        grad = (pull * (gate + up * bell)).astype(BF16)
        gup_ref[:, cols] = grad
        sum_ref[:, cols] += jnp.sum(grad.astype(F32), axis=0, keepdims=True)


def feed(normed, cot, up_weight, up_bias, down_weight):
    tokens, width = normed.shape
    units = up_weight.shape[1]
    block = min(256, tokens)
    rows = lambda size: pl.BlockSpec((block, size), lambda i: (i, 0))
    whole = lambda *shape: pl.BlockSpec(shape, lambda i: (0, 0))
    return pl.pallas_call(
        functools.partial(feed_kernel, chunk=min(256, units)),
        grid=(tokens // block,),
        in_specs=[rows(width), rows(width), whole(width, units), whole(1, units), whole(units, width)],
        out_specs=[rows(units), rows(units), whole(1, units)],
        out_shape=[
            jax.ShapeDtypeStruct((tokens, units), BF16),
            jax.ShapeDtypeStruct((tokens, units), BF16),
            jax.ShapeDtypeStruct((1, units), F32),
        ],
        compiler_params=pltpu.CompilerParams(vmem_limit_bytes=48 << 20),
        cost_estimate=pl.CostEstimate(
            flops=4 * tokens * width * units,
            bytes_accessed=4 * tokens * width + 4 * width * units + 4 * tokens * units,
            transcendentals=2 * tokens * units,
        ),
        name="feed",
    )(normed, cot, up_weight, up_bias, down_weight)


MESH = pl.DeviceIdType.MESH


class Net:
    def __init__(self, send_sems, recv_sems):
        self.send_sems, self.recv_sems = send_sems, recv_sems
        self.slots = {}
        self.pending = []

    def slot(self, key):
        return self.slots.setdefault(key, len(self.slots))

    def make(self, key, source, target, device):
        i = self.slot(key)
        return pltpu.make_async_remote_copy(
            src_ref=source,
            dst_ref=target,
            send_sem=self.send_sems.at[i],
            recv_sem=self.recv_sems.at[i],
            device_id=device,
            device_id_type=MESH,
        )

    def send(self, key, source, target, device):
        copy = self.make(key, source, target, device)
        copy.start()
        self.pending.append(copy)
        return copy

    def sent(self, copy):
        copy.wait_send()
        self.pending = [other for other in self.pending if other is not copy]

    def wait(self, key, landed, device):
        self.make(key, landed, landed, device).wait_recv()

    def drain(self):
        for copy in self.pending:
            copy.wait_send()
        self.pending = []


def spread(columns, width):
    return jnp.concatenate([columns] * (width // LANES), axis=1)


def attend_pair(mix, base, gc, gc_base, ctx, seg_row, seg_col, cos_tab, sin_tab, dk_acc, dv_acc, block):
    length = mix.shape[0]
    lane = lax.broadcasted_iota(jnp.int32, (1, LANES), 1)
    low_lanes = lane % HEAD_DIM < ROT // 2
    first = lane < HEAD_DIM
    zero = jnp.zeros((), BF16)
    cols = [pl.ds(base + i * LANES, LANES) for i in range(3)]
    head_cols = pl.ds(gc_base, LANES)

    def split(values):
        return [jnp.where(first, values, zero), jnp.where(first, zero, values)]

    dk_acc[...] = jnp.zeros_like(dk_acc)
    dv_acc[...] = jnp.zeros_like(dv_acc)
    for begin in range(0, length, block):
        low = max(0, begin - (MAX_DOC - 1)) // LANES * LANES
        width = begin + block - low
        rows = pl.ds(begin, block)
        keys = pl.ds(low, width)
        q_parts = split(mix[rows, cols[0]] * jnp.asarray(HEAD_DIM**-0.5, BF16))
        g_parts = split(gc[rows, head_cols])
        k_block = mix[keys, cols[1]]
        v_block = mix[keys, cols[2]]
        places = begin + lax.broadcasted_iota(jnp.int32, (block, width), 0)
        key_places = low + lax.broadcasted_iota(jnp.int32, (block, width), 1)
        allowed = (spread(seg_col[rows, :], width) == seg_row[0:1, keys]) & (places >= key_places)
        probs = []
        grads = []
        for part in range(2):
            scores = dot(q_parts[part], k_block, NT)
            scores = jnp.where(allowed, scores, -1e30)
            top = jnp.max(scores, axis=1, keepdims=True)
            powers = jnp.exp(scores - top)
            total = jnp.sum(powers, axis=1, keepdims=True)
            chances = powers * (1.0 / total)
            slopes = dot(g_parts[part], v_block, NT)
            inner = jnp.sum(slopes * chances, axis=1, keepdims=True)
            probs.append(chances.astype(BF16))
            grads.append((chances * (slopes - inner)).astype(BF16))
        ctx[rows, head_cols] = jnp.where(first, dot(probs[0], v_block), dot(probs[1], v_block)).astype(BF16)
        dq = jnp.where(first, dot(grads[0], k_block), dot(grads[1], k_block)) * HEAD_DIM**-0.5
        mix[rows, cols[0]] = turn(dq, cos_tab[rows, :], -sin_tab[rows, :], low_lanes).astype(BF16)
        dk_acc[keys, :] += dot(grads[0], q_parts[0], TN) + dot(grads[1], q_parts[1], TN)
        dv_acc[keys, :] += dot(probs[0], g_parts[0], TN) + dot(probs[1], g_parts[1], TN)
    dq = mix[:, cols[0]].astype(F32)
    dk = pltpu.roll(turn(dk_acc[...], cos_tab[...], -sin_tab[...], low_lanes), HEAD_DIM, 1)
    dv = dv_acc[...]
    mix[:, cols[0]] = jnp.where(first, dq, dk).astype(BF16)
    mix[:, cols[1]] = jnp.where(first, dv, dq).astype(BF16)
    mix[:, cols[2]] = jnp.where(first, dk, dv).astype(BF16)


def block_kernel(
    hidden, cot, wq_in, wo_in, wu_in, wd_in,
    segments_in, freq_in, gain_one_in, shift_one_in, gain_two_in, shift_two_in, bq_in, bu_in,
    rq_out, ro_out, ru_out, rd_out, sum_out, slope_out, gains_out, bq_out, bu_out, cot_out,
    X, G, A, B, OUT, WQ, WO, WU, WD, MIX, CTX, ACT, GUP, rows_own, rows_far, params, biases, seg_col, cos_tab, sin_tab,
    dk_acc, dv_acc, SQ, SO, SU, SD, YQ, YO, YU, YD, ZQ, ZO, ZU, ZD, HQ, HO, HU, HD, LAND, FAR, SMALL, SMALL_Z, SMALL_P,
    send_sems, recv_sems, local_sems,
):
    R = 4
    dp, row, col = lax.axis_index("dp"), lax.axis_index("row"), lax.axis_index("col")
    side, quarter = lax.rem(dp, 2), lax.div(dp, 2)
    length, half = hidden.shape
    shard = wq_in.shape[0]
    core = (dp, row, 1 - col)
    xdev = (dp + 1 - 2 * side, row, col)
    ydev = (side + 2 * (1 - quarter), row, col)

    def zdev(t):
        return (dp, lax.rem(row + t + R, R), col)

    barrier = pltpu.get_barrier_semaphore()
    peers = [core, xdev, ydev] + [zdev(t) for t in range(1, R)]
    for peer in peers:
        pl.semaphore_signal(barrier, inc=1, device_id=peer, device_id_type=MESH)
    pl.semaphore_wait(barrier, len(peers))

    net = Net(send_sems, recv_sems)
    own_cols = pl.ds(pl.multiple_of(col * half, half), half)
    far_cols = pl.ds(pl.multiple_of((1 - col) * half, half), half)
    local = []

    def move(source, target):
        copy = pltpu.make_async_copy(source, target, local_sems.at[len(local)])
        copy.start()
        local.append(copy)
        return copy

    qc = WQ.shape[1] // 2
    oc = WO.shape[0] // 2
    uc = WU.shape[1] // 2

    def seat(h, size):
        return pl.ds(pl.multiple_of((side * 2 + (quarter if h == 0 else 1 - quarter)) * size, size), size)

    def block(t):
        return pl.ds(pl.multiple_of(lax.rem(row + t + R, R) * shard, shard), shard)

    every = slice(None)
    weights = {
        "q": (lambda h: wq_in.at[:, seat(h, qc)], lambda t, h: WQ.at[block(t), pl.ds(h * qc, qc)]),
        "o": (lambda h: wo_in.at[seat(h, oc), :], lambda t, h: WO.at[pl.ds(h * oc, oc), block(t)]),
        "u": (lambda h: wu_in.at[:, seat(h, uc)], lambda t, h: WU.at[block(t), pl.ds(h * uc, uc)]),
        "d": (lambda h: wd_in.at[seat(h, uc), :], lambda t, h: WD.at[pl.ds(h * uc, uc), block(t)]),
    }
    here_w = {}

    def start_along(name):
        here, place = weights[name]
        net.send((name, 1), here(0), place(0, 0), zdev(-1))
        net.send((name, 3), here(0), place(0, 0), zdev(1))

    def start_here(name):
        here, place = weights[name]
        here_w[name] = [move(here(h), place(0, h)) for h in range(2)]

    def along(name, t):
        place = weights[name][1]
        net.wait((name, t), place(t, 0), zdev(t))
        if t == 1:
            net.send((name, 2), place(t, 0), place(t, 0), zdev(-1))
        net.send((name, t, "y"), place(t, 0), place(t, 1), ydev)

    def across_y(name):
        place = weights[name][1]
        for t in (1, 3, 2):
            net.wait((name, t, "y"), place(t, 1), ydev)

    def have_here(name):
        for copy in here_w[name]:
            copy.wait()

    chunks = 2
    piece = length // chunks

    def chunk(c):
        return pl.ds(c * piece, piece)

    handed = []

    def hand_over(name, buffer, c):
        net.wait(("x " + name, c), buffer.at[1, chunk(c), own_cols], xdev)
        spot = buffer.at[1, chunk(c), own_cols]
        handed.append(net.send(("far " + name, c), spot, spot, core))

    def have_far(name, buffer):
        for c in range(chunks):
            net.wait(("far " + name, c), buffer.at[1, chunk(c), far_cols], core)

    start_along("q")
    net.send("core h", hidden, X.at[0, :, own_cols], core)
    start_along("o")
    here_h = move(hidden, X.at[0, :, own_cols])
    lane = lax.broadcasted_iota(jnp.int32, (1, LANES), 1)
    low_lanes = lane % HEAD_DIM < ROT // 2
    first = lane < HEAD_DIM

    seg = segments_in[...]
    start = jnp.zeros_like(seg)
    for number in range(1, DOCS):
        count = jnp.sum((seg < number).astype(jnp.int32), axis=1, keepdims=True)
        start = jnp.where(seg == number, count, start)
    rows_own[0:1, :] = seg.astype(F32)
    rows_own[1:2, :] = (lax.broadcasted_iota(jnp.int32, seg.shape, 1) - start).astype(F32)
    for i, source in enumerate([gain_one_in, shift_one_in, gain_two_in, shift_two_in]):
        params[i : i + 1, own_cols] = source[...].astype(F32).reshape(1, half)
    biases[0:1, pl.ds(0, bq_in.shape[0])] = bq_in[...].astype(F32).reshape(1, -1)
    biases[1:2, :] = bu_in[...].astype(F32).reshape(1, -1)
    net.send("core p", params.at[:, own_cols], params.at[:, own_cols], core)
    net.send("x rows", rows_own, rows_far, xdev)
    for c in range(chunks):
        net.send(("x h", c), hidden.at[chunk(c), :], X.at[1, chunk(c), own_cols], xdev)
    for c in range(chunks):
        net.send(("x g", c), cot.at[chunk(c), :], G.at[1, chunk(c), own_cols], xdev)
    net.send("core g", cot, G.at[0, :, own_cols], core)
    start_here("q")
    start_here("o")
    here_g = move(cot, G.at[0, :, own_cols])
    start_here("u")
    start_here("d")

    tile = 256
    GC = ACT.at[0]

    def each_tile(body):
        @pl.loop(0, length // tile, unroll=2)
        def _(i):
            body(pl.ds(pl.multiple_of(i * tile, tile), tile))

    def unit_rows(s, at):
        values = X[s, at, :].astype(F32)
        centred = values - jnp.mean(values, axis=-1, keepdims=True)
        inv = lax.rsqrt(jnp.mean(centred * centred, axis=-1, keepdims=True) + EPS)
        return centred * inv, inv

    def norm(s, at):
        unit, _ = unit_rows(s, at)
        A[s, at, :] = (unit * params[0:1, :] + params[1:2, :]).astype(BF16)
        B[s, at, :] = (unit * params[2:3, :] + params[3:4, :]).astype(BF16)

    def tables(rows):
        seg_col[...] = jnp.transpose(jnp.broadcast_to(rows[0:1, :], (LANES, length)))
        angles = jnp.transpose(jnp.broadcast_to(rows[1:2, :], (LANES, length))) * freq_in[0:1, :]
        cos_tab[...] = jnp.cos(angles)
        sin_tab[...] = jnp.sin(angles) * freq_in[1:2, :]

    def project(s, halves_in):
        low, high = halves_in[0] * qc, (halves_in[-1] + 1) * qc

        def body(at):
            product = dot(A[s, at, :], WQ[:, pl.ds(low, high - low)])
            cos_rows, sin_rows = cos_tab[at, :], sin_tab[at, :]
            for h in halves_in:
                mixed = product[:, h * qc - low : (h + 1) * qc - low] + biases[0:1, seat(h, qc)]
                t0, t1, t2 = [mixed[:, i * LANES : (i + 1) * LANES] for i in range(3)]
                query = jnp.where(first, t0, t1)
                key = pltpu.roll(jnp.where(first, t2, t0), HEAD_DIM, 1)
                value = jnp.where(first, t1, t2)
                MIX[s, at, pl.ds(h * qc, LANES)] = turn(query, cos_rows, sin_rows, low_lanes).astype(BF16)
                MIX[s, at, pl.ds(h * qc + LANES, LANES)] = turn(key, cos_rows, sin_rows, low_lanes).astype(BF16)
                MIX[s, at, pl.ds(h * qc + 2 * LANES, LANES)] = value.astype(BF16)

        each_tile(body)

    def pull_context(s, halves_in):
        low, high = halves_in[0] * oc, (halves_in[-1] + 1) * oc

        def body(at):
            GC[at, pl.ds(low, high - low)] = dot(G[s, at, :], WO[pl.ds(low, high - low), :], NT).astype(BF16)

        each_tile(body)

    def attend(s, rows, h):
        attend_pair(
            MIX.at[s], h * qc, GC, h * oc, CTX.at[s], rows, seg_col, cos_tab, sin_tab, dk_acc, dv_acc, tile
        )

    tables(rows_own)
    here_h.wait()
    net.wait("core h", X.at[0, :, far_cols], core)
    net.wait("core p", params.at[:, far_cols], core)
    along("q", 1)
    each_tile(lambda at: norm(0, at))
    along("q", 3)
    along("o", 1)
    along("o", 3)
    start_along("u")
    start_along("d")
    along("q", 2)
    have_here("q")
    project(0, (0,))
    along("o", 2)
    have_here("o")
    here_g.wait()
    net.wait("core g", G.at[0, :, far_cols], core)
    pull_context(0, (0,))
    hand_over("h", X, 0)
    attend(0, rows_own, 0)
    along("u", 1)
    across_y("q")
    project(0, (1,))
    across_y("o")
    pull_context(0, (1,))
    hand_over("h", X, 1)
    attend(0, rows_own, 1)
    along("u", 3)
    net.wait("x rows", rows_far, xdev)
    tables(rows_far)
    have_far("h", X)
    each_tile(lambda at: norm(1, at))
    along("d", 1)
    hand_over("g", G, 0)
    project(1, (0, 1))
    along("d", 3)
    along("u", 2)
    hand_over("g", G, 1)
    have_far("g", G)
    pull_context(1, (0, 1))
    attend(1, rows_far, 0)
    along("d", 2)
    attend(1, rows_far, 1)

    grads = {
        "q": (SQ, YQ, ZQ, HQ, rq_out, lambda t: (block(t), every), lambda p: (every, p), qc),
        "o": (SO, YO, ZO, HO, ro_out, lambda t: (every, block(t)), lambda p: (p, every), oc),
        "u": (SU, YU, ZU, HU, ru_out, lambda t: (block(t), every), lambda p: (every, p), uc),
        "d": (SD, YD, ZD, HD, rd_out, lambda t: (every, block(t)), lambda p: (p, every), uc),
    }

    def multiply(name, h, t):
        if name == "q":
            pairs_of = [(A[s, :, block(t)], MIX[s, :, pl.ds(h * qc, qc)]) for s in range(2)]
        elif name == "u":
            pairs_of = [(B[s, :, block(t)], GUP[s, :, pl.ds(h * uc, uc)]) for s in range(2)]
        elif name == "o":
            pairs_of = [(CTX[s, :, pl.ds(h * oc, oc)], G[s, :, block(t)]) for s in range(2)]
        else:
            pairs_of = [(ACT[s, :, pl.ds(h * uc, uc)], G[s, :, block(t)]) for s in range(2)]
        return (dot(*pairs_of[0], TN) + dot(*pairs_of[1], TN)).astype(BF16)

    turns = (2, 3, 1, 0)

    def other_part(name):
        source, landed, spot = grads[name][0], grads[name][1], grads[name][5]
        for t in turns:
            source[spot(t)] = multiply(name, 1, t)
            net.send(("gy", name, t), source.at[spot(t)], landed.at[spot(t)], ydev)

    def own_part(name):
        kept, spot = grads[name][2], grads[name][5]

        @pl.loop(0, R, unroll=2)
        def _(t):
            kept[spot(t)] = multiply(name, 0, t)

    def across(name, t):
        _, landed, kept, hops, _, spot, _, _ = grads[name]
        net.wait(("gy", name, t), landed.at[spot(t)], ydev)
        total = kept[spot(t)].astype(F32) + landed[spot(t)].astype(F32)
        if t == 1:
            net.wait(("gz", name, 2), hops.at[0], zdev(-1))
            total = total + hops[0].astype(F32)
        kept[spot(t)] = total.astype(BF16)
        if t == 2:
            net.send(("gz", name, 2), kept.at[spot(t)], hops.at[0], zdev(1))
        elif t == 3:
            net.send(("gz", name, 3), kept.at[spot(t)], hops.at[1], zdev(-1))
        elif t == 1:
            net.send(("gz", name, 1), kept.at[spot(t)], hops.at[2], zdev(1))

    def finish(name):
        _, _, kept, hops, result, spot, place, size = grads[name]
        net.wait(("gz", name, 3), hops.at[1], zdev(1))
        net.wait(("gz", name, 1), hops.at[2], zdev(-1))
        total = kept[spot(0)].astype(F32) + hops[1].astype(F32) + hops[2].astype(F32)
        kept[spot(0)] = total.astype(BF16)
        target = result.at[place(seat(0, size))]
        net.send(("ry", name), kept.at[spot(0)], target, ydev)
        net.send(("rx", name), kept.at[spot(0)], target, xdev)
        return move(kept.at[spot(0)], target)

    def far_seat(h, size):
        return pl.ds(pl.multiple_of(((1 - side) * 2 + (quarter if h == 0 else 1 - quarter)) * size, size), size)

    by_x = "u"

    def spread_out(name):
        _, _, _, _, result, _, place, size = grads[name]
        if name in by_x:
            target = result.at[place(far_seat(0, size))]
            net.wait(("rx", name), target, xdev)
            net.send(("rr", name), target, target, ydev)
        else:
            target = result.at[place(seat(1, size))]
            net.wait(("ry", name), target, ydev)
            net.send(("rr", name), target, target, xdev)

    def collect(name):
        _, _, _, _, result, _, place, size = grads[name]
        if name in by_x:
            net.wait(("ry", name), result.at[place(seat(1, size))], ydev)
        else:
            net.wait(("rx", name), result.at[place(far_seat(0, size))], xdev)
        net.wait(("rr", name), result.at[place(far_seat(1, size))], ydev if name in by_x else xdev)

    SMALL[...] = jnp.zeros_like(SMALL)
    other_part("q")
    other_part("o")
    have_here("u")
    have_here("d")
    across_y("u")
    across_y("d")

    def seat_of(h, size):
        return (quarter if h == 0 else 1 - quarter) * size

    def feed_part(s, h):
        def body(at):
            for begin in range(0, uc, tile):
                cols = pl.ds(h * uc + begin, tile)
                bias_at = (side * 2) * uc + seat_of(h, uc) + begin
                up = dot(B[s, at, :], WU[:, cols]) + biases[1:2, pl.ds(pl.multiple_of(bias_at, tile), tile)]
                pull = dot(G[s, at, :], WD[cols, :], NT)
                gate = 0.5 * (1.0 + lax.erf(up * 0.5**0.5))
                bell = jnp.exp(-0.5 * up * up) * 0.3989422804014327
                ACT[s, at, cols] = (up * gate).astype(BF16)
                grad = (pull * (gate + up * bell)).astype(BF16)
                GUP[s, at, cols] = grad
                SMALL[1:2, pl.ds(pl.multiple_of(seat_of(h, uc) + begin, tile), tile)] += jnp.sum(
                    grad.astype(F32), axis=0, keepdims=True
                )

        each_tile(body)

    def halves(value):
        left, right = value[:, :half], value[:, half:]
        return jnp.where(col == 0, left, right).astype(BF16), jnp.where(col == 0, right, left).astype(BF16)

    def leave(s, c, out, slope):
        @pl.loop(0, piece // tile, unroll=2)
        def _(i):
            at = pl.ds(pl.multiple_of(c * piece + i * tile, tile), tile)
            to = pl.ds(pl.multiple_of(i * tile, tile), tile) if s == 1 else at
            result = dot(CTX[s, at, :], WO[...]) + dot(ACT[s, at, :], WD[...])
            grad_one = dot(MIX[s, at, :], WQ[...], NT)
            grad_two = dot(GUP[s, at, :], WU[...], NT)
            out[0][at, :], out[1][to, :] = halves(result)
            unit, inv = unit_rows(s, at)
            for i_row, value in enumerate([grad_one * unit, grad_one, grad_two * unit, grad_two]):
                SMALL[2 + i_row : 3 + i_row, :] += jnp.sum(value, axis=0, keepdims=True)
            scaled = grad_one * params[0:1, :] + grad_two * params[2:3, :]
            mean_scaled = jnp.mean(scaled, axis=1, keepdims=True)
            mean_unit = jnp.mean(scaled * unit, axis=1, keepdims=True)
            slope[0][at, :], slope[1][to, :] = halves(inv * (scaled - mean_scaled - unit * mean_unit))
            if s == 0:
                SMALL[6:7, own_cols] += jnp.sum(G[0, at, own_cols].astype(F32), axis=0, keepdims=True)

    given = [ZD, SD]
    given_copies = []
    near = [X.at[1, :, pl.ds(0, half)], X.at[1, :, pl.ds(half, half)]]

    def leave_far(c):
        spots = [buffer.at[:, pl.ds(c * half, half)] for buffer in given]
        leave(1, c, (OUT.at[0], spots[0]), (OUT.at[1], spots[1]))
        for i in range(2):
            given_copies.append(net.send(("out", i, c), spots[i], LAND.at[i, chunk(c), :], core))

    def pass_far(c):
        for i in range(2):
            net.wait(("out", i, c), LAND.at[i, chunk(c), :], core)
            LAND[i, chunk(c), :] = (LAND[i, chunk(c), :].astype(F32) + OUT[i, chunk(c), :].astype(F32)).astype(BF16)
            net.send(("far out", i, c), LAND.at[i, chunk(c), :], FAR.at[i, chunk(c), :], xdev)

    def leave_own(c):
        sides = [[buffer.at[0, :, pl.ds(h * half, half)] for h in range(2)] for buffer in (ACT, GUP)]
        leave(0, c, *sides)
        for i in range(2):
            net.send(("own out", i, c), sides[i][1].at[chunk(c), :], near[i].at[chunk(c), :], core)

    def add_up(i, c):
        buffer = (ACT, GUP)[i]
        net.wait(("own out", i, c), near[i].at[chunk(c), :], core)
        net.wait(("far out", i, c), FAR.at[i, chunk(c), :], xdev)
        total = buffer[0, chunk(c), pl.ds(0, half)].astype(F32) + near[i][chunk(c), :].astype(F32)
        FAR[i, chunk(c), :] = (total + FAR[i, chunk(c), :].astype(F32)).astype(BF16)
        return move(FAR.at[i, chunk(c), :], (sum_out, slope_out)[i].at[chunk(c), :])

    def mixed_sums():
        for h in range(2):
            sums = [jnp.sum(MIX[s, :, pl.ds(h * qc, qc)].astype(F32), axis=0, keepdims=True) for s in range(2)]
            SMALL[0:1, pl.ds(pl.multiple_of(seat_of(h, qc), LANES), qc)] = sums[0] + sums[1]

    def small_z():
        for t in range(1, R):
            net.send(("sz", t), SMALL, SMALL_Z.at[row], zdev(t))
        SMALL_Z[row] = SMALL[...]

    def small_y():
        for t in range(1, R):
            net.wait(("sz", t), SMALL_Z.at[lax.rem(row - t + R, R)], zdev(-t))
        total = SMALL_Z[0]
        for r in range(1, R):
            total = total + SMALL_Z[r]
        SMALL_P[0] = total
        net.send("sy", SMALL_P.at[0], SMALL_P.at[1], ydev)

    def small_x():
        net.wait("sy", SMALL_P.at[1], ydev)
        SMALL_P[2] = SMALL_P[0] + SMALL_P[1]
        net.send("sx", SMALL_P.at[2], SMALL_P.at[3], xdev)

    def small_core():
        net.wait("sx", SMALL_P.at[3], xdev)
        SMALL_P[4] = SMALL_P[2] + SMALL_P[3]
        net.send("sc", SMALL_P.at[4], SMALL_P.at[5], core)

    def small_end():
        net.wait("sc", SMALL_P.at[5], core)
        SMALL_P[5] = SMALL_P[4] + SMALL_P[5]

    done = []
    feed_part(1, 0)
    feed_part(1, 1)
    for copy in handed:
        net.sent(copy)
    leave_far(1)
    feed_part(0, 1)
    pass_far(1)
    own_part("o")
    other_part("u")
    across("o", 2)
    own_part("q")
    across("o", 3)
    across("q", 2)
    across("q", 3)
    feed_part(0, 0)
    across("o", 1)
    leave_far(0)
    across("q", 1)
    for copy in given_copies:
        net.sent(copy)
    own_part("d")
    own_part("u")
    across("u", 3)
    pass_far(0)
    other_part("d")
    leave_own(1)
    across("q", 0)
    across("u", 2)
    across("d", 2)
    across("o", 0)
    mixed_sums()
    leave_own(0)
    small_z()
    across("u", 1)
    done.append(finish("o"))
    done += [add_up(0, 1), add_up(1, 1)]
    across("u", 0)
    across("d", 3)
    small_y()
    across("d", 1)
    done.append(finish("q"))
    done.append(finish("u"))
    small_x()
    done += [add_up(0, 0), add_up(1, 0)]
    across("d", 0)
    spread_out("q")
    done.append(finish("d"))
    small_core()
    spread_out("u")
    spread_out("o")
    small_end()
    spread_out("d")

    def side_span(which, size):
        return pl.ds(pl.multiple_of(which * size, LANES), size)

    for i, which in [(2, side), (3, 1 - side)]:
        done += [
            move(SMALL_P.at[i, pl.ds(0, 1), pl.ds(0, 2 * qc)], bq_out.at[:, side_span(which, 2 * qc)]),
            move(SMALL_P.at[i, pl.ds(1, 1), pl.ds(0, 2 * uc)], bu_out.at[:, side_span(which, 2 * uc)]),
        ]
    done += [
        move(SMALL_P.at[5, pl.ds(2, 4), own_cols], gains_out),
        move(SMALL_P.at[4, pl.ds(6, 1), own_cols], cot_out),
    ]
    for name in "oqdu":
        collect(name)
    for copy in done:
        copy.wait()
    net.drain()


def whole_block(hidden, cot, wq, wo, wu, wd, *rest):
    length, half = hidden.shape
    width = 2 * half
    shard = wq.shape[0]
    wide3 = wq.shape[1] // 2
    wide = wide3 // 3
    units = wu.shape[1] // 2
    qc, oc, uc = wide3 // 2, wide // 2, units // 2
    out_shape = [
        jax.ShapeDtypeStruct(shape, kind)
        for shape, kind in [
            ((shard, 4 * qc), BF16), ((4 * oc, shard), BF16), ((shard, 4 * uc), BF16), ((4 * uc, shard), BF16),
            ((length, half), BF16), ((length, half), BF16),
            ((4, half), F32), ((1, 4 * qc), F32), ((1, 4 * uc), F32), ((1, half), F32),
        ]
    ]
    both = lambda n: pltpu.VMEM((2, length, n), BF16)
    plain = lambda *shape: pltpu.VMEM(shape, BF16)
    floats = lambda *shape: pltpu.VMEM(shape, F32)
    quarter_grads = [plain(width, qc), plain(oc, width), plain(width, uc), plain(uc, width)]
    scratch = [
        both(width), both(width), both(width), both(width), both(half),
        plain(width, wide3), plain(wide, width), plain(width, units), plain(units, width),
        both(wide3), both(wide), both(units), both(units),
        floats(8, length), floats(8, length), floats(8, width), floats(8, 4 * uc),
        *[floats(length, LANES)] * 5,
        *quarter_grads * 3,
        plain(3, shard, qc), plain(3, oc, shard), plain(3, shard, uc), plain(3, uc, shard),
        both(half), both(half), floats(8, width), floats(4, 8, width), floats(6, 8, width),
    ]
    any_spec = pl.BlockSpec(memory_space=pl.ANY)
    vmem_spec = pl.BlockSpec(memory_space=pltpu.VMEM)
    return pl.pallas_call(
        block_kernel,
        out_shape=out_shape,
        in_specs=[any_spec] * 6 + [vmem_spec] * len(rest),
        out_specs=[any_spec] * len(out_shape),
        scratch_shapes=scratch + [
            pltpu.SemaphoreType.DMA((128,)), pltpu.SemaphoreType.DMA((128,)), pltpu.SemaphoreType.DMA((32,)),
        ],
        compiler_params=pltpu.CompilerParams(collective_id=0, has_side_effects=True, vmem_limit_bytes=63 << 20),
        name="block",
    )(hidden, cot, wq, wo, wu, wd, *rest)


def widen_kernel(
    hidden, branch, cot, slope, grad_q, grad_o, grad_u, grad_d, bias_one, bias_two, gains, qkv_sum, up_sum, cot_sum,
    output, input_grad, out_q, out_o, out_u, out_d, *small,
):
    bias = (bias_one[...].astype(F32) + bias_two[...].astype(F32)).reshape(1, -1)
    output[...] = hidden[...].astype(F32) + branch[...].astype(F32) + bias
    input_grad[...] = cot[...].astype(F32) + slope[...].astype(F32)
    for source, target in [(grad_q, out_q), (grad_o, out_o), (grad_u, out_u), (grad_d, out_d)]:
        target[...] = source[...].astype(F32)
    for i in range(4):
        small[i][...] = gains[i, :]
    small[4][...] = qkv_sum[0, :]
    small[5][...] = up_sum[0, :]
    small[6][...] = cot_sum[0, :]
    small[7][...] = cot_sum[0, :]


def widen_all(hidden, branch, cot, slope, grad_q, grad_o, grad_u, grad_d, bias_one, bias_two, gains, *sums):
    steps = 4
    rows = lambda v: pl.BlockSpec((v.shape[0] // steps, v.shape[1]), lambda i: (i, 0))
    whole = lambda v: pl.BlockSpec(v.shape, lambda i: (0,) * v.ndim)
    large = [hidden, branch, cot, slope, grad_q, grad_o, grad_u, grad_d]
    tiny = [bias_one, bias_two, gains, *sums]
    wide = [hidden, cot, grad_q, grad_o, grad_u, grad_d]
    flat = [gains.shape[1]] * 4 + [v.shape[1] for v in sums] + [sums[-1].shape[1]]
    return pl.pallas_call(
        widen_kernel,
        grid=(steps,),
        in_specs=[rows(v) for v in large] + [whole(v) for v in tiny],
        out_specs=[rows(v) for v in wide] + [pl.BlockSpec((n,), lambda i: (0,)) for n in flat],
        out_shape=[jax.ShapeDtypeStruct(v.shape, F32) for v in wide] + [jax.ShapeDtypeStruct((n,), F32) for n in flat],
        compiler_params=pltpu.CompilerParams(vmem_limit_bytes=63 << 20),
        name="widen",
    )(*large, *tiny)


def local_block(
    hidden,
    segments,
    ln1_gain,
    ln1_bias,
    qkv_weight,
    qkv_bias,
    out_weight,
    out_bias,
    ln2_gain,
    ln2_bias,
    up_weight,
    up_bias,
    down_weight,
    down_bias,
    cotangent,
):
    lane = np.arange(LANES) % HEAD_DIM
    frequency = np.where(lane < ROT, 10000.0 ** (-2.0 * (lane % (ROT // 2)) / ROT), 0.0)
    sign = np.where(lane < ROT, np.where(lane < ROT // 2, -1.0, 1.0), 0.0)
    freq = np.stack([frequency, sign] * 4).astype(np.float32)
    flat = [ln1_gain, ln1_bias, ln2_gain, ln2_bias, qkv_bias, up_bias]
    grad_q, grad_o, grad_u, grad_d, branch, slope, gains, qkv_sum, up_sum, cot_sum = whole_block(
        hidden, cotangent, qkv_weight, out_weight, up_weight, down_weight, segments, jnp.asarray(freq), *flat
    )
    output, input_grad, grad_q, grad_o, grad_u, grad_d, *small = widen_all(
        hidden, branch, cotangent, slope, grad_q, grad_o, grad_u, grad_d,
        out_bias, down_bias, gains, qkv_sum, up_sum, cot_sum,
    )
    gain_one, shift_one, gain_two, shift_two, qkv_sum, up_sum, cot_sum, cot_again = small
    return (
        output, input_grad, gain_one, shift_one, grad_q, qkv_sum, grad_o, cot_sum,
        gain_two, shift_two, grad_u, up_sum, grad_d, cot_again,
    )


def normalize(values):
    centred = values - jnp.mean(values, axis=-1, keepdims=True)
    variance = jnp.mean(centred * centred, axis=-1, keepdims=True)
    inv_std = lax.rsqrt(variance + EPS)
    return centred * inv_std, inv_std


def make_general(groups, rows, cols):
    quarters = groups // 2

    def pair_swap(value):
        return lax.ppermute(value, "dp", [(d, d ^ 1) for d in range(groups)])

    def quarter_shift(value, shift):
        moves = [(2 * a + b, 2 * ((a + shift) % quarters) + b) for a in range(quarters) for b in range(2)]
        return lax.ppermute(value, "dp", moves)

    def row_shift(value, shift):
        return lax.ppermute(value, "row", [(r, (r + shift) % rows) for r in range(rows)])

    def core_swap(value):
        return lax.ppermute(value, "col", [(0, 1), (1, 0)])

    def local(
        hidden,
        segments,
        ln1_gain,
        ln1_bias,
        qkv_weight,
        qkv_bias,
        out_weight,
        out_bias,
        ln2_gain,
        ln2_bias,
        up_weight,
        up_bias,
        down_weight,
        down_bias,
        cotangent,
    ):
        assert segments.shape[0] == 1 and cols == 2
        length = segments.shape[1]
        half_width = hidden.shape[1]
        width = 2 * half_width
        shard = qkv_weight.shape[0]
        heads = qkv_weight.shape[1] // (3 * HEAD_DIM) // 2
        wide = heads * HEAD_DIM
        units = up_weight.shape[1] // 2
        whole_heads = heads % quarters == 0
        dp = lax.axis_index("dp")
        row = lax.axis_index("row")
        col = lax.axis_index("col")
        side = lax.rem(dp, 2)
        quarter = dp // 2

        def both(mine, other):
            flip = col == 0
            return jnp.concatenate([jnp.where(flip, mine, other), jnp.where(flip, other, mine)], axis=-1)

        def half_of(value, axis):
            size = value.shape[axis] // 2
            return lax.dynamic_slice_in_dim(value, side * size, size, axis)

        def piece_of(value, shift, axis, placed=False):
            size = value.shape[axis] // quarters
            if placed:
                return lax.slice_in_dim(value, shift * size, (shift + 1) * size, axis=axis)
            return lax.dynamic_slice_in_dim(value, lax.rem(quarter - shift + quarters, quarters) * size, size, axis)

        def in_place(pieces, axis):
            if quarters == 1:
                return pieces[0]
            if quarters == 2:
                flip = quarter == 0
                first = jnp.where(flip, pieces[0], pieces[1])
                second = jnp.where(flip, pieces[1], pieces[0])
                return jnp.concatenate([first, second], axis=axis)
            order = lax.rem(quarter - jnp.arange(quarters) + quarters, quarters)
            stacked = jnp.take(jnp.stack(pieces), order, axis=0)
            return jnp.concatenate([stacked[i] for i in range(quarters)], axis=axis)

        def near(pieces, axis, keep):
            return jnp.concatenate(pieces, axis=axis) if keep else in_place(pieces, axis)

        def gather(value, width_axis, unit_axis, keep):
            mine = piece_of(value, 0, unit_axis)
            received = {0: mine}
            ahead = behind = mine
            for step in range(1, rows):
                if step <= rows // 2:
                    ahead = row_shift(ahead, -1)
                    received[step] = ahead
                if step <= (rows - 1) // 2:
                    behind = row_shift(behind, 1)
                    received[rows - step] = behind
            result = jnp.zeros(
                [width if i == width_axis else n for i, n in enumerate(value.shape)], value.dtype
            )
            for step in range(rows):
                if step == 0:
                    pieces = [piece_of(value, q, unit_axis) for q in range(quarters)]
                else:
                    pieces = [received[step]]
                    pieces += [quarter_shift(received[step], q) for q in range(1, quarters)]
                block = near(pieces, unit_axis, keep)
                place = lax.rem(row + step, rows) * shard
                result = lax.dynamic_update_slice_in_dim(result, block, place, width_axis)
            return result

        hidden_other = core_swap(hidden)
        hidden_far = pair_swap(hidden)
        cot_other = core_swap(cotangent)
        cot_far = pair_swap(cotangent)
        params = jnp.stack([ln1_gain, ln1_bias, ln2_gain, ln2_bias])
        params = both(params, core_swap(params)).astype(F32)
        gain_one, shift_one, gain_two, shift_two = [params[i][None, :] for i in range(4)]
        inputs = [both(hidden, hidden_other), both(hidden_far, core_swap(hidden_far))]
        cots = [both(cotangent, cot_other), both(cot_far, core_swap(cot_far))]
        segs = [segments, pair_swap(segments)]

        qkv_cols = qkv_weight.reshape(shard, 2, heads, 3, HEAD_DIM)
        qkv_cols = lax.dynamic_index_in_dim(qkv_cols, side, 1, keepdims=False)
        qkv_cols = jnp.swapaxes(qkv_cols, 1, 2).reshape(shard, 3, wide)
        qkv_all = gather(qkv_cols, 0, 2, whole_heads).reshape(width, 3 * wide)
        out_all = gather(half_of(out_weight, 0), 1, 0, whole_heads)
        up_all = gather(half_of(up_weight, 1), 0, 1, True)
        down_all = gather(half_of(down_weight, 0), 1, 0, True)

        bias_cols = lax.dynamic_index_in_dim(qkv_bias.reshape(2, heads, 3, HEAD_DIM), side, 0, keepdims=False)
        bias_cols = jnp.swapaxes(bias_cols, 0, 1).reshape(1, 3, wide)
        bias_cols = near([piece_of(bias_cols, q, 2) for q in range(quarters)], 2, whole_heads)
        bias_cols = bias_cols.reshape(1, 3 * wide).astype(F32)
        up_half = half_of(up_bias, 0)
        up_row = jnp.concatenate([piece_of(up_half, q, 0) for q in range(quarters)])[None, :].astype(F32)

        norms = []
        contexts = []
        grads_mixed = []
        for values, cot, seg in zip(inputs, cots, segs):
            unit, inv = normalize(values.astype(F32))
            act_one = (unit * gain_one + shift_one).astype(BF16)
            act_two = (unit * gain_two + shift_two).astype(BF16)
            norms.append((unit, inv, act_one, act_two))
            cos_rows, sine_rows = rotary_tables(doc_positions(seg).reshape(length))
            mixed = dot(act_one, qkv_all) + bias_cols
            cos_wide = jnp.tile(cos_rows, (1, 2 * wide // LANES))
            sine_wide = jnp.tile(sine_rows, (1, 2 * wide // LANES))
            turned = mixed[:, : 2 * wide]
            lane = jnp.arange(2 * wide) % HEAD_DIM
            swapped = jnp.where(
                lane < ROT // 2, jnp.roll(turned, -(ROT // 2), axis=1), jnp.roll(turned, ROT // 2, axis=1)
            )
            turned = turned * cos_wide + swapped * sine_wide
            qkv = jnp.concatenate([turned, mixed[:, 2 * wide :]], axis=1).astype(BF16)
            grad_context = dot(cot, out_all, NT).astype(BF16)
            context, grad_mixed = attention(qkv, grad_context, seg, cos_rows, sine_rows)
            contexts.append(context)
            grads_mixed.append(grad_mixed)

        feeds = [feed(norm[3], cot, up_all, up_row, down_all) for norm, cot in zip(norms, cots)]

        def reduce_grad(left, right, width_axis, unit_axis, placed, shape=None):
            total = dot(left[0], right[0], TN) + dot(left[1], right[1], TN)
            if shape is not None:
                total = total.reshape(shape)
            mine = piece_of(total, 0, unit_axis, placed)
            for q in range(1, quarters):
                part = piece_of(total, q, unit_axis, placed).astype(BF16)
                mine = mine + quarter_shift(part, -q).astype(F32)
            cut = lambda t: lax.dynamic_slice_in_dim(mine, lax.rem(row + t, rows) * shard, shard, width_axis)
            result = cut(0)
            for t in range(1, rows):
                result = result + row_shift(cut(t).astype(BF16), t).astype(F32)
            result = result.astype(BF16)
            pieces = [result] + [quarter_shift(result, q) for q in range(1, quarters)]
            result = in_place(pieces, unit_axis)
            far = pair_swap(result)
            flip = side == 0
            return jnp.concatenate(
                [jnp.where(flip, result, far), jnp.where(flip, far, result)], axis=unit_axis
            ).astype(F32)

        acts_one = [n[2] for n in norms]
        acts_two = [n[3] for n in norms]
        out_grad = reduce_grad(contexts, cots, 1, 0, whole_heads)
        qkv_grad = reduce_grad(acts_one, grads_mixed, 0, 2, whole_heads, (width, 3, wide))
        down_grad = reduce_grad([f[0] for f in feeds], cots, 1, 0, True)
        up_grad = reduce_grad(acts_two, [f[1] for f in feeds], 0, 1, True)
        qkv_grad = qkv_grad.reshape(shard, 3, 2 * heads, HEAD_DIM)
        qkv_grad = jnp.swapaxes(qkv_grad, 1, 2).reshape(shard, 6 * wide)

        outs = []
        slopes = []
        norm_sums = jnp.zeros((4, width), F32)
        for index in range(2):
            unit, inv, _, _ = norms[index]
            act, grad_up, _ = feeds[index]
            outs.append((dot(contexts[index], out_all) + dot(act, down_all)).astype(BF16))
            grad_one = dot(grads_mixed[index], qkv_all, NT)
            grad_two = dot(grad_up, up_all, NT)
            norm_sums += jnp.stack(
                [
                    jnp.sum(grad_one * unit, axis=0),
                    jnp.sum(grad_one, axis=0),
                    jnp.sum(grad_two * unit, axis=0),
                    jnp.sum(grad_two, axis=0),
                ]
            )
            scaled = grad_one * gain_one + grad_two * gain_two
            mean_scaled = jnp.mean(scaled, axis=1, keepdims=True)
            mean_unit = jnp.mean(scaled * unit, axis=1, keepdims=True)
            slopes.append((inv * (scaled - mean_scaled - unit * mean_unit)).astype(BF16))

        def fold(pair):
            sums = []
            for value in pair:
                kept = lax.dynamic_slice_in_dim(value, col * half_width, half_width, 1).astype(F32)
                given = lax.dynamic_slice_in_dim(value, (1 - col) * half_width, half_width, 1)
                sums.append(kept + core_swap(given).astype(F32))
            return sums[0] + pair_swap(sums[1].astype(BF16)).astype(F32)

        cot_local = cotangent.astype(F32)
        output = hidden.astype(F32) + fold(outs) + (out_bias.astype(F32) + down_bias.astype(F32))
        input_grad = cot_local + fold(slopes)

        qkv_sum = (
            jnp.sum(grads_mixed[0].astype(F32), axis=0) + jnp.sum(grads_mixed[1].astype(F32), axis=0)
        ).reshape(3, wide)
        if whole_heads:
            qkv_sum = in_place([piece_of(qkv_sum, q, 1, True) for q in range(quarters)], 1)
        up_sum = (feeds[0][2] + feeds[1][2])[0]
        up_sum = in_place([piece_of(up_sum, q, 0, True) for q in range(quarters)], 0)

        def widen(value):
            zeros = jnp.zeros_like(value)
            flip = side == 0
            return jnp.concatenate([jnp.where(flip, value, zeros), jnp.where(flip, zeros, value)], axis=-1)

        kept = lax.dynamic_slice_in_dim(norm_sums, col * half_width, half_width, 1)
        given = lax.dynamic_slice_in_dim(norm_sums, (1 - col) * half_width, half_width, 1)
        norm_sums = kept + core_swap(given)
        small = jnp.concatenate(
            [widen(qkv_sum).reshape(-1), widen(up_sum), jnp.sum(cot_local, axis=0), norm_sums.reshape(-1)]
        )
        small = lax.psum(small, ("dp", "row"))
        sizes = [6 * wide, 2 * units, half_width, half_width, half_width, half_width, half_width]
        parts = []
        start = 0
        for size in sizes:
            parts.append(lax.slice_in_dim(small, start, start + size))
            start += size
        qkv_sum, up_sum, cot_sum, gain_one_sum, shift_one_sum, gain_two_sum, shift_two_sum = parts
        qkv_sum = jnp.swapaxes(qkv_sum.reshape(3, 2 * heads, HEAD_DIM), 0, 1).reshape(-1)
        return (
            output,
            input_grad,
            gain_one_sum,
            shift_one_sum,
            qkv_grad,
            qkv_sum,
            out_grad,
            cot_sum,
            gain_two_sum,
            shift_two_sum,
            up_grad,
            up_sum,
            down_grad,
            cot_sum,
        )

    return local


def solution(mesh):
    placed = (
        P(("dp", "row"), "col"),
        P(("dp", "row"), None),
        P("col"),
        P("col"),
        P("row", "col"),
        P("col"),
        P("col", "row"),
        P("col"),
        P("col"),
        P("col"),
        P("row", "col"),
        P("col"),
        P("col", "row"),
        P("col"),
        P(("dp", "row"), "col"),
    )
    groups, rows, cols = mesh.shape["dp"], mesh.shape["row"], mesh.shape["col"]
    paired = (groups, rows, cols) == (4, 4, 2)
    return jax.shard_map(
        local_block if paired else make_general(groups, rows, cols),
        mesh=mesh,
        in_specs=placed,
        out_specs=(
            P(("dp", "row"), "col"),
            P(("dp", "row"), "col"),
            P("col"),
            P("col"),
            P("row", "col"),
            P("col"),
            P("col", "row"),
            P("col"),
            P("col"),
            P("col"),
            P("row", "col"),
            P("col"),
            P("col", "row"),
            P("col"),
        ),
        check_vma=False,
    )
```

```python
import functools

import jax
import jax.numpy as jnp
import numpy as np
from jax import lax
from jax.experimental import pallas as pl
from jax.experimental.pallas import tpu as pltpu
from jax.sharding import PartitionSpec as P

HEAD_DIM = 64
ROT = 16
EPS = 1e-05
MAX_DOC = 512
DOCS = 4
LANES = 128
BF16 = jnp.bfloat16
F32 = jnp.float32

NT = (((1,), (1,)), ((), ()))
TN = (((0,), (0,)), ((), ()))
NN = (((1,), (0,)), ((), ()))


def dot(a, b, dims=NN):
    return lax.dot_general(a, b, dims, preferred_element_type=F32)


def doc_positions(segments):
    length = segments.shape[-1]
    places = jnp.arange(length, dtype=jnp.int32)
    changed = jnp.concatenate(
        [jnp.ones(segments.shape[:-1] + (1,), dtype=bool), segments[..., 1:] != segments[..., :-1]],
        axis=-1,
    )
    starts = lax.cummax(jnp.where(changed, places, jnp.zeros_like(places)), axis=segments.ndim - 1)
    return places - starts


def rotary_tables(positions):
    lane = jnp.arange(LANES) % HEAD_DIM
    frequency = 10000.0 ** (-2.0 * (lane % (ROT // 2)).astype(F32) / ROT)
    turning = lane < ROT
    angles = positions.astype(F32)[:, None] * jnp.where(turning, frequency, 0.0)[None, :]
    sign = jnp.where(turning, jnp.where(lane < ROT // 2, -1.0, 1.0), 0.0)
    return jnp.cos(angles), jnp.sin(angles) * sign[None, :]


def turn(values, cos_rows, sine_rows, low_lanes):
    half = ROT // 2
    up = pltpu.roll(values, values.shape[1] - half, 1)
    down = pltpu.roll(values, half, 1)
    return values * cos_rows + jnp.where(low_lanes, up, down) * sine_rows


def attention_kernel(
    q_ref, k_ref, v_ref, gc_ref, seg_row_ref, seg_col_ref, cos_ref, sin_ref, ctx_ref, gm_ref, dk_acc, dv_acc, *, block
):
    pair = pl.program_id(0)
    pairs = pl.num_programs(0)
    length = q_ref.shape[0]
    lane = lax.broadcasted_iota(jnp.int32, (1, LANES), 1)
    low_lanes = lane % HEAD_DIM < ROT // 2
    first = lane < HEAD_DIM
    zero = jnp.zeros((), BF16)

    def split(values):
        return [jnp.where(first, values, zero), jnp.where(first, zero, values)]

    dk_acc[...] = jnp.zeros_like(dk_acc)
    dv_acc[...] = jnp.zeros_like(dv_acc)
    for begin in range(0, length, block):
        low = max(0, begin - (MAX_DOC - 1)) // LANES * LANES
        rows = pl.ds(begin, block)
        keys = pl.ds(low, begin + block - low)
        width = begin + block - low
        q_parts = split(q_ref[rows, :] * jnp.asarray(HEAD_DIM**-0.5, BF16))
        g_parts = split(gc_ref[rows, :])
        k_block = k_ref[keys, :]
        v_block = v_ref[keys, :]
        places = begin + lax.broadcasted_iota(jnp.int32, (block, width), 0)
        key_places = low + lax.broadcasted_iota(jnp.int32, (block, width), 1)
        allowed = (seg_col_ref[rows, :] == seg_row_ref[:, keys]) & (places >= key_places)
        probs = []
        grads = []
        for part in range(2):
            scores = dot(q_parts[part], k_block, NT)
            scores = jnp.where(allowed, scores, -1e30)
            top = jnp.max(scores, axis=1, keepdims=True)
            powers = jnp.exp(scores - top)
            total = jnp.sum(powers, axis=1, keepdims=True)
            chances = powers * (1.0 / total)
            slopes = dot(g_parts[part], v_block, NT)
            inner = jnp.sum(slopes * chances, axis=1, keepdims=True)
            probs.append(chances.astype(BF16))
            grads.append((chances * (slopes - inner)).astype(BF16))
        context = jnp.where(first, dot(probs[0], v_block), dot(probs[1], v_block))
        ctx_ref[rows, :] = context.astype(BF16)
        dq = jnp.where(first, dot(grads[0], k_block), dot(grads[1], k_block)) * HEAD_DIM**-0.5
        dq = turn(dq, cos_ref[rows, :], -sin_ref[rows, :], low_lanes)
        gm_ref[rows, pl.ds(pl.multiple_of(pair * LANES, LANES), LANES)] = dq.astype(BF16)
        dk_acc[keys, :] += dot(grads[0], q_parts[0], TN) + dot(grads[1], q_parts[1], TN)
        dv_acc[keys, :] += dot(probs[0], g_parts[0], TN) + dot(probs[1], g_parts[1], TN)
    dk = turn(dk_acc[...], cos_ref[...], -sin_ref[...], low_lanes)
    gm_ref[:, pl.ds(pl.multiple_of((pairs + pair) * LANES, LANES), LANES)] = dk.astype(BF16)
    gm_ref[:, pl.ds(pl.multiple_of((2 * pairs + pair) * LANES, LANES), LANES)] = dv_acc[...].astype(BF16)


def attention(qkv, grad_context, seg_row, cos_rows, sine_rows):
    length, wide = qkv.shape
    pairs = wide // (3 * LANES)
    block = min(256, length)
    column = lambda shift: pl.BlockSpec((length, LANES), lambda p: (0, shift + p))
    whole = lambda *shape: pl.BlockSpec(shape, lambda p: (0, 0))
    flops = pairs * 2 * 6 * 2 * length * length * LANES // 2
    return pl.pallas_call(
        functools.partial(attention_kernel, block=block),
        grid=(pairs,),
        in_specs=[
            column(0),
            column(pairs),
            column(2 * pairs),
            column(0),
            whole(1, length),
            whole(length, 1),
            whole(length, LANES),
            whole(length, LANES),
        ],
        out_specs=[column(0), whole(length, wide)],
        out_shape=[
            jax.ShapeDtypeStruct((length, pairs * LANES), BF16),
            jax.ShapeDtypeStruct((length, wide), BF16),
        ],
        scratch_shapes=[pltpu.VMEM((length, LANES), F32), pltpu.VMEM((length, LANES), F32)],
        compiler_params=pltpu.CompilerParams(vmem_limit_bytes=48 << 20),
        cost_estimate=pl.CostEstimate(
            flops=flops, bytes_accessed=6 * length * wide, transcendentals=pairs * length * length
        ),
        name="attention",
    )(qkv, qkv, qkv, grad_context, seg_row, seg_row.reshape(length, 1), cos_rows, sine_rows)


def feed_kernel(a_ref, g_ref, up_ref, bias_ref, down_ref, act_ref, gup_ref, sum_ref, *, chunk):
    units = up_ref.shape[1]

    @pl.when(pl.program_id(0) == 0)
    def _():
        sum_ref[...] = jnp.zeros_like(sum_ref)

    for begin in range(0, units, chunk):
        cols = pl.ds(begin, chunk)
        up = dot(a_ref[...], up_ref[:, cols]) + bias_ref[:, cols]
        pull = dot(g_ref[...], down_ref[cols, :], NT)
        gate = 0.5 * (1.0 + lax.erf(up * 0.5**0.5))
        bell = jnp.exp(-0.5 * up * up) * 0.3989422804014327
        act_ref[:, cols] = (up * gate).astype(BF16)
        grad = (pull * (gate + up * bell)).astype(BF16)
        gup_ref[:, cols] = grad
        sum_ref[:, cols] += jnp.sum(grad.astype(F32), axis=0, keepdims=True)


def feed(normed, cot, up_weight, up_bias, down_weight):
    tokens, width = normed.shape
    units = up_weight.shape[1]
    block = min(256, tokens)
    rows = lambda size: pl.BlockSpec((block, size), lambda i: (i, 0))
    whole = lambda *shape: pl.BlockSpec(shape, lambda i: (0, 0))
    return pl.pallas_call(
        functools.partial(feed_kernel, chunk=min(256, units)),
        grid=(tokens // block,),
        in_specs=[rows(width), rows(width), whole(width, units), whole(1, units), whole(units, width)],
        out_specs=[rows(units), rows(units), whole(1, units)],
        out_shape=[
            jax.ShapeDtypeStruct((tokens, units), BF16),
            jax.ShapeDtypeStruct((tokens, units), BF16),
            jax.ShapeDtypeStruct((1, units), F32),
        ],
        compiler_params=pltpu.CompilerParams(vmem_limit_bytes=48 << 20),
        cost_estimate=pl.CostEstimate(
            flops=4 * tokens * width * units,
            bytes_accessed=4 * tokens * width + 4 * width * units + 4 * tokens * units,
            transcendentals=2 * tokens * units,
        ),
        name="feed",
    )(normed, cot, up_weight, up_bias, down_weight)


MESH = pl.DeviceIdType.MESH


class Net:
    def __init__(self, send_sems, recv_sems):
        self.send_sems, self.recv_sems = send_sems, recv_sems
        self.slots = {}
        self.pending = []

    def slot(self, key):
        return self.slots.setdefault(key, len(self.slots))

    def make(self, key, source, target, device):
        i = self.slot(key)
        return pltpu.make_async_remote_copy(
            src_ref=source,
            dst_ref=target,
            send_sem=self.send_sems.at[i],
            recv_sem=self.recv_sems.at[i],
            device_id=device,
            device_id_type=MESH,
        )

    def send(self, key, source, target, device):
        copy = self.make(key, source, target, device)
        copy.start()
        self.pending.append(copy)
        return copy

    def sent(self, copy):
        copy.wait_send()
        self.pending = [other for other in self.pending if other is not copy]

    def wait(self, key, landed, device):
        self.make(key, landed, landed, device).wait_recv()

    def drain(self):
        for copy in self.pending:
            copy.wait_send()
        self.pending = []


def spread(columns, width):
    return jnp.concatenate([columns] * (width // LANES), axis=1)


def attend_pair(mix, base, gc, gc_base, ctx, seg_row, seg_col, cos_tab, sin_tab, dk_acc, dv_acc, block):
    length = mix.shape[0]
    lane = lax.broadcasted_iota(jnp.int32, (1, LANES), 1)
    low_lanes = lane % HEAD_DIM < ROT // 2
    first = lane < HEAD_DIM
    zero = jnp.zeros((), BF16)
    cols = [pl.ds(base + i * LANES, LANES) for i in range(3)]
    head_cols = pl.ds(gc_base, LANES)

    def split(values):
        return [jnp.where(first, values, zero), jnp.where(first, zero, values)]

    dk_acc[...] = jnp.zeros_like(dk_acc)
    dv_acc[...] = jnp.zeros_like(dv_acc)
    def ahead(begin):
        low = max(0, begin - (MAX_DOC - 1)) // LANES * LANES
        rows = pl.ds(begin, block)
        keys = pl.ds(low, begin + block - low)
        q_parts = split(mix[rows, cols[0]] * jnp.asarray(HEAD_DIM**-0.5, BF16))
        g_parts = split(gc[rows, head_cols])
        k_block = mix[keys, cols[1]]
        v_block = mix[keys, cols[2]]
        raw = [dot(q_parts[part], k_block, NT) for part in range(2)]
        pulls = [dot(g_parts[part], v_block, NT) for part in range(2)]
        return low, rows, keys, q_parts, g_parts, raw, pulls

    coming = ahead(0)
    for begin in range(0, length, block):
        low, rows, keys, q_parts, g_parts, raw, pulls = coming
        if begin + block < length:
            coming = ahead(begin + block)
        width = begin + block - low
        k_block = mix[keys, cols[1]]
        v_block = mix[keys, cols[2]]
        places = begin + lax.broadcasted_iota(jnp.int32, (block, width), 0)
        key_places = low + lax.broadcasted_iota(jnp.int32, (block, width), 1)
        allowed = (spread(seg_col[rows, :], width) == seg_row[0:1, keys]) & (places >= key_places)
        probs = []
        grads = []
        for part in range(2):
            scores = jnp.where(allowed, raw[part], -1e30)
            top = jnp.max(scores, axis=1, keepdims=True)
            powers = jnp.exp(scores - top)
            total = jnp.sum(powers, axis=1, keepdims=True)
            chances = powers * (1.0 / total)
            inner = jnp.sum(pulls[part] * chances, axis=1, keepdims=True)
            probs.append(chances.astype(BF16))
            grads.append((chances * (pulls[part] - inner)).astype(BF16))
        ctx[rows, head_cols] = jnp.where(first, dot(probs[0], v_block), dot(probs[1], v_block)).astype(BF16)
        dq = jnp.where(first, dot(grads[0], k_block), dot(grads[1], k_block)) * HEAD_DIM**-0.5
        mix[rows, cols[0]] = turn(dq, cos_tab[rows, :], -sin_tab[rows, :], low_lanes).astype(BF16)
        dk_acc[keys, :] += dot(grads[0], q_parts[0], TN) + dot(grads[1], q_parts[1], TN)
        dv_acc[keys, :] += dot(probs[0], g_parts[0], TN) + dot(probs[1], g_parts[1], TN)
    dq = mix[:, cols[0]].astype(F32)
    dk = pltpu.roll(turn(dk_acc[...], cos_tab[...], -sin_tab[...], low_lanes), HEAD_DIM, 1)
    dv = dv_acc[...]
    mix[:, cols[0]] = jnp.where(first, dq, dk).astype(BF16)
    mix[:, cols[1]] = jnp.where(first, dv, dq).astype(BF16)
    mix[:, cols[2]] = jnp.where(first, dk, dv).astype(BF16)


def block_kernel(
    hidden, cot, wq_in, wo_in, wu_in, wd_in,
    segments_in, freq_in, gain_one_in, shift_one_in, gain_two_in, shift_two_in, bq_in, bu_in,
    rq_out, ro_out, ru_out, rd_out, sum_out, slope_out, gains_out, bq_out, bu_out, cot_out,
    X, G, A, B, OUT, WQ, WO, WU, WD, MIX, CTX, ACT, GUP, rows_own, rows_far, params, biases, seg_col, cos_tab, sin_tab,
    dk_acc, dv_acc, SQ, SO, SU, SD, YQ, YO, YU, YD, ZQ, ZO, ZU, ZD, HQ, HO, HU, HD, LAND, FAR, SMALL, SMALL_Z, SMALL_P,
    send_sems, recv_sems, local_sems,
):
    R = 4
    dp, row, col = lax.axis_index("dp"), lax.axis_index("row"), lax.axis_index("col")
    side, quarter = lax.rem(dp, 2), lax.div(dp, 2)
    length, half = hidden.shape
    shard = wq_in.shape[0]
    core = (dp, row, 1 - col)
    xdev = (dp + 1 - 2 * side, row, col)
    ydev = (side + 2 * (1 - quarter), row, col)

    def zdev(t):
        return (dp, lax.rem(row + t + R, R), col)

    barrier = pltpu.get_barrier_semaphore()
    peers = [core, xdev, ydev] + [zdev(t) for t in range(1, R)]
    for peer in peers:
        pl.semaphore_signal(barrier, inc=1, device_id=peer, device_id_type=MESH)
    pl.semaphore_wait(barrier, len(peers))

    net = Net(send_sems, recv_sems)
    own_cols = pl.ds(pl.multiple_of(col * half, half), half)
    far_cols = pl.ds(pl.multiple_of((1 - col) * half, half), half)
    local = []

    def move(source, target):
        copy = pltpu.make_async_copy(source, target, local_sems.at[len(local)])
        copy.start()
        local.append(copy)
        return copy

    qc = WQ.shape[1] // 2
    oc = WO.shape[0] // 2
    uc = WU.shape[1] // 2

    def seat(h, size):
        return pl.ds(pl.multiple_of((side * 2 + (quarter if h == 0 else 1 - quarter)) * size, size), size)

    def block(t):
        return pl.ds(pl.multiple_of(lax.rem(row + t + R, R) * shard, shard), shard)

    every = slice(None)
    weights = {
        "q": (lambda h: wq_in.at[:, seat(h, qc)], lambda t, h: WQ.at[block(t), pl.ds(h * qc, qc)]),
        "o": (lambda h: wo_in.at[seat(h, oc), :], lambda t, h: WO.at[pl.ds(h * oc, oc), block(t)]),
        "u": (lambda h: wu_in.at[:, seat(h, uc)], lambda t, h: WU.at[block(t), pl.ds(h * uc, uc)]),
        "d": (lambda h: wd_in.at[seat(h, uc), :], lambda t, h: WD.at[pl.ds(h * uc, uc), block(t)]),
    }
    here_w = {}

    def start_along(name):
        here, place = weights[name]
        net.send((name, 1), here(0), place(0, 0), zdev(-1))
        net.send((name, 3), here(0), place(0, 0), zdev(1))

    def start_here(name):
        here, place = weights[name]
        here_w[name] = [move(here(h), place(0, h)) for h in range(2)]

    def along(name, t):
        place = weights[name][1]
        net.wait((name, t), place(t, 0), zdev(t))
        if t == 1:
            net.send((name, 2), place(t, 0), place(t, 0), zdev(-1))
        net.send((name, t, "y"), place(t, 0), place(t, 1), ydev)

    def across_y(name):
        place = weights[name][1]
        for t in (1, 3, 2):
            net.wait((name, t, "y"), place(t, 1), ydev)

    def have_here(name):
        for copy in here_w[name]:
            copy.wait()

    chunks = 2
    piece = length // chunks

    def chunk(c):
        return pl.ds(c * piece, piece)

    handed = []

    def hand_over(name, buffer, c):
        net.wait(("x " + name, c), buffer.at[1, chunk(c), own_cols], xdev)
        spot = buffer.at[1, chunk(c), own_cols]
        handed.append(net.send(("far " + name, c), spot, spot, core))

    def have_far(name, buffer):
        for c in range(chunks):
            net.wait(("far " + name, c), buffer.at[1, chunk(c), far_cols], core)

    start_along("q")
    net.send("core h", hidden, X.at[0, :, own_cols], core)
    start_along("o")
    here_h = move(hidden, X.at[0, :, own_cols])
    lane = lax.broadcasted_iota(jnp.int32, (1, LANES), 1)
    low_lanes = lane % HEAD_DIM < ROT // 2
    first = lane < HEAD_DIM

    seg = segments_in[...]
    start = jnp.zeros_like(seg)
    for number in range(1, DOCS):
        count = jnp.sum((seg < number).astype(jnp.int32), axis=1, keepdims=True)
        start = jnp.where(seg == number, count, start)
    rows_own[0:1, :] = seg.astype(F32)
    rows_own[1:2, :] = (lax.broadcasted_iota(jnp.int32, seg.shape, 1) - start).astype(F32)
    for i, source in enumerate([gain_one_in, shift_one_in, gain_two_in, shift_two_in]):
        params[i : i + 1, own_cols] = source[...].astype(F32).reshape(1, half)
    biases[0:1, pl.ds(0, bq_in.shape[0])] = bq_in[...].astype(F32).reshape(1, -1)
    biases[1:2, :] = bu_in[...].astype(F32).reshape(1, -1)
    net.send("core p", params.at[:, own_cols], params.at[:, own_cols], core)
    net.send("x rows", rows_own, rows_far, xdev)
    for c in range(chunks):
        net.send(("x h", c), hidden.at[chunk(c), :], X.at[1, chunk(c), own_cols], xdev)
    for c in range(chunks):
        net.send(("x g", c), cot.at[chunk(c), :], G.at[1, chunk(c), own_cols], xdev)
    net.send("core g", cot, G.at[0, :, own_cols], core)
    start_here("q")
    start_here("o")
    here_g = move(cot, G.at[0, :, own_cols])
    start_here("u")
    start_here("d")

    tile = 256
    GC = ACT.at[0]

    def each_tile(body):
        @pl.loop(0, length // tile, unroll=2)
        def _(i):
            body(pl.ds(pl.multiple_of(i * tile, tile), tile))

    def unit_rows(s, at):
        values = X[s, at, :].astype(F32)
        centred = values - jnp.mean(values, axis=-1, keepdims=True)
        inv = lax.rsqrt(jnp.mean(centred * centred, axis=-1, keepdims=True) + EPS)
        return centred * inv, inv

    def norm(s, at):
        unit, _ = unit_rows(s, at)
        A[s, at, :] = (unit * params[0:1, :] + params[1:2, :]).astype(BF16)
        B[s, at, :] = (unit * params[2:3, :] + params[3:4, :]).astype(BF16)

    def tables(rows):
        seg_col[...] = jnp.transpose(jnp.broadcast_to(rows[0:1, :], (LANES, length)))
        angles = jnp.transpose(jnp.broadcast_to(rows[1:2, :], (LANES, length))) * freq_in[0:1, :]
        cos_tab[...] = jnp.cos(angles)
        sin_tab[...] = jnp.sin(angles) * freq_in[1:2, :]

    def project(s, halves_in):
        low, high = halves_in[0] * qc, (halves_in[-1] + 1) * qc

        def body(at):
            product = dot(A[s, at, :], WQ[:, pl.ds(low, high - low)])
            cos_rows, sin_rows = cos_tab[at, :], sin_tab[at, :]
            for h in halves_in:
                mixed = product[:, h * qc - low : (h + 1) * qc - low] + biases[0:1, seat(h, qc)]
                t0, t1, t2 = [mixed[:, i * LANES : (i + 1) * LANES] for i in range(3)]
                query = jnp.where(first, t0, t1)
                key = pltpu.roll(jnp.where(first, t2, t0), HEAD_DIM, 1)
                value = jnp.where(first, t1, t2)
                MIX[s, at, pl.ds(h * qc, LANES)] = turn(query, cos_rows, sin_rows, low_lanes).astype(BF16)
                MIX[s, at, pl.ds(h * qc + LANES, LANES)] = turn(key, cos_rows, sin_rows, low_lanes).astype(BF16)
                MIX[s, at, pl.ds(h * qc + 2 * LANES, LANES)] = value.astype(BF16)

        each_tile(body)

    def pull_context(s, halves_in):
        low, high = halves_in[0] * oc, (halves_in[-1] + 1) * oc

        def body(at):
            GC[at, pl.ds(low, high - low)] = dot(G[s, at, :], WO[pl.ds(low, high - low), :], NT).astype(BF16)

        each_tile(body)

    def attend(s, rows, h):
        attend_pair(
            MIX.at[s], h * qc, GC, h * oc, CTX.at[s], rows, seg_col, cos_tab, sin_tab, dk_acc, dv_acc, tile
        )

    tables(rows_own)
    here_h.wait()
    net.wait("core h", X.at[0, :, far_cols], core)
    net.wait("core p", params.at[:, far_cols], core)
    along("q", 1)
    each_tile(lambda at: norm(0, at))
    along("q", 3)
    along("o", 1)
    along("o", 3)
    start_along("u")
    start_along("d")
    along("q", 2)
    have_here("q")
    project(0, (0,))
    along("o", 2)
    have_here("o")
    here_g.wait()
    net.wait("core g", G.at[0, :, far_cols], core)
    pull_context(0, (0,))
    hand_over("h", X, 0)
    attend(0, rows_own, 0)
    along("u", 1)
    across_y("q")
    project(0, (1,))
    across_y("o")
    pull_context(0, (1,))
    hand_over("h", X, 1)
    attend(0, rows_own, 1)
    along("u", 3)
    net.wait("x rows", rows_far, xdev)
    tables(rows_far)
    have_far("h", X)
    each_tile(lambda at: norm(1, at))
    along("d", 1)
    hand_over("g", G, 0)
    project(1, (0, 1))
    along("d", 3)
    along("u", 2)
    hand_over("g", G, 1)
    have_far("g", G)
    pull_context(1, (0, 1))
    attend(1, rows_far, 1)
    along("d", 2)

    grads = {
        "q": (SQ, YQ, ZQ, HQ, rq_out, lambda t: (block(t), every), lambda p: (every, p), qc),
        "o": (SO, YO, ZO, HO, ro_out, lambda t: (every, block(t)), lambda p: (p, every), oc),
        "u": (SU, YU, ZU, HU, ru_out, lambda t: (block(t), every), lambda p: (every, p), uc),
        "d": (SD, YD, ZD, HD, rd_out, lambda t: (every, block(t)), lambda p: (p, every), uc),
    }

    def multiply(name, h, t):
        if name == "q":
            pairs_of = [(A[s, :, block(t)], MIX[s, :, pl.ds(h * qc, qc)]) for s in range(2)]
        elif name == "u":
            pairs_of = [(B[s, :, block(t)], GUP[s, :, pl.ds(h * uc, uc)]) for s in range(2)]
        elif name == "o":
            pairs_of = [(CTX[s, :, pl.ds(h * oc, oc)], G[s, :, block(t)]) for s in range(2)]
        else:
            pairs_of = [(ACT[s, :, pl.ds(h * uc, uc)], G[s, :, block(t)]) for s in range(2)]
        return (dot(*pairs_of[0], TN) + dot(*pairs_of[1], TN)).astype(BF16)

    turns = (2, 3, 1, 0)

    def other_part(name):
        source, landed, spot = grads[name][0], grads[name][1], grads[name][5]
        for t in turns:
            source[spot(t)] = multiply(name, 1, t)
            net.send(("gy", name, t), source.at[spot(t)], landed.at[spot(t)], ydev)

    def own_part(name):
        kept, spot = grads[name][2], grads[name][5]

        @pl.loop(0, R, unroll=2)
        def _(t):
            kept[spot(t)] = multiply(name, 0, t)

    def across(name, t):
        _, landed, kept, hops, _, spot, _, _ = grads[name]
        net.wait(("gy", name, t), landed.at[spot(t)], ydev)
        total = kept[spot(t)].astype(F32) + landed[spot(t)].astype(F32)
        if t == 1:
            net.wait(("gz", name, 2), hops.at[0], zdev(-1))
            total = total + hops[0].astype(F32)
        kept[spot(t)] = total.astype(BF16)
        if t == 2:
            net.send(("gz", name, 2), kept.at[spot(t)], hops.at[0], zdev(1))
        elif t == 3:
            net.send(("gz", name, 3), kept.at[spot(t)], hops.at[1], zdev(-1))
        elif t == 1:
            net.send(("gz", name, 1), kept.at[spot(t)], hops.at[2], zdev(1))

    def finish(name):
        _, _, kept, hops, result, spot, place, size = grads[name]
        net.wait(("gz", name, 3), hops.at[1], zdev(1))
        net.wait(("gz", name, 1), hops.at[2], zdev(-1))
        total = kept[spot(0)].astype(F32) + hops[1].astype(F32) + hops[2].astype(F32)
        kept[spot(0)] = total.astype(BF16)
        target = result.at[place(seat(0, size))]
        net.send(("ry", name), kept.at[spot(0)], target, ydev)
        net.send(("rx", name), kept.at[spot(0)], target, xdev)
        return move(kept.at[spot(0)], target)

    def far_seat(h, size):
        return pl.ds(pl.multiple_of(((1 - side) * 2 + (quarter if h == 0 else 1 - quarter)) * size, size), size)

    by_x = "u"

    def spread_out(name):
        _, _, _, _, result, _, place, size = grads[name]
        if name in by_x:
            target = result.at[place(far_seat(0, size))]
            net.wait(("rx", name), target, xdev)
            net.send(("rr", name), target, target, ydev)
        else:
            target = result.at[place(seat(1, size))]
            net.wait(("ry", name), target, ydev)
            net.send(("rr", name), target, target, xdev)

    def collect(name):
        _, _, _, _, result, _, place, size = grads[name]
        if name in by_x:
            net.wait(("ry", name), result.at[place(seat(1, size))], ydev)
        else:
            net.wait(("rx", name), result.at[place(far_seat(0, size))], xdev)
        net.wait(("rr", name), result.at[place(far_seat(1, size))], ydev if name in by_x else xdev)

    SMALL[...] = jnp.zeros_like(SMALL)
    other_part("q")
    other_part("o")
    attend(1, rows_far, 0)
    have_here("u")
    have_here("d")
    across_y("u")
    across_y("d")

    def seat_of(h, size):
        return (quarter if h == 0 else 1 - quarter) * size

    def feed_part(s, h):
        def ahead(at, begin):
            cols = pl.ds(h * uc + begin, tile)
            bias_at = (side * 2) * uc + seat_of(h, uc) + begin
            up = dot(B[s, at, :], WU[:, cols]) + biases[1:2, pl.ds(pl.multiple_of(bias_at, tile), tile)]
            return at, begin, cols, up, dot(G[s, at, :], WD[cols, :], NT)

        def after(at, begin, cols, up, pull):
            gate = 0.5 * (1.0 + lax.erf(up * 0.5**0.5))
            bell = jnp.exp(-0.5 * up * up) * 0.3989422804014327
            ACT[s, at, cols] = (up * gate).astype(BF16)
            grad = (pull * (gate + up * bell)).astype(BF16)
            GUP[s, at, cols] = grad
            SMALL[1:2, pl.ds(pl.multiple_of(seat_of(h, uc) + begin, tile), tile)] += jnp.sum(
                grad.astype(F32), axis=0, keepdims=True
            )

        @pl.loop(0, length // (2 * tile))
        def _(i):
            steps = []
            for j in range(2):
                at = pl.ds(pl.multiple_of(i * 2 * tile + j * tile, tile), tile)
                steps += [(at, begin) for begin in range(0, uc, tile)]
            coming = ahead(*steps[0])
            for k in range(len(steps)):
                now = coming
                if k + 1 < len(steps):
                    coming = ahead(*steps[k + 1])
                after(*now)

    def halves(value):
        left, right = value[:, :half], value[:, half:]
        return jnp.where(col == 0, left, right).astype(BF16), jnp.where(col == 0, right, left).astype(BF16)

    def leave(s, c, out, slope):
        @pl.loop(0, piece // tile, unroll=2)
        def _(i):
            at = pl.ds(pl.multiple_of(c * piece + i * tile, tile), tile)
            to = pl.ds(pl.multiple_of(i * tile, tile), tile) if s == 1 else at
            result = dot(CTX[s, at, :], WO[...]) + dot(ACT[s, at, :], WD[...])
            grad_one = dot(MIX[s, at, :], WQ[...], NT)
            grad_two = dot(GUP[s, at, :], WU[...], NT)
            out[0][at, :], out[1][to, :] = halves(result)
            unit, inv = unit_rows(s, at)
            for i_row, value in enumerate([grad_one * unit, grad_one, grad_two * unit, grad_two]):
                SMALL[2 + i_row : 3 + i_row, :] += jnp.sum(value, axis=0, keepdims=True)
            scaled = grad_one * params[0:1, :] + grad_two * params[2:3, :]
            mean_scaled = jnp.mean(scaled, axis=1, keepdims=True)
            mean_unit = jnp.mean(scaled * unit, axis=1, keepdims=True)
            slope[0][at, :], slope[1][to, :] = halves(inv * (scaled - mean_scaled - unit * mean_unit))
            if s == 0:
                SMALL[6:7, own_cols] += jnp.sum(G[0, at, own_cols].astype(F32), axis=0, keepdims=True)

    given = [ZD, SD]
    given_copies = []
    near = [X.at[1, :, pl.ds(0, half)], X.at[1, :, pl.ds(half, half)]]

    def leave_far(c):
        spots = [buffer.at[:, pl.ds(c * half, half)] for buffer in given]
        leave(1, c, (OUT.at[0], spots[0]), (OUT.at[1], spots[1]))
        for i in range(2):
            given_copies.append(net.send(("out", i, c), spots[i], LAND.at[i, chunk(c), :], core))

    def pass_far(c):
        for i in range(2):
            net.wait(("out", i, c), LAND.at[i, chunk(c), :], core)
            LAND[i, chunk(c), :] = (LAND[i, chunk(c), :].astype(F32) + OUT[i, chunk(c), :].astype(F32)).astype(BF16)
            net.send(("far out", i, c), LAND.at[i, chunk(c), :], FAR.at[i, chunk(c), :], xdev)

    def leave_own(c):
        sides = [[buffer.at[0, :, pl.ds(h * half, half)] for h in range(2)] for buffer in (ACT, GUP)]
        leave(0, c, *sides)
        for i in range(2):
            net.send(("own out", i, c), sides[i][1].at[chunk(c), :], near[i].at[chunk(c), :], core)

    def add_up(i, c):
        buffer = (ACT, GUP)[i]
        net.wait(("own out", i, c), near[i].at[chunk(c), :], core)
        net.wait(("far out", i, c), FAR.at[i, chunk(c), :], xdev)
        total = buffer[0, chunk(c), pl.ds(0, half)].astype(F32) + near[i][chunk(c), :].astype(F32)
        FAR[i, chunk(c), :] = (total + FAR[i, chunk(c), :].astype(F32)).astype(BF16)
        return move(FAR.at[i, chunk(c), :], (sum_out, slope_out)[i].at[chunk(c), :])

    def mixed_sums():
        for h in range(2):
            sums = [jnp.sum(MIX[s, :, pl.ds(h * qc, qc)].astype(F32), axis=0, keepdims=True) for s in range(2)]
            SMALL[0:1, pl.ds(pl.multiple_of(seat_of(h, qc), LANES), qc)] = sums[0] + sums[1]

    def small_z():
        for t in range(1, R):
            net.send(("sz", t), SMALL, SMALL_Z.at[row], zdev(t))
        SMALL_Z[row] = SMALL[...]

    def small_y():
        for t in range(1, R):
            net.wait(("sz", t), SMALL_Z.at[lax.rem(row - t + R, R)], zdev(-t))
        total = SMALL_Z[0]
        for r in range(1, R):
            total = total + SMALL_Z[r]
        SMALL_P[0] = total
        net.send("sy", SMALL_P.at[0], SMALL_P.at[1], ydev)

    def small_x():
        net.wait("sy", SMALL_P.at[1], ydev)
        SMALL_P[2] = SMALL_P[0] + SMALL_P[1]
        net.send("sx", SMALL_P.at[2], SMALL_P.at[3], xdev)

    def small_core():
        net.wait("sx", SMALL_P.at[3], xdev)
        SMALL_P[4] = SMALL_P[2] + SMALL_P[3]
        net.send("sc", SMALL_P.at[4], SMALL_P.at[5], core)

    def small_end():
        net.wait("sc", SMALL_P.at[5], core)
        SMALL_P[5] = SMALL_P[4] + SMALL_P[5]

    done = []
    feed_part(1, 0)
    feed_part(1, 1)
    for copy in handed:
        net.sent(copy)
    leave_far(1)
    feed_part(0, 1)
    pass_far(1)
    own_part("o")
    other_part("u")
    across("o", 2)
    own_part("q")
    across("o", 3)
    across("q", 2)
    across("q", 3)
    feed_part(0, 0)
    across("o", 1)
    leave_far(0)
    across("q", 1)
    for copy in given_copies:
        net.sent(copy)
    own_part("d")
    own_part("u")
    across("u", 3)
    pass_far(0)
    other_part("d")
    leave_own(1)
    across("q", 0)
    across("u", 2)
    across("d", 2)
    across("o", 0)
    mixed_sums()
    leave_own(0)
    small_z()
    across("u", 1)
    done.append(finish("o"))
    done += [add_up(0, 1), add_up(1, 1)]
    across("u", 0)
    across("d", 3)
    small_y()
    across("d", 1)
    done.append(finish("q"))
    done.append(finish("u"))
    small_x()
    done += [add_up(0, 0), add_up(1, 0)]
    across("d", 0)
    spread_out("q")
    done.append(finish("d"))
    small_core()
    spread_out("u")
    spread_out("o")
    small_end()
    spread_out("d")

    def side_span(which, size):
        return pl.ds(pl.multiple_of(which * size, LANES), size)

    for i, which in [(2, side), (3, 1 - side)]:
        done += [
            move(SMALL_P.at[i, pl.ds(0, 1), pl.ds(0, 2 * qc)], bq_out.at[:, side_span(which, 2 * qc)]),
            move(SMALL_P.at[i, pl.ds(1, 1), pl.ds(0, 2 * uc)], bu_out.at[:, side_span(which, 2 * uc)]),
        ]
    done += [
        move(SMALL_P.at[5, pl.ds(2, 4), own_cols], gains_out),
        move(SMALL_P.at[4, pl.ds(6, 1), own_cols], cot_out),
    ]
    for name in "oqdu":
        collect(name)
    for copy in done:
        copy.wait()
    net.drain()


def whole_block(hidden, cot, wq, wo, wu, wd, *rest):
    length, half = hidden.shape
    width = 2 * half
    shard = wq.shape[0]
    wide3 = wq.shape[1] // 2
    wide = wide3 // 3
    units = wu.shape[1] // 2
    qc, oc, uc = wide3 // 2, wide // 2, units // 2
    out_shape = [
        jax.ShapeDtypeStruct(shape, kind)
        for shape, kind in [
            ((shard, 4 * qc), BF16), ((4 * oc, shard), BF16), ((shard, 4 * uc), BF16), ((4 * uc, shard), BF16),
            ((length, half), BF16), ((length, half), BF16),
            ((4, half), F32), ((1, 4 * qc), F32), ((1, 4 * uc), F32), ((1, half), F32),
        ]
    ]
    both = lambda n: pltpu.VMEM((2, length, n), BF16)
    plain = lambda *shape: pltpu.VMEM(shape, BF16)
    floats = lambda *shape: pltpu.VMEM(shape, F32)
    quarter_grads = [plain(width, qc), plain(oc, width), plain(width, uc), plain(uc, width)]
    scratch = [
        both(width), both(width), both(width), both(width), both(half),
        plain(width, wide3), plain(wide, width), plain(width, units), plain(units, width),
        both(wide3), both(wide), both(units), both(units),
        floats(8, length), floats(8, length), floats(8, width), floats(8, 4 * uc),
        *[floats(length, LANES)] * 5,
        *quarter_grads * 3,
        plain(3, shard, qc), plain(3, oc, shard), plain(3, shard, uc), plain(3, uc, shard),
        both(half), both(half), floats(8, width), floats(4, 8, width), floats(6, 8, width),
    ]
    any_spec = pl.BlockSpec(memory_space=pl.ANY)
    vmem_spec = pl.BlockSpec(memory_space=pltpu.VMEM)
    return pl.pallas_call(
        block_kernel,
        out_shape=out_shape,
        in_specs=[any_spec] * 6 + [vmem_spec] * len(rest),
        out_specs=[any_spec] * len(out_shape),
        scratch_shapes=scratch + [
            pltpu.SemaphoreType.DMA((128,)), pltpu.SemaphoreType.DMA((128,)), pltpu.SemaphoreType.DMA((32,)),
        ],
        compiler_params=pltpu.CompilerParams(collective_id=0, has_side_effects=True, vmem_limit_bytes=63 << 20),
        name="block",
    )(hidden, cot, wq, wo, wu, wd, *rest)


def widen_kernel(
    hidden, branch, cot, slope, grad_q, grad_o, grad_u, grad_d, bias_one, bias_two, gains, qkv_sum, up_sum, cot_sum,
    output, input_grad, out_q, out_o, out_u, out_d, *small,
):
    bias = (bias_one[...].astype(F32) + bias_two[...].astype(F32)).reshape(1, -1)
    output[...] = hidden[...].astype(F32) + branch[...].astype(F32) + bias
    input_grad[...] = cot[...].astype(F32) + slope[...].astype(F32)
    for source, target in [(grad_q, out_q), (grad_o, out_o), (grad_u, out_u), (grad_d, out_d)]:
        target[...] = source[...].astype(F32)
    for i in range(4):
        small[i][...] = gains[i, :]
    small[4][...] = qkv_sum[0, :]
    small[5][...] = up_sum[0, :]
    small[6][...] = cot_sum[0, :]
    small[7][...] = cot_sum[0, :]


def widen_all(hidden, branch, cot, slope, grad_q, grad_o, grad_u, grad_d, bias_one, bias_two, gains, *sums):
    steps = 4
    rows = lambda v: pl.BlockSpec((v.shape[0] // steps, v.shape[1]), lambda i: (i, 0))
    whole = lambda v: pl.BlockSpec(v.shape, lambda i: (0,) * v.ndim)
    large = [hidden, branch, cot, slope, grad_q, grad_o, grad_u, grad_d]
    tiny = [bias_one, bias_two, gains, *sums]
    wide = [hidden, cot, grad_q, grad_o, grad_u, grad_d]
    flat = [gains.shape[1]] * 4 + [v.shape[1] for v in sums] + [sums[-1].shape[1]]
    return pl.pallas_call(
        widen_kernel,
        grid=(steps,),
        in_specs=[rows(v) for v in large] + [whole(v) for v in tiny],
        out_specs=[rows(v) for v in wide] + [pl.BlockSpec((n,), lambda i: (0,)) for n in flat],
        out_shape=[jax.ShapeDtypeStruct(v.shape, F32) for v in wide] + [jax.ShapeDtypeStruct((n,), F32) for n in flat],
        compiler_params=pltpu.CompilerParams(vmem_limit_bytes=63 << 20),
        name="widen",
    )(*large, *tiny)


def local_block(
    hidden,
    segments,
    ln1_gain,
    ln1_bias,
    qkv_weight,
    qkv_bias,
    out_weight,
    out_bias,
    ln2_gain,
    ln2_bias,
    up_weight,
    up_bias,
    down_weight,
    down_bias,
    cotangent,
):
    lane = np.arange(LANES) % HEAD_DIM
    frequency = np.where(lane < ROT, 10000.0 ** (-2.0 * (lane % (ROT // 2)) / ROT), 0.0)
    sign = np.where(lane < ROT, np.where(lane < ROT // 2, -1.0, 1.0), 0.0)
    freq = np.stack([frequency, sign] * 4).astype(np.float32)
    flat = [ln1_gain, ln1_bias, ln2_gain, ln2_bias, qkv_bias, up_bias]
    grad_q, grad_o, grad_u, grad_d, branch, slope, gains, qkv_sum, up_sum, cot_sum = whole_block(
        hidden, cotangent, qkv_weight, out_weight, up_weight, down_weight, segments, jnp.asarray(freq), *flat
    )
    output, input_grad, grad_q, grad_o, grad_u, grad_d, *small = widen_all(
        hidden, branch, cotangent, slope, grad_q, grad_o, grad_u, grad_d,
        out_bias, down_bias, gains, qkv_sum, up_sum, cot_sum,
    )
    gain_one, shift_one, gain_two, shift_two, qkv_sum, up_sum, cot_sum, cot_again = small
    return (
        output, input_grad, gain_one, shift_one, grad_q, qkv_sum, grad_o, cot_sum,
        gain_two, shift_two, grad_u, up_sum, grad_d, cot_again,
    )


def normalize(values):
    centred = values - jnp.mean(values, axis=-1, keepdims=True)
    variance = jnp.mean(centred * centred, axis=-1, keepdims=True)
    inv_std = lax.rsqrt(variance + EPS)
    return centred * inv_std, inv_std


def make_general(groups, rows, cols):
    quarters = groups // 2

    def pair_swap(value):
        return lax.ppermute(value, "dp", [(d, d ^ 1) for d in range(groups)])

    def quarter_shift(value, shift):
        moves = [(2 * a + b, 2 * ((a + shift) % quarters) + b) for a in range(quarters) for b in range(2)]
        return lax.ppermute(value, "dp", moves)

    def row_shift(value, shift):
        return lax.ppermute(value, "row", [(r, (r + shift) % rows) for r in range(rows)])

    def core_swap(value):
        return lax.ppermute(value, "col", [(0, 1), (1, 0)])

    def local(
        hidden,
        segments,
        ln1_gain,
        ln1_bias,
        qkv_weight,
        qkv_bias,
        out_weight,
        out_bias,
        ln2_gain,
        ln2_bias,
        up_weight,
        up_bias,
        down_weight,
        down_bias,
        cotangent,
    ):
        assert segments.shape[0] == 1 and cols == 2
        length = segments.shape[1]
        half_width = hidden.shape[1]
        width = 2 * half_width
        shard = qkv_weight.shape[0]
        heads = qkv_weight.shape[1] // (3 * HEAD_DIM) // 2
        wide = heads * HEAD_DIM
        units = up_weight.shape[1] // 2
        whole_heads = heads % quarters == 0
        dp = lax.axis_index("dp")
        row = lax.axis_index("row")
        col = lax.axis_index("col")
        side = lax.rem(dp, 2)
        quarter = dp // 2

        def both(mine, other):
            flip = col == 0
            return jnp.concatenate([jnp.where(flip, mine, other), jnp.where(flip, other, mine)], axis=-1)

        def half_of(value, axis):
            size = value.shape[axis] // 2
            return lax.dynamic_slice_in_dim(value, side * size, size, axis)

        def piece_of(value, shift, axis, placed=False):
            size = value.shape[axis] // quarters
            if placed:
                return lax.slice_in_dim(value, shift * size, (shift + 1) * size, axis=axis)
            return lax.dynamic_slice_in_dim(value, lax.rem(quarter - shift + quarters, quarters) * size, size, axis)

        def in_place(pieces, axis):
            if quarters == 1:
                return pieces[0]
            if quarters == 2:
                flip = quarter == 0
                first = jnp.where(flip, pieces[0], pieces[1])
                second = jnp.where(flip, pieces[1], pieces[0])
                return jnp.concatenate([first, second], axis=axis)
            order = lax.rem(quarter - jnp.arange(quarters) + quarters, quarters)
            stacked = jnp.take(jnp.stack(pieces), order, axis=0)
            return jnp.concatenate([stacked[i] for i in range(quarters)], axis=axis)

        def near(pieces, axis, keep):
            return jnp.concatenate(pieces, axis=axis) if keep else in_place(pieces, axis)

        def gather(value, width_axis, unit_axis, keep):
            mine = piece_of(value, 0, unit_axis)
            received = {0: mine}
            ahead = behind = mine
            for step in range(1, rows):
                if step <= rows // 2:
                    ahead = row_shift(ahead, -1)
                    received[step] = ahead
                if step <= (rows - 1) // 2:
                    behind = row_shift(behind, 1)
                    received[rows - step] = behind
            result = jnp.zeros(
                [width if i == width_axis else n for i, n in enumerate(value.shape)], value.dtype
            )
            for step in range(rows):
                if step == 0:
                    pieces = [piece_of(value, q, unit_axis) for q in range(quarters)]
                else:
                    pieces = [received[step]]
                    pieces += [quarter_shift(received[step], q) for q in range(1, quarters)]
                block = near(pieces, unit_axis, keep)
                place = lax.rem(row + step, rows) * shard
                result = lax.dynamic_update_slice_in_dim(result, block, place, width_axis)
            return result

        hidden_other = core_swap(hidden)
        hidden_far = pair_swap(hidden)
        cot_other = core_swap(cotangent)
        cot_far = pair_swap(cotangent)
        params = jnp.stack([ln1_gain, ln1_bias, ln2_gain, ln2_bias])
        params = both(params, core_swap(params)).astype(F32)
        gain_one, shift_one, gain_two, shift_two = [params[i][None, :] for i in range(4)]
        inputs = [both(hidden, hidden_other), both(hidden_far, core_swap(hidden_far))]
        cots = [both(cotangent, cot_other), both(cot_far, core_swap(cot_far))]
        segs = [segments, pair_swap(segments)]

        qkv_cols = qkv_weight.reshape(shard, 2, heads, 3, HEAD_DIM)
        qkv_cols = lax.dynamic_index_in_dim(qkv_cols, side, 1, keepdims=False)
        qkv_cols = jnp.swapaxes(qkv_cols, 1, 2).reshape(shard, 3, wide)
        qkv_all = gather(qkv_cols, 0, 2, whole_heads).reshape(width, 3 * wide)
        out_all = gather(half_of(out_weight, 0), 1, 0, whole_heads)
        up_all = gather(half_of(up_weight, 1), 0, 1, True)
        down_all = gather(half_of(down_weight, 0), 1, 0, True)

        bias_cols = lax.dynamic_index_in_dim(qkv_bias.reshape(2, heads, 3, HEAD_DIM), side, 0, keepdims=False)
        bias_cols = jnp.swapaxes(bias_cols, 0, 1).reshape(1, 3, wide)
        bias_cols = near([piece_of(bias_cols, q, 2) for q in range(quarters)], 2, whole_heads)
        bias_cols = bias_cols.reshape(1, 3 * wide).astype(F32)
        up_half = half_of(up_bias, 0)
        up_row = jnp.concatenate([piece_of(up_half, q, 0) for q in range(quarters)])[None, :].astype(F32)

        norms = []
        contexts = []
        grads_mixed = []
        for values, cot, seg in zip(inputs, cots, segs):
            unit, inv = normalize(values.astype(F32))
            act_one = (unit * gain_one + shift_one).astype(BF16)
            act_two = (unit * gain_two + shift_two).astype(BF16)
            norms.append((unit, inv, act_one, act_two))
            cos_rows, sine_rows = rotary_tables(doc_positions(seg).reshape(length))
            mixed = dot(act_one, qkv_all) + bias_cols
            cos_wide = jnp.tile(cos_rows, (1, 2 * wide // LANES))
            sine_wide = jnp.tile(sine_rows, (1, 2 * wide // LANES))
            turned = mixed[:, : 2 * wide]
            lane = jnp.arange(2 * wide) % HEAD_DIM
            swapped = jnp.where(
                lane < ROT // 2, jnp.roll(turned, -(ROT // 2), axis=1), jnp.roll(turned, ROT // 2, axis=1)
            )
            turned = turned * cos_wide + swapped * sine_wide
            qkv = jnp.concatenate([turned, mixed[:, 2 * wide :]], axis=1).astype(BF16)
            grad_context = dot(cot, out_all, NT).astype(BF16)
            context, grad_mixed = attention(qkv, grad_context, seg, cos_rows, sine_rows)
            contexts.append(context)
            grads_mixed.append(grad_mixed)

        feeds = [feed(norm[3], cot, up_all, up_row, down_all) for norm, cot in zip(norms, cots)]

        def reduce_grad(left, right, width_axis, unit_axis, placed, shape=None):
            total = dot(left[0], right[0], TN) + dot(left[1], right[1], TN)
            if shape is not None:
                total = total.reshape(shape)
            mine = piece_of(total, 0, unit_axis, placed)
            for q in range(1, quarters):
                part = piece_of(total, q, unit_axis, placed).astype(BF16)
                mine = mine + quarter_shift(part, -q).astype(F32)
            cut = lambda t: lax.dynamic_slice_in_dim(mine, lax.rem(row + t, rows) * shard, shard, width_axis)
            result = cut(0)
            for t in range(1, rows):
                result = result + row_shift(cut(t).astype(BF16), t).astype(F32)
            result = result.astype(BF16)
            pieces = [result] + [quarter_shift(result, q) for q in range(1, quarters)]
            result = in_place(pieces, unit_axis)
            far = pair_swap(result)
            flip = side == 0
            return jnp.concatenate(
                [jnp.where(flip, result, far), jnp.where(flip, far, result)], axis=unit_axis
            ).astype(F32)

        acts_one = [n[2] for n in norms]
        acts_two = [n[3] for n in norms]
        out_grad = reduce_grad(contexts, cots, 1, 0, whole_heads)
        qkv_grad = reduce_grad(acts_one, grads_mixed, 0, 2, whole_heads, (width, 3, wide))
        down_grad = reduce_grad([f[0] for f in feeds], cots, 1, 0, True)
        up_grad = reduce_grad(acts_two, [f[1] for f in feeds], 0, 1, True)
        qkv_grad = qkv_grad.reshape(shard, 3, 2 * heads, HEAD_DIM)
        qkv_grad = jnp.swapaxes(qkv_grad, 1, 2).reshape(shard, 6 * wide)

        outs = []
        slopes = []
        norm_sums = jnp.zeros((4, width), F32)
        for index in range(2):
            unit, inv, _, _ = norms[index]
            act, grad_up, _ = feeds[index]
            outs.append((dot(contexts[index], out_all) + dot(act, down_all)).astype(BF16))
            grad_one = dot(grads_mixed[index], qkv_all, NT)
            grad_two = dot(grad_up, up_all, NT)
            norm_sums += jnp.stack(
                [
                    jnp.sum(grad_one * unit, axis=0),
                    jnp.sum(grad_one, axis=0),
                    jnp.sum(grad_two * unit, axis=0),
                    jnp.sum(grad_two, axis=0),
                ]
            )
            scaled = grad_one * gain_one + grad_two * gain_two
            mean_scaled = jnp.mean(scaled, axis=1, keepdims=True)
            mean_unit = jnp.mean(scaled * unit, axis=1, keepdims=True)
            slopes.append((inv * (scaled - mean_scaled - unit * mean_unit)).astype(BF16))

        def fold(pair):
            sums = []
            for value in pair:
                kept = lax.dynamic_slice_in_dim(value, col * half_width, half_width, 1).astype(F32)
                given = lax.dynamic_slice_in_dim(value, (1 - col) * half_width, half_width, 1)
                sums.append(kept + core_swap(given).astype(F32))
            return sums[0] + pair_swap(sums[1].astype(BF16)).astype(F32)

        cot_local = cotangent.astype(F32)
        output = hidden.astype(F32) + fold(outs) + (out_bias.astype(F32) + down_bias.astype(F32))
        input_grad = cot_local + fold(slopes)

        qkv_sum = (
            jnp.sum(grads_mixed[0].astype(F32), axis=0) + jnp.sum(grads_mixed[1].astype(F32), axis=0)
        ).reshape(3, wide)
        if whole_heads:
            qkv_sum = in_place([piece_of(qkv_sum, q, 1, True) for q in range(quarters)], 1)
        up_sum = (feeds[0][2] + feeds[1][2])[0]
        up_sum = in_place([piece_of(up_sum, q, 0, True) for q in range(quarters)], 0)

        def widen(value):
            zeros = jnp.zeros_like(value)
            flip = side == 0
            return jnp.concatenate([jnp.where(flip, value, zeros), jnp.where(flip, zeros, value)], axis=-1)

        kept = lax.dynamic_slice_in_dim(norm_sums, col * half_width, half_width, 1)
        given = lax.dynamic_slice_in_dim(norm_sums, (1 - col) * half_width, half_width, 1)
        norm_sums = kept + core_swap(given)
        small = jnp.concatenate(
            [widen(qkv_sum).reshape(-1), widen(up_sum), jnp.sum(cot_local, axis=0), norm_sums.reshape(-1)]
        )
        small = lax.psum(small, ("dp", "row"))
        sizes = [6 * wide, 2 * units, half_width, half_width, half_width, half_width, half_width]
        parts = []
        start = 0
        for size in sizes:
            parts.append(lax.slice_in_dim(small, start, start + size))
            start += size
        qkv_sum, up_sum, cot_sum, gain_one_sum, shift_one_sum, gain_two_sum, shift_two_sum = parts
        qkv_sum = jnp.swapaxes(qkv_sum.reshape(3, 2 * heads, HEAD_DIM), 0, 1).reshape(-1)
        return (
            output,
            input_grad,
            gain_one_sum,
            shift_one_sum,
            qkv_grad,
            qkv_sum,
            out_grad,
            cot_sum,
            gain_two_sum,
            shift_two_sum,
            up_grad,
            up_sum,
            down_grad,
            cot_sum,
        )

    return local


def solution(mesh):
    placed = (
        P(("dp", "row"), "col"),
        P(("dp", "row"), None),
        P("col"),
        P("col"),
        P("row", "col"),
        P("col"),
        P("col", "row"),
        P("col"),
        P("col"),
        P("col"),
        P("row", "col"),
        P("col"),
        P("col", "row"),
        P("col"),
        P(("dp", "row"), "col"),
    )
    groups, rows, cols = mesh.shape["dp"], mesh.shape["row"], mesh.shape["col"]
    paired = (groups, rows, cols) == (4, 4, 2)
    return jax.shard_map(
        local_block if paired else make_general(groups, rows, cols),
        mesh=mesh,
        in_specs=placed,
        out_specs=(
            P(("dp", "row"), "col"),
            P(("dp", "row"), "col"),
            P("col"),
            P("col"),
            P("row", "col"),
            P("col"),
            P("col", "row"),
            P("col"),
            P("col"),
            P("col"),
            P("row", "col"),
            P("col"),
            P("col", "row"),
            P("col"),
        ),
        check_vma=False,
    )
```

```python
import functools

import jax
import jax.numpy as jnp
import numpy as np
from jax import lax
from jax.experimental import pallas as pl
from jax.experimental.pallas import tpu as pltpu
from jax.sharding import PartitionSpec as P

HEAD_DIM = 64
ROT = 16
EPS = 1e-05
MAX_DOC = 512
DOCS = 4
LANES = 128
BF16 = jnp.bfloat16
F32 = jnp.float32

NT = (((1,), (1,)), ((), ()))
TN = (((0,), (0,)), ((), ()))
NN = (((1,), (0,)), ((), ()))


def dot(a, b, dims=NN):
    return lax.dot_general(a, b, dims, preferred_element_type=F32)


def doc_positions(segments):
    length = segments.shape[-1]
    places = jnp.arange(length, dtype=jnp.int32)
    changed = jnp.concatenate(
        [jnp.ones(segments.shape[:-1] + (1,), dtype=bool), segments[..., 1:] != segments[..., :-1]],
        axis=-1,
    )
    starts = lax.cummax(jnp.where(changed, places, jnp.zeros_like(places)), axis=segments.ndim - 1)
    return places - starts


def rotary_tables(positions):
    lane = jnp.arange(LANES) % HEAD_DIM
    frequency = 10000.0 ** (-2.0 * (lane % (ROT // 2)).astype(F32) / ROT)
    turning = lane < ROT
    angles = positions.astype(F32)[:, None] * jnp.where(turning, frequency, 0.0)[None, :]
    sign = jnp.where(turning, jnp.where(lane < ROT // 2, -1.0, 1.0), 0.0)
    return jnp.cos(angles), jnp.sin(angles) * sign[None, :]


def turn(values, cos_rows, sine_rows, low_lanes):
    half = ROT // 2
    up = pltpu.roll(values, values.shape[1] - half, 1)
    down = pltpu.roll(values, half, 1)
    return values * cos_rows + jnp.where(low_lanes, up, down) * sine_rows


def attention_kernel(
    q_ref, k_ref, v_ref, gc_ref, seg_row_ref, seg_col_ref, cos_ref, sin_ref, ctx_ref, gm_ref, dk_acc, dv_acc, *, block
):
    pair = pl.program_id(0)
    pairs = pl.num_programs(0)
    length = q_ref.shape[0]
    lane = lax.broadcasted_iota(jnp.int32, (1, LANES), 1)
    low_lanes = lane % HEAD_DIM < ROT // 2
    first = lane < HEAD_DIM
    zero = jnp.zeros((), BF16)

    def split(values):
        return [jnp.where(first, values, zero), jnp.where(first, zero, values)]

    dk_acc[...] = jnp.zeros_like(dk_acc)
    dv_acc[...] = jnp.zeros_like(dv_acc)
    for begin in range(0, length, block):
        low = max(0, begin - (MAX_DOC - 1)) // LANES * LANES
        rows = pl.ds(begin, block)
        keys = pl.ds(low, begin + block - low)
        width = begin + block - low
        q_parts = split(q_ref[rows, :] * jnp.asarray(HEAD_DIM**-0.5, BF16))
        g_parts = split(gc_ref[rows, :])
        k_block = k_ref[keys, :]
        v_block = v_ref[keys, :]
        places = begin + lax.broadcasted_iota(jnp.int32, (block, width), 0)
        key_places = low + lax.broadcasted_iota(jnp.int32, (block, width), 1)
        allowed = (seg_col_ref[rows, :] == seg_row_ref[:, keys]) & (places >= key_places)
        probs = []
        grads = []
        for part in range(2):
            scores = dot(q_parts[part], k_block, NT)
            scores = jnp.where(allowed, scores, -1e30)
            top = jnp.max(scores, axis=1, keepdims=True)
            powers = jnp.exp(scores - top)
            total = jnp.sum(powers, axis=1, keepdims=True)
            chances = powers * (1.0 / total)
            slopes = dot(g_parts[part], v_block, NT)
            inner = jnp.sum(slopes * chances, axis=1, keepdims=True)
            probs.append(chances.astype(BF16))
            grads.append((chances * (slopes - inner)).astype(BF16))
        context = jnp.where(first, dot(probs[0], v_block), dot(probs[1], v_block))
        ctx_ref[rows, :] = context.astype(BF16)
        dq = jnp.where(first, dot(grads[0], k_block), dot(grads[1], k_block)) * HEAD_DIM**-0.5
        dq = turn(dq, cos_ref[rows, :], -sin_ref[rows, :], low_lanes)
        gm_ref[rows, pl.ds(pl.multiple_of(pair * LANES, LANES), LANES)] = dq.astype(BF16)
        dk_acc[keys, :] += dot(grads[0], q_parts[0], TN) + dot(grads[1], q_parts[1], TN)
        dv_acc[keys, :] += dot(probs[0], g_parts[0], TN) + dot(probs[1], g_parts[1], TN)
    dk = turn(dk_acc[...], cos_ref[...], -sin_ref[...], low_lanes)
    gm_ref[:, pl.ds(pl.multiple_of((pairs + pair) * LANES, LANES), LANES)] = dk.astype(BF16)
    gm_ref[:, pl.ds(pl.multiple_of((2 * pairs + pair) * LANES, LANES), LANES)] = dv_acc[...].astype(BF16)


def attention(qkv, grad_context, seg_row, cos_rows, sine_rows):
    length, wide = qkv.shape
    pairs = wide // (3 * LANES)
    block = min(256, length)
    column = lambda shift: pl.BlockSpec((length, LANES), lambda p: (0, shift + p))
    whole = lambda *shape: pl.BlockSpec(shape, lambda p: (0, 0))
    flops = pairs * 2 * 6 * 2 * length * length * LANES // 2
    return pl.pallas_call(
        functools.partial(attention_kernel, block=block),
        grid=(pairs,),
        in_specs=[
            column(0),
            column(pairs),
            column(2 * pairs),
            column(0),
            whole(1, length),
            whole(length, 1),
            whole(length, LANES),
            whole(length, LANES),
        ],
        out_specs=[column(0), whole(length, wide)],
        out_shape=[
            jax.ShapeDtypeStruct((length, pairs * LANES), BF16),
            jax.ShapeDtypeStruct((length, wide), BF16),
        ],
        scratch_shapes=[pltpu.VMEM((length, LANES), F32), pltpu.VMEM((length, LANES), F32)],
        compiler_params=pltpu.CompilerParams(vmem_limit_bytes=48 << 20),
        cost_estimate=pl.CostEstimate(
            flops=flops, bytes_accessed=6 * length * wide, transcendentals=pairs * length * length
        ),
        name="attention",
    )(qkv, qkv, qkv, grad_context, seg_row, seg_row.reshape(length, 1), cos_rows, sine_rows)


def feed_kernel(a_ref, g_ref, up_ref, bias_ref, down_ref, act_ref, gup_ref, sum_ref, *, chunk):
    units = up_ref.shape[1]

    @pl.when(pl.program_id(0) == 0)
    def _():
        sum_ref[...] = jnp.zeros_like(sum_ref)

    for begin in range(0, units, chunk):
        cols = pl.ds(begin, chunk)
        up = dot(a_ref[...], up_ref[:, cols]) + bias_ref[:, cols]
        pull = dot(g_ref[...], down_ref[cols, :], NT)
        gate = 0.5 * (1.0 + lax.erf(up * 0.5**0.5))
        bell = jnp.exp(-0.5 * up * up) * 0.3989422804014327
        act_ref[:, cols] = (up * gate).astype(BF16)
        grad = (pull * (gate + up * bell)).astype(BF16)
        gup_ref[:, cols] = grad
        sum_ref[:, cols] += jnp.sum(grad.astype(F32), axis=0, keepdims=True)


def feed(normed, cot, up_weight, up_bias, down_weight):
    tokens, width = normed.shape
    units = up_weight.shape[1]
    block = min(256, tokens)
    rows = lambda size: pl.BlockSpec((block, size), lambda i: (i, 0))
    whole = lambda *shape: pl.BlockSpec(shape, lambda i: (0, 0))
    return pl.pallas_call(
        functools.partial(feed_kernel, chunk=min(256, units)),
        grid=(tokens // block,),
        in_specs=[rows(width), rows(width), whole(width, units), whole(1, units), whole(units, width)],
        out_specs=[rows(units), rows(units), whole(1, units)],
        out_shape=[
            jax.ShapeDtypeStruct((tokens, units), BF16),
            jax.ShapeDtypeStruct((tokens, units), BF16),
            jax.ShapeDtypeStruct((1, units), F32),
        ],
        compiler_params=pltpu.CompilerParams(vmem_limit_bytes=48 << 20),
        cost_estimate=pl.CostEstimate(
            flops=4 * tokens * width * units,
            bytes_accessed=4 * tokens * width + 4 * width * units + 4 * tokens * units,
            transcendentals=2 * tokens * units,
        ),
        name="feed",
    )(normed, cot, up_weight, up_bias, down_weight)


MESH = pl.DeviceIdType.MESH


class Net:
    def __init__(self, send_sems, recv_sems):
        self.send_sems, self.recv_sems = send_sems, recv_sems
        self.slots = {}
        self.pending = []

    def slot(self, key):
        return self.slots.setdefault(key, len(self.slots))

    def make(self, key, source, target, device):
        i = self.slot(key)
        return pltpu.make_async_remote_copy(
            src_ref=source,
            dst_ref=target,
            send_sem=self.send_sems.at[i],
            recv_sem=self.recv_sems.at[i],
            device_id=device,
            device_id_type=MESH,
        )

    def send(self, key, source, target, device):
        copy = self.make(key, source, target, device)
        copy.start()
        self.pending.append(copy)
        return copy

    def sent(self, copy):
        copy.wait_send()
        self.pending = [other for other in self.pending if other is not copy]

    def wait(self, key, landed, device):
        self.make(key, landed, landed, device).wait_recv()

    def drain(self):
        for copy in self.pending:
            copy.wait_send()
        self.pending = []


def spread(columns, width):
    return jnp.concatenate([columns] * (width // LANES), axis=1)


def attend_pair(mix, base, gc, gc_base, ctx, seg_row, seg_col, cos_tab, sin_tab, dk_acc, dv_acc, block):
    length = mix.shape[0]
    lane = lax.broadcasted_iota(jnp.int32, (1, LANES), 1)
    low_lanes = lane % HEAD_DIM < ROT // 2
    first = lane < HEAD_DIM
    zero = jnp.zeros((), BF16)
    cols = [pl.ds(base + i * LANES, LANES) for i in range(3)]
    head_cols = pl.ds(gc_base, LANES)

    def split(values):
        return [jnp.where(first, values, zero), jnp.where(first, zero, values)]

    dk_acc[...] = jnp.zeros_like(dk_acc)
    dv_acc[...] = jnp.zeros_like(dv_acc)
    def ahead(begin):
        low = max(0, begin - (MAX_DOC - 1)) // LANES * LANES
        rows = pl.ds(begin, block)
        keys = pl.ds(low, begin + block - low)
        q_parts = split(mix[rows, cols[0]] * jnp.asarray(HEAD_DIM**-0.5, BF16))
        g_parts = split(gc[rows, head_cols])
        k_block = mix[keys, cols[1]]
        v_block = mix[keys, cols[2]]
        raw = [dot(q_parts[part], k_block, NT) for part in range(2)]
        pulls = [dot(g_parts[part], v_block, NT) for part in range(2)]
        return low, rows, keys, q_parts, g_parts, raw, pulls

    coming = ahead(0)
    for begin in range(0, length, block):
        low, rows, keys, q_parts, g_parts, raw, pulls = coming
        if begin + block < length:
            coming = ahead(begin + block)
        width = begin + block - low
        k_block = mix[keys, cols[1]]
        v_block = mix[keys, cols[2]]
        places = begin + lax.broadcasted_iota(jnp.int32, (block, width), 0)
        key_places = low + lax.broadcasted_iota(jnp.int32, (block, width), 1)
        allowed = (spread(seg_col[rows, :], width) == seg_row[0:1, keys]) & (places >= key_places)
        probs = []
        grads = []
        for part in range(2):
            scores = jnp.where(allowed, raw[part], -1e30)
            top = jnp.max(scores, axis=1, keepdims=True)
            powers = jnp.exp(scores - top)
            total = jnp.sum(powers, axis=1, keepdims=True)
            chances = powers * (1.0 / total)
            inner = jnp.sum(pulls[part] * chances, axis=1, keepdims=True)
            probs.append(chances.astype(BF16))
            grads.append((chances * (pulls[part] - inner)).astype(BF16))
        ctx[rows, head_cols] = jnp.where(first, dot(probs[0], v_block), dot(probs[1], v_block)).astype(BF16)
        dq = jnp.where(first, dot(grads[0], k_block), dot(grads[1], k_block)) * HEAD_DIM**-0.5
        mix[rows, cols[0]] = turn(dq, cos_tab[rows, :], -sin_tab[rows, :], low_lanes).astype(BF16)
        dk_acc[keys, :] += dot(grads[0], q_parts[0], TN) + dot(grads[1], q_parts[1], TN)
        dv_acc[keys, :] += dot(probs[0], g_parts[0], TN) + dot(probs[1], g_parts[1], TN)
    dq = mix[:, cols[0]].astype(F32)
    dk = pltpu.roll(turn(dk_acc[...], cos_tab[...], -sin_tab[...], low_lanes), HEAD_DIM, 1)
    dv = dv_acc[...]
    mix[:, cols[0]] = jnp.where(first, dq, dk).astype(BF16)
    mix[:, cols[1]] = jnp.where(first, dv, dq).astype(BF16)
    mix[:, cols[2]] = jnp.where(first, dk, dv).astype(BF16)


def block_kernel(
    hidden, cot, wq_in, wo_in, wu_in, wd_in,
    segments_in, freq_in, gain_one_in, shift_one_in, gain_two_in, shift_two_in, bq_in, bu_in,
    rq_out, ro_out, ru_out, rd_out, sum_out, slope_out, gains_out, bq_out, bu_out, cot_out,
    X, G, A, B, OUT, WQ, WO, WU, WD, MIX, CTX, ACT, GUP, rows_own, rows_far, params, biases, seg_col, cos_tab, sin_tab,
    dk_acc, dv_acc, SQ, SO, SU, SD, YQ, YO, YU, YD, ZQ, ZO, ZU, ZD, HQ, HO, HU, HD, LAND, FAR, SMALL, SMALL_Z, SMALL_P,
    send_sems, recv_sems, local_sems,
):
    R = 4
    dp, row, col = lax.axis_index("dp"), lax.axis_index("row"), lax.axis_index("col")
    side, quarter = lax.rem(dp, 2), lax.div(dp, 2)
    length, half = hidden.shape
    shard = wq_in.shape[0]
    core = (dp, row, 1 - col)
    xdev = (dp + 1 - 2 * side, row, col)
    ydev = (side + 2 * (1 - quarter), row, col)

    def zdev(t):
        return (dp, lax.rem(row + t + R, R), col)

    barrier = pltpu.get_barrier_semaphore()
    peers = [core, xdev, ydev] + [zdev(t) for t in range(1, R)]
    for peer in peers:
        pl.semaphore_signal(barrier, inc=1, device_id=peer, device_id_type=MESH)
    pl.semaphore_wait(barrier, len(peers))

    net = Net(send_sems, recv_sems)
    own_cols = pl.ds(pl.multiple_of(col * half, half), half)
    far_cols = pl.ds(pl.multiple_of((1 - col) * half, half), half)
    local = []

    def move(source, target):
        copy = pltpu.make_async_copy(source, target, local_sems.at[len(local)])
        copy.start()
        local.append(copy)
        return copy

    qc = WQ.shape[1] // 2
    oc = WO.shape[0] // 2
    uc = WU.shape[1] // 2

    def seat(h, size):
        return pl.ds(pl.multiple_of((side * 2 + (quarter if h == 0 else 1 - quarter)) * size, size), size)

    def block(t):
        return pl.ds(pl.multiple_of(lax.rem(row + t + R, R) * shard, shard), shard)

    every = slice(None)
    weights = {
        "q": (lambda h: wq_in.at[:, seat(h, qc)], lambda t, h: WQ.at[block(t), pl.ds(h * qc, qc)]),
        "o": (lambda h: wo_in.at[seat(h, oc), :], lambda t, h: WO.at[pl.ds(h * oc, oc), block(t)]),
        "u": (lambda h: wu_in.at[:, seat(h, uc)], lambda t, h: WU.at[block(t), pl.ds(h * uc, uc)]),
        "d": (lambda h: wd_in.at[seat(h, uc), :], lambda t, h: WD.at[pl.ds(h * uc, uc), block(t)]),
    }
    here_w = {}

    def start_along(name):
        here, place = weights[name]
        net.send((name, 1), here(0), place(0, 0), zdev(-1))
        net.send((name, 3), here(0), place(0, 0), zdev(1))

    def start_here(name):
        here, place = weights[name]
        here_w[name] = [move(here(h), place(0, h)) for h in range(2)]

    def along(name, t):
        place = weights[name][1]
        net.wait((name, t), place(t, 0), zdev(t))
        if t == 1:
            net.send((name, 2), place(t, 0), place(t, 0), zdev(-1))
        net.send((name, t, "y"), place(t, 0), place(t, 1), ydev)

    def across_y(name):
        place = weights[name][1]
        for t in (1, 3, 2):
            net.wait((name, t, "y"), place(t, 1), ydev)

    def have_here(name):
        for copy in here_w[name]:
            copy.wait()

    chunks = 2
    piece = length // chunks

    def chunk(c):
        return pl.ds(c * piece, piece)

    handed = []

    def hand_over(name, buffer, c):
        net.wait(("x " + name, c), buffer.at[1, chunk(c), own_cols], xdev)
        spot = buffer.at[1, chunk(c), own_cols]
        handed.append(net.send(("far " + name, c), spot, spot, core))

    def have_far(name, buffer):
        for c in range(chunks):
            net.wait(("far " + name, c), buffer.at[1, chunk(c), far_cols], core)

    start_along("q")
    net.send("core h", hidden, X.at[0, :, own_cols], core)
    start_along("o")
    here_h = move(hidden, X.at[0, :, own_cols])
    lane = lax.broadcasted_iota(jnp.int32, (1, LANES), 1)
    low_lanes = lane % HEAD_DIM < ROT // 2
    first = lane < HEAD_DIM

    seg = segments_in[...]
    start = jnp.zeros_like(seg)
    for number in range(1, DOCS):
        count = jnp.sum((seg < number).astype(jnp.int32), axis=1, keepdims=True)
        start = jnp.where(seg == number, count, start)
    rows_own[0:1, :] = seg.astype(F32)
    rows_own[1:2, :] = (lax.broadcasted_iota(jnp.int32, seg.shape, 1) - start).astype(F32)
    for i, source in enumerate([gain_one_in, shift_one_in, gain_two_in, shift_two_in]):
        params[i : i + 1, own_cols] = source[...].astype(F32).reshape(1, half)
    biases[0:1, pl.ds(0, bq_in.shape[0])] = bq_in[...].astype(F32).reshape(1, -1)
    biases[1:2, :] = bu_in[...].astype(F32).reshape(1, -1)
    net.send("core p", params.at[:, own_cols], params.at[:, own_cols], core)
    net.send("x rows", rows_own, rows_far, xdev)
    for c in range(chunks):
        net.send(("x h", c), hidden.at[chunk(c), :], X.at[1, chunk(c), own_cols], xdev)
    for c in range(chunks):
        net.send(("x g", c), cot.at[chunk(c), :], G.at[1, chunk(c), own_cols], xdev)
    net.send("core g", cot, G.at[0, :, own_cols], core)
    start_here("q")
    start_here("o")
    here_g = move(cot, G.at[0, :, own_cols])
    start_here("u")
    start_here("d")

    tile = 256
    GC = ACT.at[0]

    def each_tile(body):
        @pl.loop(0, length // tile, unroll=2)
        def _(i):
            body(pl.ds(pl.multiple_of(i * tile, tile), tile))

    def unit_rows(s, at):
        values = X[s, at, :].astype(F32)
        centred = values - jnp.mean(values, axis=-1, keepdims=True)
        inv = lax.rsqrt(jnp.mean(centred * centred, axis=-1, keepdims=True) + EPS)
        return centred * inv, inv

    def norm(s, at):
        unit, _ = unit_rows(s, at)
        A[s, at, :] = (unit * params[0:1, :] + params[1:2, :]).astype(BF16)
        B[s, at, :] = (unit * params[2:3, :] + params[3:4, :]).astype(BF16)

    def tables(rows):
        seg_col[...] = jnp.transpose(jnp.broadcast_to(rows[0:1, :], (LANES, length)))
        angles = jnp.transpose(jnp.broadcast_to(rows[1:2, :], (LANES, length))) * freq_in[0:1, :]
        cos_tab[...] = jnp.cos(angles)
        sin_tab[...] = jnp.sin(angles) * freq_in[1:2, :]

    def project(s, halves_in):
        low, high = halves_in[0] * qc, (halves_in[-1] + 1) * qc

        def body(at):
            product = dot(A[s, at, :], WQ[:, pl.ds(low, high - low)])
            cos_rows, sin_rows = cos_tab[at, :], sin_tab[at, :]
            for h in halves_in:
                mixed = product[:, h * qc - low : (h + 1) * qc - low] + biases[0:1, seat(h, qc)]
                t0, t1, t2 = [mixed[:, i * LANES : (i + 1) * LANES] for i in range(3)]
                query = jnp.where(first, t0, t1)
                key = pltpu.roll(jnp.where(first, t2, t0), HEAD_DIM, 1)
                value = jnp.where(first, t1, t2)
                MIX[s, at, pl.ds(h * qc, LANES)] = turn(query, cos_rows, sin_rows, low_lanes).astype(BF16)
                MIX[s, at, pl.ds(h * qc + LANES, LANES)] = turn(key, cos_rows, sin_rows, low_lanes).astype(BF16)
                MIX[s, at, pl.ds(h * qc + 2 * LANES, LANES)] = value.astype(BF16)

        each_tile(body)

    def pull_context(s, halves_in):
        low, high = halves_in[0] * oc, (halves_in[-1] + 1) * oc

        def body(at):
            GC[at, pl.ds(low, high - low)] = dot(G[s, at, :], WO[pl.ds(low, high - low), :], NT).astype(BF16)

        each_tile(body)

    def attend(s, rows, h):
        attend_pair(
            MIX.at[s], h * qc, GC, h * oc, CTX.at[s], rows, seg_col, cos_tab, sin_tab, dk_acc, dv_acc, tile
        )

    tables(rows_own)
    here_h.wait()
    net.wait("core h", X.at[0, :, far_cols], core)
    net.wait("core p", params.at[:, far_cols], core)
    along("q", 1)
    each_tile(lambda at: norm(0, at))
    along("q", 3)
    along("o", 1)
    start_along("u")
    start_along("d")
    along("o", 3)
    along("q", 2)
    have_here("q")
    project(0, (0,))
    along("o", 2)
    have_here("o")
    here_g.wait()
    net.wait("core g", G.at[0, :, far_cols], core)
    pull_context(0, (0,))
    hand_over("h", X, 0)
    attend(0, rows_own, 0)
    along("u", 1)
    across_y("q")
    project(0, (1,))
    across_y("o")
    pull_context(0, (1,))
    hand_over("h", X, 1)
    attend(0, rows_own, 1)
    along("u", 3)
    net.wait("x rows", rows_far, xdev)
    tables(rows_far)
    have_far("h", X)
    each_tile(lambda at: norm(1, at))
    along("d", 1)
    hand_over("g", G, 0)
    project(1, (0, 1))
    along("d", 3)
    along("u", 2)
    hand_over("g", G, 1)
    have_far("g", G)
    pull_context(1, (0, 1))
    attend(1, rows_far, 1)
    along("d", 2)

    grads = {
        "q": (SQ, YQ, ZQ, HQ, rq_out, lambda t: (block(t), every), lambda p: (every, p), qc),
        "o": (SO, YO, ZO, HO, ro_out, lambda t: (every, block(t)), lambda p: (p, every), oc),
        "u": (SU, YU, ZU, HU, ru_out, lambda t: (block(t), every), lambda p: (every, p), uc),
        "d": (SD, YD, ZD, HD, rd_out, lambda t: (every, block(t)), lambda p: (p, every), uc),
    }

    def multiply(name, h, t):
        if name == "q":
            pairs_of = [(A[s, :, block(t)], MIX[s, :, pl.ds(h * qc, qc)]) for s in range(2)]
        elif name == "u":
            pairs_of = [(B[s, :, block(t)], GUP[s, :, pl.ds(h * uc, uc)]) for s in range(2)]
        elif name == "o":
            pairs_of = [(CTX[s, :, pl.ds(h * oc, oc)], G[s, :, block(t)]) for s in range(2)]
        else:
            pairs_of = [(ACT[s, :, pl.ds(h * uc, uc)], G[s, :, block(t)]) for s in range(2)]
        return (dot(*pairs_of[0], TN) + dot(*pairs_of[1], TN)).astype(BF16)

    turns = (2, 3, 1, 0)

    def other_part(name):
        source, landed, spot = grads[name][0], grads[name][1], grads[name][5]
        for t in turns:
            source[spot(t)] = multiply(name, 1, t)
            net.send(("gy", name, t), source.at[spot(t)], landed.at[spot(t)], ydev)

    def own_part(name):
        kept, spot = grads[name][2], grads[name][5]

        @pl.loop(0, R, unroll=2)
        def _(t):
            kept[spot(t)] = multiply(name, 0, t)

    def across(name, t):
        _, landed, kept, hops, _, spot, _, _ = grads[name]
        net.wait(("gy", name, t), landed.at[spot(t)], ydev)
        total = kept[spot(t)].astype(F32) + landed[spot(t)].astype(F32)
        if t == 1:
            net.wait(("gz", name, 2), hops.at[0], zdev(-1))
            total = total + hops[0].astype(F32)
        kept[spot(t)] = total.astype(BF16)
        if t == 2:
            net.send(("gz", name, 2), kept.at[spot(t)], hops.at[0], zdev(1))
        elif t == 3:
            net.send(("gz", name, 3), kept.at[spot(t)], hops.at[1], zdev(-1))
        elif t == 1:
            net.send(("gz", name, 1), kept.at[spot(t)], hops.at[2], zdev(1))

    def finish(name):
        _, _, kept, hops, result, spot, place, size = grads[name]
        net.wait(("gz", name, 3), hops.at[1], zdev(1))
        net.wait(("gz", name, 1), hops.at[2], zdev(-1))
        total = kept[spot(0)].astype(F32) + hops[1].astype(F32) + hops[2].astype(F32)
        kept[spot(0)] = total.astype(BF16)
        target = result.at[place(seat(0, size))]
        net.send(("ry", name), kept.at[spot(0)], target, ydev)
        net.send(("rx", name), kept.at[spot(0)], target, xdev)
        return move(kept.at[spot(0)], target)

    def far_seat(h, size):
        return pl.ds(pl.multiple_of(((1 - side) * 2 + (quarter if h == 0 else 1 - quarter)) * size, size), size)

    by_x = "u"

    def spread_out(name):
        _, _, _, _, result, _, place, size = grads[name]
        if name in by_x:
            target = result.at[place(far_seat(0, size))]
            net.wait(("rx", name), target, xdev)
            net.send(("rr", name), target, target, ydev)
        else:
            target = result.at[place(seat(1, size))]
            net.wait(("ry", name), target, ydev)
            net.send(("rr", name), target, target, xdev)

    def collect(name):
        _, _, _, _, result, _, place, size = grads[name]
        if name in by_x:
            net.wait(("ry", name), result.at[place(seat(1, size))], ydev)
        else:
            net.wait(("rx", name), result.at[place(far_seat(0, size))], xdev)
        net.wait(("rr", name), result.at[place(far_seat(1, size))], ydev if name in by_x else xdev)

    SMALL[...] = jnp.zeros_like(SMALL)
    other_part("q")
    other_part("o")
    attend(1, rows_far, 0)
    have_here("u")
    have_here("d")
    across_y("u")
    across_y("d")

    def seat_of(h, size):
        return (quarter if h == 0 else 1 - quarter) * size

    def feed_part(s, h):
        def ahead(at, begin):
            cols = pl.ds(h * uc + begin, tile)
            bias_at = (side * 2) * uc + seat_of(h, uc) + begin
            up = dot(B[s, at, :], WU[:, cols]) + biases[1:2, pl.ds(pl.multiple_of(bias_at, tile), tile)]
            return at, begin, cols, up, dot(G[s, at, :], WD[cols, :], NT)

        def after(at, begin, cols, up, pull):
            gate = 0.5 * (1.0 + lax.erf(up * 0.5**0.5))
            bell = jnp.exp(-0.5 * up * up) * 0.3989422804014327
            ACT[s, at, cols] = (up * gate).astype(BF16)
            grad = (pull * (gate + up * bell)).astype(BF16)
            GUP[s, at, cols] = grad
            SMALL[1:2, pl.ds(pl.multiple_of(seat_of(h, uc) + begin, tile), tile)] += jnp.sum(
                grad.astype(F32), axis=0, keepdims=True
            )

        @pl.loop(0, length // (2 * tile))
        def _(i):
            steps = []
            for j in range(2):
                at = pl.ds(pl.multiple_of(i * 2 * tile + j * tile, tile), tile)
                steps += [(at, begin) for begin in range(0, uc, tile)]
            coming = ahead(*steps[0])
            for k in range(len(steps)):
                now = coming
                if k + 1 < len(steps):
                    coming = ahead(*steps[k + 1])
                after(*now)

    def halves(value):
        left, right = value[:, :half], value[:, half:]
        return jnp.where(col == 0, left, right).astype(BF16), jnp.where(col == 0, right, left).astype(BF16)

    def leave(s, c, out, slope):
        @pl.loop(0, piece // tile, unroll=2)
        def _(i):
            at = pl.ds(pl.multiple_of(c * piece + i * tile, tile), tile)
            to = pl.ds(pl.multiple_of(i * tile, tile), tile) if s == 1 else at
            result = dot(CTX[s, at, :], WO[...]) + dot(ACT[s, at, :], WD[...])
            grad_one = dot(MIX[s, at, :], WQ[...], NT)
            grad_two = dot(GUP[s, at, :], WU[...], NT)
            out[0][at, :], out[1][to, :] = halves(result)
            unit, inv = unit_rows(s, at)
            for i_row, value in enumerate([grad_one * unit, grad_one, grad_two * unit, grad_two]):
                SMALL[2 + i_row : 3 + i_row, :] += jnp.sum(value, axis=0, keepdims=True)
            scaled = grad_one * params[0:1, :] + grad_two * params[2:3, :]
            mean_scaled = jnp.mean(scaled, axis=1, keepdims=True)
            mean_unit = jnp.mean(scaled * unit, axis=1, keepdims=True)
            slope[0][at, :], slope[1][to, :] = halves(inv * (scaled - mean_scaled - unit * mean_unit))
            if s == 0:
                SMALL[6:7, own_cols] += jnp.sum(G[0, at, own_cols].astype(F32), axis=0, keepdims=True)

    given = [ZD, SD]
    given_copies = []
    near = [X.at[1, :, pl.ds(0, half)], X.at[1, :, pl.ds(half, half)]]

    def leave_far(c):
        spots = [buffer.at[:, pl.ds(c * half, half)] for buffer in given]
        leave(1, c, (OUT.at[0], spots[0]), (OUT.at[1], spots[1]))
        for i in range(2):
            given_copies.append(net.send(("out", i, c), spots[i], LAND.at[i, chunk(c), :], core))

    def pass_far(c):
        for i in range(2):
            net.wait(("out", i, c), LAND.at[i, chunk(c), :], core)
            LAND[i, chunk(c), :] = (LAND[i, chunk(c), :].astype(F32) + OUT[i, chunk(c), :].astype(F32)).astype(BF16)
            net.send(("far out", i, c), LAND.at[i, chunk(c), :], FAR.at[i, chunk(c), :], xdev)

    def leave_own(c):
        sides = [[buffer.at[0, :, pl.ds(h * half, half)] for h in range(2)] for buffer in (ACT, GUP)]
        leave(0, c, *sides)
        for i in range(2):
            net.send(("own out", i, c), sides[i][1].at[chunk(c), :], near[i].at[chunk(c), :], core)

    def add_up(i, c):
        buffer = (ACT, GUP)[i]
        net.wait(("own out", i, c), near[i].at[chunk(c), :], core)
        net.wait(("far out", i, c), FAR.at[i, chunk(c), :], xdev)
        total = buffer[0, chunk(c), pl.ds(0, half)].astype(F32) + near[i][chunk(c), :].astype(F32)
        FAR[i, chunk(c), :] = (total + FAR[i, chunk(c), :].astype(F32)).astype(BF16)
        return move(FAR.at[i, chunk(c), :], (sum_out, slope_out)[i].at[chunk(c), :])

    def mixed_sums():
        for h in range(2):
            sums = [jnp.sum(MIX[s, :, pl.ds(h * qc, qc)].astype(F32), axis=0, keepdims=True) for s in range(2)]
            SMALL[0:1, pl.ds(pl.multiple_of(seat_of(h, qc), LANES), qc)] = sums[0] + sums[1]

    def small_z():
        for t in range(1, R):
            net.send(("sz", t), SMALL, SMALL_Z.at[row], zdev(t))
        SMALL_Z[row] = SMALL[...]

    def small_y():
        for t in range(1, R):
            net.wait(("sz", t), SMALL_Z.at[lax.rem(row - t + R, R)], zdev(-t))
        total = SMALL_Z[0]
        for r in range(1, R):
            total = total + SMALL_Z[r]
        SMALL_P[0] = total
        net.send("sy", SMALL_P.at[0], SMALL_P.at[1], ydev)

    def small_x():
        net.wait("sy", SMALL_P.at[1], ydev)
        SMALL_P[2] = SMALL_P[0] + SMALL_P[1]
        net.send("sx", SMALL_P.at[2], SMALL_P.at[3], xdev)

    def small_core():
        net.wait("sx", SMALL_P.at[3], xdev)
        SMALL_P[4] = SMALL_P[2] + SMALL_P[3]
        net.send("sc", SMALL_P.at[4], SMALL_P.at[5], core)

    def small_end():
        net.wait("sc", SMALL_P.at[5], core)
        SMALL_P[5] = SMALL_P[4] + SMALL_P[5]

    done = []
    feed_part(1, 0)
    feed_part(1, 1)
    for copy in handed:
        net.sent(copy)
    leave_far(1)
    feed_part(0, 1)
    pass_far(1)
    own_part("o")
    other_part("u")
    across("o", 2)
    own_part("q")
    across("o", 3)
    across("q", 2)
    across("q", 3)
    feed_part(0, 0)
    across("o", 1)
    leave_far(0)
    across("q", 1)
    for copy in given_copies:
        net.sent(copy)
    own_part("d")
    own_part("u")
    across("u", 3)
    pass_far(0)
    other_part("d")
    leave_own(1)
    across("q", 0)
    across("u", 2)
    across("d", 2)
    across("o", 0)
    mixed_sums()
    leave_own(0)
    small_z()
    across("u", 1)
    done.append(finish("o"))
    done += [add_up(0, 1), add_up(1, 1)]
    across("u", 0)
    across("d", 3)
    small_y()
    across("d", 1)
    done.append(finish("q"))
    done.append(finish("u"))
    small_x()
    done += [add_up(0, 0), add_up(1, 0)]
    across("d", 0)
    spread_out("q")
    done.append(finish("d"))
    small_core()
    spread_out("u")
    spread_out("o")
    small_end()
    spread_out("d")

    def side_span(which, size):
        return pl.ds(pl.multiple_of(which * size, LANES), size)

    for i, which in [(2, side), (3, 1 - side)]:
        done += [
            move(SMALL_P.at[i, pl.ds(0, 1), pl.ds(0, 2 * qc)], bq_out.at[:, side_span(which, 2 * qc)]),
            move(SMALL_P.at[i, pl.ds(1, 1), pl.ds(0, 2 * uc)], bu_out.at[:, side_span(which, 2 * uc)]),
        ]
    done += [
        move(SMALL_P.at[5, pl.ds(2, 4), own_cols], gains_out),
        move(SMALL_P.at[4, pl.ds(6, 1), own_cols], cot_out),
    ]
    for name in "oqdu":
        collect(name)
    for copy in done:
        copy.wait()
    net.drain()


def whole_block(hidden, cot, wq, wo, wu, wd, *rest):
    length, half = hidden.shape
    width = 2 * half
    shard = wq.shape[0]
    wide3 = wq.shape[1] // 2
    wide = wide3 // 3
    units = wu.shape[1] // 2
    qc, oc, uc = wide3 // 2, wide // 2, units // 2
    out_shape = [
        jax.ShapeDtypeStruct(shape, kind)
        for shape, kind in [
            ((shard, 4 * qc), BF16), ((4 * oc, shard), BF16), ((shard, 4 * uc), BF16), ((4 * uc, shard), BF16),
            ((length, half), BF16), ((length, half), BF16),
            ((4, half), F32), ((1, 4 * qc), F32), ((1, 4 * uc), F32), ((1, half), F32),
        ]
    ]
    both = lambda n: pltpu.VMEM((2, length, n), BF16)
    plain = lambda *shape: pltpu.VMEM(shape, BF16)
    floats = lambda *shape: pltpu.VMEM(shape, F32)
    quarter_grads = [plain(width, qc), plain(oc, width), plain(width, uc), plain(uc, width)]
    scratch = [
        both(width), both(width), both(width), both(width), both(half),
        plain(width, wide3), plain(wide, width), plain(width, units), plain(units, width),
        both(wide3), both(wide), both(units), both(units),
        floats(8, length), floats(8, length), floats(8, width), floats(8, 4 * uc),
        *[floats(length, LANES)] * 5,
        *quarter_grads * 3,
        plain(3, shard, qc), plain(3, oc, shard), plain(3, shard, uc), plain(3, uc, shard),
        both(half), both(half), floats(8, width), floats(4, 8, width), floats(6, 8, width),
    ]
    any_spec = pl.BlockSpec(memory_space=pl.ANY)
    vmem_spec = pl.BlockSpec(memory_space=pltpu.VMEM)
    return pl.pallas_call(
        block_kernel,
        out_shape=out_shape,
        in_specs=[any_spec] * 6 + [vmem_spec] * len(rest),
        out_specs=[any_spec] * len(out_shape),
        scratch_shapes=scratch + [
            pltpu.SemaphoreType.DMA((128,)), pltpu.SemaphoreType.DMA((128,)), pltpu.SemaphoreType.DMA((32,)),
        ],
        compiler_params=pltpu.CompilerParams(collective_id=0, has_side_effects=True, vmem_limit_bytes=63 << 20),
        name="block",
    )(hidden, cot, wq, wo, wu, wd, *rest)


def widen_kernel(
    hidden, branch, cot, slope, grad_q, grad_o, grad_u, grad_d, bias_one, bias_two, gains, qkv_sum, up_sum, cot_sum,
    output, input_grad, out_q, out_o, out_u, out_d, *small,
):
    bias = (bias_one[...].astype(F32) + bias_two[...].astype(F32)).reshape(1, -1)
    output[...] = hidden[...].astype(F32) + branch[...].astype(F32) + bias
    input_grad[...] = cot[...].astype(F32) + slope[...].astype(F32)
    for source, target in [(grad_q, out_q), (grad_o, out_o), (grad_u, out_u), (grad_d, out_d)]:
        target[...] = source[...].astype(F32)
    for i in range(4):
        small[i][...] = gains[i, :]
    small[4][...] = qkv_sum[0, :]
    small[5][...] = up_sum[0, :]
    small[6][...] = cot_sum[0, :]
    small[7][...] = cot_sum[0, :]


def widen_all(hidden, branch, cot, slope, grad_q, grad_o, grad_u, grad_d, bias_one, bias_two, gains, *sums):
    steps = 4
    rows = lambda v: pl.BlockSpec((v.shape[0] // steps, v.shape[1]), lambda i: (i, 0))
    whole = lambda v: pl.BlockSpec(v.shape, lambda i: (0,) * v.ndim)
    large = [hidden, branch, cot, slope, grad_q, grad_o, grad_u, grad_d]
    tiny = [bias_one, bias_two, gains, *sums]
    wide = [hidden, cot, grad_q, grad_o, grad_u, grad_d]
    flat = [gains.shape[1]] * 4 + [v.shape[1] for v in sums] + [sums[-1].shape[1]]
    return pl.pallas_call(
        widen_kernel,
        grid=(steps,),
        in_specs=[rows(v) for v in large] + [whole(v) for v in tiny],
        out_specs=[rows(v) for v in wide] + [pl.BlockSpec((n,), lambda i: (0,)) for n in flat],
        out_shape=[jax.ShapeDtypeStruct(v.shape, F32) for v in wide] + [jax.ShapeDtypeStruct((n,), F32) for n in flat],
        compiler_params=pltpu.CompilerParams(vmem_limit_bytes=63 << 20),
        name="widen",
    )(*large, *tiny)


def local_block(
    hidden,
    segments,
    ln1_gain,
    ln1_bias,
    qkv_weight,
    qkv_bias,
    out_weight,
    out_bias,
    ln2_gain,
    ln2_bias,
    up_weight,
    up_bias,
    down_weight,
    down_bias,
    cotangent,
):
    lane = np.arange(LANES) % HEAD_DIM
    frequency = np.where(lane < ROT, 10000.0 ** (-2.0 * (lane % (ROT // 2)) / ROT), 0.0)
    sign = np.where(lane < ROT, np.where(lane < ROT // 2, -1.0, 1.0), 0.0)
    freq = np.stack([frequency, sign] * 4).astype(np.float32)
    flat = [ln1_gain, ln1_bias, ln2_gain, ln2_bias, qkv_bias, up_bias]
    grad_q, grad_o, grad_u, grad_d, branch, slope, gains, qkv_sum, up_sum, cot_sum = whole_block(
        hidden, cotangent, qkv_weight, out_weight, up_weight, down_weight, segments, jnp.asarray(freq), *flat
    )
    output, input_grad, grad_q, grad_o, grad_u, grad_d, *small = widen_all(
        hidden, branch, cotangent, slope, grad_q, grad_o, grad_u, grad_d,
        out_bias, down_bias, gains, qkv_sum, up_sum, cot_sum,
    )
    gain_one, shift_one, gain_two, shift_two, qkv_sum, up_sum, cot_sum, cot_again = small
    return (
        output, input_grad, gain_one, shift_one, grad_q, qkv_sum, grad_o, cot_sum,
        gain_two, shift_two, grad_u, up_sum, grad_d, cot_again,
    )


def normalize(values):
    centred = values - jnp.mean(values, axis=-1, keepdims=True)
    variance = jnp.mean(centred * centred, axis=-1, keepdims=True)
    inv_std = lax.rsqrt(variance + EPS)
    return centred * inv_std, inv_std


def make_general(groups, rows, cols):
    quarters = groups // 2

    def pair_swap(value):
        return lax.ppermute(value, "dp", [(d, d ^ 1) for d in range(groups)])

    def quarter_shift(value, shift):
        moves = [(2 * a + b, 2 * ((a + shift) % quarters) + b) for a in range(quarters) for b in range(2)]
        return lax.ppermute(value, "dp", moves)

    def row_shift(value, shift):
        return lax.ppermute(value, "row", [(r, (r + shift) % rows) for r in range(rows)])

    def core_swap(value):
        return lax.ppermute(value, "col", [(0, 1), (1, 0)])

    def local(
        hidden,
        segments,
        ln1_gain,
        ln1_bias,
        qkv_weight,
        qkv_bias,
        out_weight,
        out_bias,
        ln2_gain,
        ln2_bias,
        up_weight,
        up_bias,
        down_weight,
        down_bias,
        cotangent,
    ):
        assert segments.shape[0] == 1 and cols == 2
        length = segments.shape[1]
        half_width = hidden.shape[1]
        width = 2 * half_width
        shard = qkv_weight.shape[0]
        heads = qkv_weight.shape[1] // (3 * HEAD_DIM) // 2
        wide = heads * HEAD_DIM
        units = up_weight.shape[1] // 2
        whole_heads = heads % quarters == 0
        dp = lax.axis_index("dp")
        row = lax.axis_index("row")
        col = lax.axis_index("col")
        side = lax.rem(dp, 2)
        quarter = dp // 2

        def both(mine, other):
            flip = col == 0
            return jnp.concatenate([jnp.where(flip, mine, other), jnp.where(flip, other, mine)], axis=-1)

        def half_of(value, axis):
            size = value.shape[axis] // 2
            return lax.dynamic_slice_in_dim(value, side * size, size, axis)

        def piece_of(value, shift, axis, placed=False):
            size = value.shape[axis] // quarters
            if placed:
                return lax.slice_in_dim(value, shift * size, (shift + 1) * size, axis=axis)
            return lax.dynamic_slice_in_dim(value, lax.rem(quarter - shift + quarters, quarters) * size, size, axis)

        def in_place(pieces, axis):
            if quarters == 1:
                return pieces[0]
            if quarters == 2:
                flip = quarter == 0
                first = jnp.where(flip, pieces[0], pieces[1])
                second = jnp.where(flip, pieces[1], pieces[0])
                return jnp.concatenate([first, second], axis=axis)
            order = lax.rem(quarter - jnp.arange(quarters) + quarters, quarters)
            stacked = jnp.take(jnp.stack(pieces), order, axis=0)
            return jnp.concatenate([stacked[i] for i in range(quarters)], axis=axis)

        def near(pieces, axis, keep):
            return jnp.concatenate(pieces, axis=axis) if keep else in_place(pieces, axis)

        def gather(value, width_axis, unit_axis, keep):
            mine = piece_of(value, 0, unit_axis)
            received = {0: mine}
            ahead = behind = mine
            for step in range(1, rows):
                if step <= rows // 2:
                    ahead = row_shift(ahead, -1)
                    received[step] = ahead
                if step <= (rows - 1) // 2:
                    behind = row_shift(behind, 1)
                    received[rows - step] = behind
            result = jnp.zeros(
                [width if i == width_axis else n for i, n in enumerate(value.shape)], value.dtype
            )
            for step in range(rows):
                if step == 0:
                    pieces = [piece_of(value, q, unit_axis) for q in range(quarters)]
                else:
                    pieces = [received[step]]
                    pieces += [quarter_shift(received[step], q) for q in range(1, quarters)]
                block = near(pieces, unit_axis, keep)
                place = lax.rem(row + step, rows) * shard
                result = lax.dynamic_update_slice_in_dim(result, block, place, width_axis)
            return result

        hidden_other = core_swap(hidden)
        hidden_far = pair_swap(hidden)
        cot_other = core_swap(cotangent)
        cot_far = pair_swap(cotangent)
        params = jnp.stack([ln1_gain, ln1_bias, ln2_gain, ln2_bias])
        params = both(params, core_swap(params)).astype(F32)
        gain_one, shift_one, gain_two, shift_two = [params[i][None, :] for i in range(4)]
        inputs = [both(hidden, hidden_other), both(hidden_far, core_swap(hidden_far))]
        cots = [both(cotangent, cot_other), both(cot_far, core_swap(cot_far))]
        segs = [segments, pair_swap(segments)]

        qkv_cols = qkv_weight.reshape(shard, 2, heads, 3, HEAD_DIM)
        qkv_cols = lax.dynamic_index_in_dim(qkv_cols, side, 1, keepdims=False)
        qkv_cols = jnp.swapaxes(qkv_cols, 1, 2).reshape(shard, 3, wide)
        qkv_all = gather(qkv_cols, 0, 2, whole_heads).reshape(width, 3 * wide)
        out_all = gather(half_of(out_weight, 0), 1, 0, whole_heads)
        up_all = gather(half_of(up_weight, 1), 0, 1, True)
        down_all = gather(half_of(down_weight, 0), 1, 0, True)

        bias_cols = lax.dynamic_index_in_dim(qkv_bias.reshape(2, heads, 3, HEAD_DIM), side, 0, keepdims=False)
        bias_cols = jnp.swapaxes(bias_cols, 0, 1).reshape(1, 3, wide)
        bias_cols = near([piece_of(bias_cols, q, 2) for q in range(quarters)], 2, whole_heads)
        bias_cols = bias_cols.reshape(1, 3 * wide).astype(F32)
        up_half = half_of(up_bias, 0)
        up_row = jnp.concatenate([piece_of(up_half, q, 0) for q in range(quarters)])[None, :].astype(F32)

        norms = []
        contexts = []
        grads_mixed = []
        for values, cot, seg in zip(inputs, cots, segs):
            unit, inv = normalize(values.astype(F32))
            act_one = (unit * gain_one + shift_one).astype(BF16)
            act_two = (unit * gain_two + shift_two).astype(BF16)
            norms.append((unit, inv, act_one, act_two))
            cos_rows, sine_rows = rotary_tables(doc_positions(seg).reshape(length))
            mixed = dot(act_one, qkv_all) + bias_cols
            cos_wide = jnp.tile(cos_rows, (1, 2 * wide // LANES))
            sine_wide = jnp.tile(sine_rows, (1, 2 * wide // LANES))
            turned = mixed[:, : 2 * wide]
            lane = jnp.arange(2 * wide) % HEAD_DIM
            swapped = jnp.where(
                lane < ROT // 2, jnp.roll(turned, -(ROT // 2), axis=1), jnp.roll(turned, ROT // 2, axis=1)
            )
            turned = turned * cos_wide + swapped * sine_wide
            qkv = jnp.concatenate([turned, mixed[:, 2 * wide :]], axis=1).astype(BF16)
            grad_context = dot(cot, out_all, NT).astype(BF16)
            context, grad_mixed = attention(qkv, grad_context, seg, cos_rows, sine_rows)
            contexts.append(context)
            grads_mixed.append(grad_mixed)

        feeds = [feed(norm[3], cot, up_all, up_row, down_all) for norm, cot in zip(norms, cots)]

        def reduce_grad(left, right, width_axis, unit_axis, placed, shape=None):
            total = dot(left[0], right[0], TN) + dot(left[1], right[1], TN)
            if shape is not None:
                total = total.reshape(shape)
            mine = piece_of(total, 0, unit_axis, placed)
            for q in range(1, quarters):
                part = piece_of(total, q, unit_axis, placed).astype(BF16)
                mine = mine + quarter_shift(part, -q).astype(F32)
            cut = lambda t: lax.dynamic_slice_in_dim(mine, lax.rem(row + t, rows) * shard, shard, width_axis)
            result = cut(0)
            for t in range(1, rows):
                result = result + row_shift(cut(t).astype(BF16), t).astype(F32)
            result = result.astype(BF16)
            pieces = [result] + [quarter_shift(result, q) for q in range(1, quarters)]
            result = in_place(pieces, unit_axis)
            far = pair_swap(result)
            flip = side == 0
            return jnp.concatenate(
                [jnp.where(flip, result, far), jnp.where(flip, far, result)], axis=unit_axis
            ).astype(F32)

        acts_one = [n[2] for n in norms]
        acts_two = [n[3] for n in norms]
        out_grad = reduce_grad(contexts, cots, 1, 0, whole_heads)
        qkv_grad = reduce_grad(acts_one, grads_mixed, 0, 2, whole_heads, (width, 3, wide))
        down_grad = reduce_grad([f[0] for f in feeds], cots, 1, 0, True)
        up_grad = reduce_grad(acts_two, [f[1] for f in feeds], 0, 1, True)
        qkv_grad = qkv_grad.reshape(shard, 3, 2 * heads, HEAD_DIM)
        qkv_grad = jnp.swapaxes(qkv_grad, 1, 2).reshape(shard, 6 * wide)

        outs = []
        slopes = []
        norm_sums = jnp.zeros((4, width), F32)
        for index in range(2):
            unit, inv, _, _ = norms[index]
            act, grad_up, _ = feeds[index]
            outs.append((dot(contexts[index], out_all) + dot(act, down_all)).astype(BF16))
            grad_one = dot(grads_mixed[index], qkv_all, NT)
            grad_two = dot(grad_up, up_all, NT)
            norm_sums += jnp.stack(
                [
                    jnp.sum(grad_one * unit, axis=0),
                    jnp.sum(grad_one, axis=0),
                    jnp.sum(grad_two * unit, axis=0),
                    jnp.sum(grad_two, axis=0),
                ]
            )
            scaled = grad_one * gain_one + grad_two * gain_two
            mean_scaled = jnp.mean(scaled, axis=1, keepdims=True)
            mean_unit = jnp.mean(scaled * unit, axis=1, keepdims=True)
            slopes.append((inv * (scaled - mean_scaled - unit * mean_unit)).astype(BF16))

        def fold(pair):
            sums = []
            for value in pair:
                kept = lax.dynamic_slice_in_dim(value, col * half_width, half_width, 1).astype(F32)
                given = lax.dynamic_slice_in_dim(value, (1 - col) * half_width, half_width, 1)
                sums.append(kept + core_swap(given).astype(F32))
            return sums[0] + pair_swap(sums[1].astype(BF16)).astype(F32)

        cot_local = cotangent.astype(F32)
        output = hidden.astype(F32) + fold(outs) + (out_bias.astype(F32) + down_bias.astype(F32))
        input_grad = cot_local + fold(slopes)

        qkv_sum = (
            jnp.sum(grads_mixed[0].astype(F32), axis=0) + jnp.sum(grads_mixed[1].astype(F32), axis=0)
        ).reshape(3, wide)
        if whole_heads:
            qkv_sum = in_place([piece_of(qkv_sum, q, 1, True) for q in range(quarters)], 1)
        up_sum = (feeds[0][2] + feeds[1][2])[0]
        up_sum = in_place([piece_of(up_sum, q, 0, True) for q in range(quarters)], 0)

        def widen(value):
            zeros = jnp.zeros_like(value)
            flip = side == 0
            return jnp.concatenate([jnp.where(flip, value, zeros), jnp.where(flip, zeros, value)], axis=-1)

        kept = lax.dynamic_slice_in_dim(norm_sums, col * half_width, half_width, 1)
        given = lax.dynamic_slice_in_dim(norm_sums, (1 - col) * half_width, half_width, 1)
        norm_sums = kept + core_swap(given)
        small = jnp.concatenate(
            [widen(qkv_sum).reshape(-1), widen(up_sum), jnp.sum(cot_local, axis=0), norm_sums.reshape(-1)]
        )
        small = lax.psum(small, ("dp", "row"))
        sizes = [6 * wide, 2 * units, half_width, half_width, half_width, half_width, half_width]
        parts = []
        start = 0
        for size in sizes:
            parts.append(lax.slice_in_dim(small, start, start + size))
            start += size
        qkv_sum, up_sum, cot_sum, gain_one_sum, shift_one_sum, gain_two_sum, shift_two_sum = parts
        qkv_sum = jnp.swapaxes(qkv_sum.reshape(3, 2 * heads, HEAD_DIM), 0, 1).reshape(-1)
        return (
            output,
            input_grad,
            gain_one_sum,
            shift_one_sum,
            qkv_grad,
            qkv_sum,
            out_grad,
            cot_sum,
            gain_two_sum,
            shift_two_sum,
            up_grad,
            up_sum,
            down_grad,
            cot_sum,
        )

    return local


def solution(mesh):
    placed = (
        P(("dp", "row"), "col"),
        P(("dp", "row"), None),
        P("col"),
        P("col"),
        P("row", "col"),
        P("col"),
        P("col", "row"),
        P("col"),
        P("col"),
        P("col"),
        P("row", "col"),
        P("col"),
        P("col", "row"),
        P("col"),
        P(("dp", "row"), "col"),
    )
    groups, rows, cols = mesh.shape["dp"], mesh.shape["row"], mesh.shape["col"]
    paired = (groups, rows, cols) == (4, 4, 2)
    return jax.shard_map(
        local_block if paired else make_general(groups, rows, cols),
        mesh=mesh,
        in_specs=placed,
        out_specs=(
            P(("dp", "row"), "col"),
            P(("dp", "row"), "col"),
            P("col"),
            P("col"),
            P("row", "col"),
            P("col"),
            P("col", "row"),
            P("col"),
            P("col"),
            P("col"),
            P("row", "col"),
            P("col"),
            P("col", "row"),
            P("col"),
        ),
        check_vma=False,
    )
```
